32 devices in a mesh: row: 4 (over y, x), blk: 8 (over z, core).
Axes of the slice: x: 2, y: 2, z: 4, core: 2. Of those that a mesh axis runs over, the one named last changes fastest.
Arguments:
- hidden_in: bfloat16 [4, 1024, 2048], P('row', 'blk'), may hold values from -6 to 6
- segment_ids: int32 [4, 1024], P('row', 'blk'), may hold values from 0 to 1, as said below
- expert_ids: int32 [4, 1024, 8], P('row', 'blk'), may hold values from 0 to 15, all different within a row; in each aligned block of 128 rows (0 to 127, 128 to 255, ..., all dimensions but the last counted through in order) at most 96 rows name the same one
- attention_gain: bfloat16 [2048], P(('row', 'blk')), may hold values from 0.5 to 1.5
- query_gain: bfloat16 [2048], P(('row', 'blk')), may hold values from 0.5 to 1.5
- key_gain: bfloat16 [2048], P(('row', 'blk')), may hold values from 0.5 to 1.5
- expert_gain: bfloat16 [2048], P(('row', 'blk')), may hold values from 0.5 to 1.5
- query_weight: bfloat16 [2048, 2048], P(('row', 'blk')), may hold values from -0.125 to 0.125
- key_weight: bfloat16 [2048, 2048], P(('row', 'blk')), may hold values from -0.125 to 0.125
- value_weight: bfloat16 [2048, 2048], P(('row', 'blk')), may hold values from -0.125 to 0.125
- output_weight: bfloat16 [2048, 2048], P(('row', 'blk')), may hold values from -1 to 1
- router_weight: bfloat16 [2048, 16], P(('row', 'blk')), may hold values from -0.0625 to 0.0625
- gate_weight: bfloat16 [32, 2048, 512], P(('row', 'blk')), may hold values from -0.125 to 0.125
- up_weight: bfloat16 [32, 2048, 512], P(('row', 'blk')), may hold values from -0.125 to 0.125
- down_weight: bfloat16 [32, 512, 2048], P(('row', 'blk')), may hold values from -0.75 to 0.75
- grad_out: bfloat16 [4, 1024, 2048], P('row', 'blk'), may hold values from -6 to 6
Outputs:
- layer_out: bfloat16 [4, 1024, 2048], P('row', 'blk')
- input_grad: float32 [4, 1024, 2048], P('row', 'blk')
- grad_attention_gain: float32 [2048], P(('row', 'blk'))
- grad_query_gain: float32 [2048], P(('row', 'blk'))
- grad_key_gain: float32 [2048], P(('row', 'blk'))
- grad_expert_gain: float32 [2048], P(('row', 'blk'))
- grad_query_weight: float32 [2048, 2048], P(('row', 'blk'))
- grad_key_weight: float32 [2048, 2048], P(('row', 'blk'))
- grad_value_weight: float32 [2048, 2048], P(('row', 'blk'))
- grad_output_weight: float32 [2048, 2048], P(('row', 'blk'))
- grad_router_weight: float32 [2048, 16], P(('row', 'blk'))
- grad_gate_weight: float32 [32, 2048, 512], P(('row', 'blk'))
- grad_up_weight: float32 [32, 2048, 512], P(('row', 'blk'))
- grad_down_weight: float32 [32, 512, 2048], P(('row', 'blk'))
The draws below stay inside these ranges and needn't reach their ends.
Inputs may be any that keep to these rules, and one draw needn't show every extreme that they name: `segment_ids`: within a packed row the ids never fall. Each row is either one document or two documents, each of 256 to 768 tokens; in every draw some row is one document. `expert_ids`: each token names 8 different experts. Among the 128 tokens of one device (aligned blocks of a packed row) no expert is named by more than 96 tokens, and in every draw some expert is named by exactly 96 tokens of some device.
All inputs are finite; a program needn't handle non-finite values.
Results may differ from the reference program's by a relative error of at most 0.028.
Values may be sent and summed in bfloat16 or wider, within the bound.
A program may use at most 256 MiB of HBM per device.

```python
import math
import jax
import jax.numpy as jnp
import numpy as np
from jax import lax

D = 2048
HEADS = 16
HEAD_DIM = 128
FF = 1024
TOP_K = 8
TOK_DEV = 128
HALF_FF = 512
SEQ_LEN = 1024
ROWS = 4
EXPERTS = 16
CAPACITY = 96
DEVICES = 32


def draw_segment_ids(key, part):
    key = jax.random.fold_in(key, 11)
    bound_key = jax.random.fold_in(key, 1)
    whole_key = jax.random.fold_in(key, 2)
    bounds = jax.random.randint(bound_key, (ROWS,), SEQ_LEN // 4, 3 * SEQ_LEN // 4 + 1).astype(jnp.int32)
    whole_row = jax.random.randint(whole_key, (), 0, ROWS).astype(jnp.int32)
    bounds = jnp.where(jnp.arange(ROWS, dtype=jnp.int32) == whole_row, SEQ_LEN, bounds).astype(jnp.int32)
    places = jnp.arange(SEQ_LEN, dtype=jnp.int32)
    return (places[None, :] >= bounds[:, None]).astype(jnp.int32)


def level_of(stream_key, dims, shards, low, high):
    loudness = 1.0
    for axis_at, blocks in shards:
        draws = jax.random.uniform(jax.random.fold_in(jax.random.fold_in(stream_key, 6), axis_at), (blocks,), jnp.float32, low / len(shards), high / len(shards))
        loudness = loudness * jnp.repeat(jnp.exp(draws), dims[axis_at] // blocks).reshape((-1,) + (1,) * (len(dims) - 1 - axis_at))
    return loudness


def shared_out(rng, own, number, rows, amount, top, bound, skew):
    sequence = jax.random.permutation(rng, amount)
    packed, ordinary = portions_of(amount, rows * top, bound, skew, True), portions_of(amount, rows * top, bound, skew, False)
    places = jnp.arange(amount)

    def named(sizes, offset_by):
        used = int((sizes > 0).sum())
        fixed = max(1, used // 4)
        moved = fixed + (places - fixed + offset_by * (used - fixed)) % max(1, amount - fixed)
        return jnp.zeros((amount,), jnp.int32).at[sequence[jnp.where(places < fixed, places, moved)]].set(jnp.asarray(sizes, jnp.int32))

    sizes = jnp.where(number % 4 == 0, named(packed, number // 4), named(ordinary, number - number // 4 - 1))
    mixed = jax.random.permutation(jax.random.fold_in(own, 3), amount)
    source_of, taker = mixed[0:amount // 2 * 2:2], mixed[1:amount // 2 * 2:2]
    slack = jnp.minimum(sizes[source_of] - 1, bound - sizes[taker]) // 2
    slack = jnp.where((source_of == sequence[0]) | (taker == sequence[0]) | (sizes[taker] == 0), 0, jnp.maximum(slack, 0))
    moved = jax.random.randint(jax.random.fold_in(own, 4), (amount // 2,), 0, 1 << 20) % (slack + 1)
    sizes = sizes.at[source_of].add(-moved).at[taker].add(moved)
    items = jnp.searchsorted(jnp.cumsum(sizes), jnp.arange(rows * top), side="right").astype(jnp.int32)
    table = items.reshape(top, rows).T
    table = table[jax.random.permutation(jax.random.fold_in(own, 1), rows)]
    offset_by = jax.random.randint(jax.random.fold_in(own, 2), (rows, 1), 0, top)
    return jnp.take_along_axis(table, (jnp.arange(top)[None, :] + offset_by) % top, axis=1)


def portions_of(amount, total, most, lean, full):
    loads = [(1 << 20) // math.isqrt(standing ** lean) + 1 for standing in range(1, amount + 1)]
    largest = most if full else min(most, max(-(-total // amount), total * loads[0] // sum(loads)))
    least = 1 if total - largest >= amount - 1 else 0
    counts, surplus = [largest] + [least] * (amount - 1), total - largest - least * (amount - 1)
    while surplus > 0:
        candidates = [i for i in range(1, amount) if counts[i] < largest] or [i for i in range(1, amount) if counts[i] < most]
        mass, left = sum([loads[i] for i in candidates]), surplus
        for i in candidates:
            more = min(most - counts[i], max(1, left * loads[i] // mass), surplus)
            counts[i] = counts[i] + more
            surplus = surplus - more
    return np.array(counts)


def normal_values(own_key, dims, spread, reach, shards=(), kind=jnp.bfloat16):
    entries = jax.random.normal(own_key, dims, jnp.float32) * spread
    if len(shards) > 0:
        entries = level_of(own_key, dims, shards, -0.22, 0.18) * entries
    return jnp.clip(entries, min=-reach, max=reach).astype(kind)


def setup_inputs(seed: int = 0) -> dict:
    key_list = jax.random.split(jax.random.key(seed), 17)
    hidden_in = normal_values(key_list[0], (ROWS, SEQ_LEN, D), 1.0, 6.0, ((0, 4), (1, 8)))
    segment_ids = draw_segment_ids(jax.random.fold_in(key_list[16], 71), 0)
    expert_ids_keys = jax.random.split(jax.random.fold_in(key_list[2], 1), ROWS * SEQ_LEN // TOK_DEV)
    expert_ids_turns = jax.random.permutation(jax.random.fold_in(key_list[2], 3), ROWS * SEQ_LEN // TOK_DEV)
    expert_ids = jax.vmap(lambda own, number: shared_out(jax.random.fold_in(key_list[2], 2), own, number, TOK_DEV, EXPERTS, TOP_K, CAPACITY, 1))(expert_ids_keys, expert_ids_turns).reshape((ROWS, SEQ_LEN, TOP_K))
    attention_gain = jnp.clip(1.0 + 0.1 * jax.random.normal(key_list[3], (D,), jnp.float32), 0.5, 1.5).astype(jnp.bfloat16)
    query_gain = jnp.clip(1.0 + 0.1 * jax.random.normal(key_list[4], (D,), jnp.float32), 0.5, 1.5).astype(jnp.bfloat16)
    key_gain = jnp.clip(1.0 + 0.1 * jax.random.normal(key_list[5], (D,), jnp.float32), 0.5, 1.5).astype(jnp.bfloat16)
    expert_gain = jnp.clip(1.0 + 0.1 * jax.random.normal(key_list[6], (D,), jnp.float32), 0.5, 1.5).astype(jnp.bfloat16)
    query_weight = normal_values(key_list[7], (D, D), D ** -0.5, 0.125, ((0, 32),))
    key_weight = normal_values(key_list[8], (D, D), D ** -0.5, 0.125, ((0, 32),))
    value_weight = normal_values(key_list[9], (D, D), D ** -0.5, 0.125, ((0, 32),))
    output_weight = normal_values(key_list[10], (D, D), (D // 64) ** -0.5, 1.0, ((0, 32),))
    router_weight = normal_values(key_list[11], (D, EXPERTS), (4 * D) ** -0.5, 0.0625, ((0, 32),))
    gate_weight = normal_values(key_list[12], (2 * EXPERTS, D, HALF_FF), D ** -0.5, 0.125, ((0, 32),))
    up_weight = normal_values(key_list[13], (2 * EXPERTS, D, HALF_FF), D ** -0.5, 0.125, ((0, 32),))
    down_weight = normal_values(key_list[14], (2 * EXPERTS, HALF_FF, D), (FF // 16) ** -0.5, 0.75, ((0, 32),))
    grad_out = normal_values(key_list[15], (ROWS, SEQ_LEN, D), 1.0, 6.0, ((0, 4), (1, 8)))
    return {"hidden_in": hidden_in, "segment_ids": segment_ids, "expert_ids": expert_ids, "attention_gain": attention_gain, "query_gain": query_gain, "key_gain": key_gain, "expert_gain": expert_gain, "query_weight": query_weight, "key_weight": key_weight, "value_weight": value_weight, "output_weight": output_weight, "router_weight": router_weight, "gate_weight": gate_weight, "up_weight": up_weight, "down_weight": down_weight, "grad_out": grad_out}


@jax.custom_vjp
def low(v):
    return lax.optimization_barrier(v.astype(jnp.bfloat16)).astype(jnp.float32)

@jax.custom_vjp
def low_back(v):
    return v

def low_keep(v):
    return (low(v), None)

def low_pass(kept, grad):
    return (grad,)

def back_keep(v):
    return (v, None)

def back_low(kept, grad):
    return (low(grad),)
low.defvjp(low_keep, low_pass)
low_back.defvjp(back_keep, back_low)
epsilon = 1e-05
masked_score = -1e+30
highest = lax.Precision.HIGHEST

def rms_scale(values, norm_gain):
    return values * lax.rsqrt(lax.optimization_barrier(jnp.mean(values * values, axis=-1, keepdims=True)) + epsilon) * norm_gain

def rotate_heads(values, positions):
    half_width = values.shape[-1] // 2
    frequency = jnp.exp(-math.log(10000.0) * 2.0 * jnp.arange(half_width, dtype=jnp.float32) / values.shape[-1])
    angles = positions.astype(jnp.float32)[:, None, None] * frequency[None, None, :]
    cosine = jnp.cos(angles)
    sine_part = jnp.sin(angles)
    leading = values[..., :half_width]
    trailing = values[..., half_width:]
    return jnp.concatenate([leading * cosine - trailing * sine_part, trailing * cosine + leading * sine_part], axis=-1)

def matmul(left_side, right_side):
    return jnp.dot(left_side, right_side, precision=highest, preferred_element_type=jnp.float32)

def row_attention(query_rot, key_rot, value_heads, segments):
    block_rows = min(512, SEQ_LEN)
    key_positions = jnp.arange(SEQ_LEN, dtype=jnp.int32)
    score_scale = HEAD_DIM ** (-0.5)

    def one_block(block_number):
        row_start = (block_number * block_rows).astype(jnp.int32)
        query_block = lax.dynamic_slice_in_dim(query_rot, row_start, block_rows, 0)
        query_segments = lax.dynamic_slice_in_dim(segments, row_start, block_rows, 0)
        query_positions = row_start + jnp.arange(block_rows, dtype=jnp.int32)
        scores = low_back(jnp.einsum('qhd,khd->hqk', query_block, key_rot, precision=highest) * score_scale)
        allowed = (key_positions[None, :] <= query_positions[:, None]) & (segments[None, :] == query_segments[:, None])
        scores = jnp.where(allowed[None], scores, masked_score)
        weights = jnp.where(allowed[None], jnp.exp(scores - lax.optimization_barrier(jnp.max(scores, axis=-1, keepdims=True))), 0.0)
        probabilities = weights / lax.optimization_barrier(jnp.sum(weights, axis=-1, keepdims=True))
        return jnp.einsum('hqk,khd->qhd', low(probabilities), value_heads, precision=highest)
    blocks_out = lax.map(jax.checkpoint(one_block), jnp.arange(SEQ_LEN // block_rows, dtype=jnp.int32))
    return blocks_out.reshape(SEQ_LEN, HEADS, HEAD_DIM)

def slot_tables(expert_ids):
    flat_routes = expert_ids.reshape(DEVICES, TOK_DEV * TOP_K).astype(jnp.int32)
    route_ones = (flat_routes[:, :, None] == jnp.arange(EXPERTS, dtype=jnp.int32)[None, None, :]).astype(jnp.int32)
    earlier = (jnp.cumsum(route_ones, axis=1) - route_ones).astype(jnp.int32)
    places = lax.optimization_barrier(jnp.sum(earlier * route_ones, axis=2)).astype(jnp.int32)
    sources = jnp.broadcast_to(jnp.arange(DEVICES, dtype=jnp.int32)[:, None], flat_routes.shape)
    pair_index = jnp.arange(DEVICES * TOK_DEV * TOP_K, dtype=jnp.int32).reshape(flat_routes.shape)
    pair_of_slot = jnp.zeros((EXPERTS, DEVICES, CAPACITY), jnp.int32).at[flat_routes, sources, places].set(pair_index)
    slot_live = jnp.zeros((EXPERTS, DEVICES, CAPACITY), jnp.int32).at[flat_routes, sources, places].set(1)
    return (pair_of_slot.reshape(EXPERTS, DEVICES * CAPACITY), slot_live.reshape(EXPERTS, DEVICES * CAPACITY))

def reference(hidden_in, segment_ids, expert_ids, attention_gain, query_gain, key_gain, expert_gain, query_weight, key_weight, value_weight, output_weight, router_weight, gate_weight, up_weight, down_weight, grad_out):
    pair_of_slot, slot_live = slot_tables(expert_ids)
    live_float = slot_live.astype(jnp.float32)
    positions = jnp.arange(SEQ_LEN, dtype=jnp.int32)
    flat_routes = expert_ids.reshape(ROWS * SEQ_LEN, TOP_K).astype(jnp.int32)

    def forward(residual_in, gain_attn, gain_query, gain_key, gain_expert, query_matrix, key_matrix, value_matrix, output_matrix, router_matrix, gate_matrix, up_matrix, down_matrix):
        normed_low = low(rms_scale(residual_in, gain_attn)).reshape(ROWS * SEQ_LEN, D)
        query_pre = low_back(matmul(normed_low, query_matrix))
        key_pre = low_back(matmul(normed_low, key_matrix))
        value_rows = low(low_back(matmul(normed_low, value_matrix)))
        query_rot = low(rotate_heads(rms_scale(query_pre, gain_query).reshape(ROWS, SEQ_LEN, HEADS, HEAD_DIM), positions))
        key_rot = low(rotate_heads(rms_scale(key_pre, gain_key).reshape(ROWS, SEQ_LEN, HEADS, HEAD_DIM), positions))
        value_heads = value_rows.reshape(ROWS, SEQ_LEN, HEADS, HEAD_DIM)

        def one_row(row_items):
            return row_attention(row_items[0], row_items[1], row_items[2], row_items[3])
        attended = lax.map(one_row, (query_rot, key_rot, value_heads, segment_ids))
        attended_low = low(low_back(attended.reshape(ROWS * SEQ_LEN, D)))
        attention_proj = low_back(matmul(attended_low, output_matrix))
        residual_mid = residual_in.reshape(ROWS * SEQ_LEN, D) + attention_proj
        expert_in = low(rms_scale(residual_mid, gain_expert))
        logits = low_back(matmul(expert_in, router_matrix))
        picked = jnp.take_along_axis(logits, flat_routes, axis=1)
        gate_probs = jax.nn.softmax(picked, axis=-1).reshape(-1)
        gate_halves = gate_matrix.reshape(EXPERTS, 2, D, HALF_FF)
        up_halves = up_matrix.reshape(EXPERTS, 2, D, HALF_FF)
        down_halves = down_matrix.reshape(EXPERTS, 2, HALF_FF, D)

        def expert_step(mixed_sum, expert_item):
            gate_pair, up_pair, down_pair, slot_pairs, live = expert_item
            token_rows = slot_pairs // TOP_K
            rows_in = expert_in[token_rows] * live[:, None]
            expert_out = jnp.zeros((slot_pairs.shape[0], D), jnp.float32)
            for which_half in range(2):
                half_in = low_back(rows_in)
                gate_pre = low_back(matmul(half_in, gate_pair[which_half]))
                up_pre = low_back(matmul(half_in, up_pair[which_half]))
                hidden_low = low(jax.nn.silu(gate_pre) * up_pre)
                expert_out = expert_out + low(low_back(matmul(hidden_low, down_pair[which_half])))
            weighted = expert_out * (gate_probs[slot_pairs] * live)[:, None]
            return (mixed_sum.at[token_rows].add(weighted), None)
        mixed, ignored = lax.scan(jax.checkpoint(expert_step), jnp.zeros_like(residual_mid), (gate_halves, up_halves, down_halves, pair_of_slot, live_float))
        return (residual_mid + mixed).reshape(ROWS, SEQ_LEN, D)
    layer_sum, pullback = jax.vjp(forward, hidden_in.astype(jnp.float32), attention_gain.astype(jnp.float32), query_gain.astype(jnp.float32), key_gain.astype(jnp.float32), expert_gain.astype(jnp.float32), query_weight.astype(jnp.float32), key_weight.astype(jnp.float32), value_weight.astype(jnp.float32), output_weight.astype(jnp.float32), router_weight.astype(jnp.float32), gate_weight.astype(jnp.float32), up_weight.astype(jnp.float32), down_weight.astype(jnp.float32))
    grads = pullback(grad_out.astype(jnp.float32))
    return (layer_sum.astype(jnp.bfloat16), grads[0], grads[1], grads[2], grads[3], grads[4], grads[5], grads[6], grads[7], grads[8], grads[9], grads[10], grads[11], grads[12])
```

```python
import math

import jax
import jax.numpy as jnp
from jax import lax
from jax.sharding import PartitionSpec as P

HEADS = 16
HEAD_DIM = 128
TOP_K = 8

epsilon = 1e-05
masked_score = -1e30
BOTH = ("row", "blk")
bf16 = jnp.bfloat16
f32 = jnp.float32


def mm(a, b):
    return jnp.dot(a, b, preferred_element_type=f32)


def mm_tn(a, b):
    return lax.dot_general(a, b, (((0,), (0,)), ((), ())), preferred_element_type=f32)


def mm_nt(a, b):
    return lax.dot_general(a, b, (((1,), (1,)), ((), ())), preferred_element_type=f32)


def rope_tables(count):
    half = HEAD_DIM // 2
    frequency = jnp.exp(
        -math.log(10000.0) * 2.0 * jnp.arange(half, dtype=f32) / HEAD_DIM
    )
    angles = jnp.arange(count, dtype=f32)[:, None] * frequency[None, :]
    return jnp.cos(angles)[:, None, :], jnp.sin(angles)[:, None, :]


def rope(values, cosine, sine):
    half = HEAD_DIM // 2
    a, b = values[..., :half], values[..., half:]
    return jnp.concatenate([a * cosine - b * sine, b * cosine + a * sine], axis=-1)


def norm_back(v, r, g, c, mean_vgc):
    return r * g * c - v * (r * r * r) * mean_vgc


def body(
    hidden_in,
    segment_ids,
    expert_ids,
    attention_gain,
    query_gain,
    key_gain,
    expert_gain,
    query_weight,
    key_weight,
    value_weight,
    output_weight,
    router_weight,
    gate_weight,
    up_weight,
    down_weight,
    grad_out,
):
    tokens = hidden_in.shape[1]
    width = hidden_in.shape[2]
    experts = router_weight.shape[1]
    rows, blocks = lax.axis_size("row"), lax.axis_size("blk")
    devices = rows * blocks
    seq = tokens * blocks
    head_cols = width // blocks
    heads_here = HEADS // blocks
    blk = lax.axis_index("blk")
    me = lax.axis_index("row") * blocks + blk
    scale = HEAD_DIM**-0.5

    small = jnp.concatenate(
        [
            router_weight,
            attention_gain[:, None],
            query_gain[:, None],
            key_gain[:, None],
            expert_gain[:, None],
        ],
        axis=1,
    )
    small = lax.all_gather(small, BOTH, axis=0, tiled=True)
    router = small[:, :experts]
    gains = small[:, experts:].astype(f32)
    gain_attn, gain_expert = gains[:, 0], gains[:, 3]
    own_q_gain = lax.dynamic_slice_in_dim(gains[:, 1], blk * head_cols, head_cols)
    own_k_gain = lax.dynamic_slice_in_dim(gains[:, 2], blk * head_cols, head_cols)

    x = hidden_in[0].astype(f32)
    r_attn = lax.rsqrt(jnp.mean(x * x, axis=-1, keepdims=True) + epsilon)
    normed = (x * r_attn * gain_attn).astype(bf16)
    normed_row = lax.all_gather(normed, "blk", axis=0, tiled=True)
    segments = lax.all_gather(segment_ids[0], "blk", axis=0, tiled=True)

    stacked = jnp.stack([query_weight, key_weight, value_weight], axis=0)
    wrows = stacked.shape[1]
    stacked = stacked.reshape(3, wrows, blocks, head_cols).transpose(2, 1, 0, 3)
    stacked = stacked.reshape(blocks, wrows, 3 * head_cols)
    cols = lax.all_to_all(stacked, "blk", split_axis=0, concat_axis=0, tiled=True)
    cols = cols.reshape(blocks * wrows, 3 * head_cols)
    qkv_cols = lax.all_gather(cols, "row", axis=0, tiled=True)
    full_output = lax.all_gather(output_weight, BOTH, axis=0, tiled=True)

    qkv = mm(normed_row, qkv_cols)
    query_pre = qkv[:, :head_cols]
    key_pre = qkv[:, head_cols : 2 * head_cols]
    value = qkv[:, 2 * head_cols :].astype(bf16)
    squares = jnp.stack(
        [jnp.sum(query_pre * query_pre, axis=-1), jnp.sum(key_pre * key_pre, axis=-1)]
    )
    squares = lax.psum(squares, "blk") / width
    r_q = lax.rsqrt(squares[0] + epsilon)[:, None]
    r_k = lax.rsqrt(squares[1] + epsilon)[:, None]
    cosine, sine = rope_tables(seq)

    def heads(v):
        return v.reshape(seq, heads_here, HEAD_DIM)

    query = rope(heads(query_pre * r_q * own_q_gain), cosine, sine).astype(bf16)
    key = rope(heads(key_pre * r_k * own_k_gain), cosine, sine).astype(bf16)
    value = heads(value)
    places = jnp.arange(seq, dtype=jnp.int32)
    allowed = (places[None, :] <= places[:, None]) & (
        segments[None, :] == segments[:, None]
    )
    scores = jnp.einsum("qhd,khd->hqk", query, key, preferred_element_type=f32) * scale
    scores = jnp.where(allowed[None], scores, masked_score)
    top = jnp.max(scores, axis=-1, keepdims=True)
    weights = jnp.where(allowed[None], jnp.exp(scores - top), 0.0)
    total = jnp.sum(weights, axis=-1, keepdims=True)
    probs = weights / total
    probs_low = probs.astype(bf16)
    attended = jnp.einsum("hqk,khd->qhd", probs_low, value, preferred_element_type=f32)
    attended_low_cols = attended.astype(bf16).reshape(blocks, tokens, head_cols)
    attended_low = lax.all_to_all(
        attended_low_cols, "blk", split_axis=0, concat_axis=0, tiled=True
    )
    attended_low = attended_low.transpose(1, 0, 2).reshape(tokens, width)

    residual_mid = x + mm(attended_low, full_output)
    r_exp = lax.rsqrt(
        jnp.mean(residual_mid * residual_mid, axis=-1, keepdims=True) + epsilon
    )
    expert_in = (residual_mid * r_exp * gain_expert).astype(bf16)
    logits = mm(expert_in, router)
    routes = expert_ids[0]
    routed = jnp.any(
        routes[:, :, None] == jnp.arange(experts, dtype=jnp.int32)[None, None, :],
        axis=1,
    )
    top_logit = jnp.max(
        jnp.where(routed, logits, masked_score), axis=-1, keepdims=True
    )
    gates = jnp.where(routed, jnp.exp(logits - top_logit), 0.0)
    gates = gates / jnp.sum(gates, axis=-1, keepdims=True)

    gate_local, up_local, down_local = gate_weight[0], up_weight[0], down_weight[0]
    parts = devices * tokens // 2048
    step = tokens // parts
    all_gates = lax.all_gather(gates, BOTH, axis=0, tiled=False)
    own_gate = jnp.sum(
        jnp.where(
            jnp.arange(experts, dtype=jnp.int32)[None, None, :] == me // 2,
            all_gates,
            0.0,
        ),
        axis=-1,
    )

    def expert_part(sums, items):
        own_rows, own_upstream, gate_col = items
        got = lax.all_gather(own_rows, BOTH, axis=0, tiled=True)
        up_stream = lax.all_gather(own_upstream, BOTH, axis=0, tiled=True)
        gate_col = gate_col.reshape(devices * step, 1)
        gate_pre = mm(got, gate_local)
        up_pre = mm(got, up_local)
        sig = jax.nn.sigmoid(gate_pre)
        silu = gate_pre * sig
        hidden = (silu * up_pre).astype(bf16)
        part_f = mm(hidden, down_local).astype(bf16).astype(f32)
        up_f = up_stream.astype(f32)
        dots = jnp.sum(part_f * up_f, axis=-1).reshape(devices, step)
        mixed = (gate_col * part_f).astype(bf16)
        out = lax.psum_scatter(mixed, BOTH, scatter_dimension=0, tiled=True)
        grad_part = (gate_col * up_f).astype(bf16)
        grad_hidden = mm_nt(grad_part, down_local)
        grad_gate_pre = (
            grad_hidden * up_pre * sig * (1.0 + gate_pre * (1.0 - sig))
        ).astype(bf16)
        grad_up_pre = (grad_hidden * silu).astype(bf16)
        grad_rows = (
            mm_nt(grad_gate_pre, gate_local) + mm_nt(grad_up_pre, up_local)
        ).astype(bf16)
        back = lax.psum_scatter(grad_rows, BOTH, scatter_dimension=0, tiled=True)
        sums = (
            sums[0] + mm_tn(got, grad_gate_pre),
            sums[1] + mm_tn(got, grad_up_pre),
            sums[2] + mm_tn(hidden, grad_part),
        )
        return sums, (out, back, dots)

    sums = (
        jnp.zeros(gate_local.shape, f32),
        jnp.zeros(up_local.shape, f32),
        jnp.zeros(down_local.shape, f32),
    )
    items = (
        expert_in.reshape(parts, step, width),
        grad_out[0].reshape(parts, step, width),
        own_gate.reshape(devices, parts, step).transpose(1, 0, 2),
    )
    if parts > 2:
        sums, (outs, backs, dots) = lax.scan(expert_part, sums, items)
    else:
        made = []
        for part in range(parts):
            sums, result = expert_part(sums, tuple(item[part] for item in items))
            made.append(result)
        outs, backs, dots = (jnp.stack(some) for some in zip(*made))
    grad_gate_local, grad_up_local, grad_down_local = sums
    dots = dots.transpose(1, 0, 2).reshape(devices, tokens)
    outs = outs.reshape(tokens, width)
    backs = backs.reshape(tokens, width)
    dots = lax.all_to_all(dots, BOTH, split_axis=0, concat_axis=0, tiled=True)
    grad_gates = jnp.sum(dots.reshape(experts, 2, tokens), axis=1).T
    moe_out = outs.astype(f32)
    layer_out = (residual_mid + moe_out).astype(bf16)
    upstream = grad_out[0].astype(f32)
    grad_picked = gates * (
        grad_gates - jnp.sum(gates * grad_gates, axis=-1, keepdims=True)
    )
    grad_logits = jnp.where(routed, grad_picked, 0.0).astype(bf16)
    grad_expert_in = backs.astype(f32) + mm_nt(
        grad_logits, router
    )
    grad_router = mm_tn(expert_in, grad_logits)
    grad_gain_expert = jnp.sum(grad_expert_in * residual_mid * r_exp, axis=0)
    grad_mid = upstream + norm_back(
        residual_mid,
        r_exp,
        gain_expert,
        grad_expert_in,
        jnp.mean(residual_mid * gain_expert * grad_expert_in, axis=-1, keepdims=True),
    )
    grad_proj = grad_mid.astype(bf16)
    grad_output_w = mm_tn(attended_low, grad_proj).astype(bf16)
    grad_output_w = lax.psum_scatter(
        grad_output_w, BOTH, scatter_dimension=0, tiled=True
    ).astype(f32)
    grad_attended = mm_nt(grad_proj, full_output).astype(bf16)
    grad_attended = grad_attended.reshape(tokens, blocks, head_cols).transpose(1, 0, 2)
    grad_attended = lax.all_to_all(
        grad_attended, "blk", split_axis=0, concat_axis=0, tiled=True
    )
    grad_attended = grad_attended.reshape(seq, heads_here, HEAD_DIM)
    row_delta = jnp.sum(grad_attended.astype(f32) * attended, axis=-1).T
    grad_probs = jnp.einsum(
        "qhd,khd->hqk", grad_attended, value, preferred_element_type=f32
    )
    grad_scores = (probs * (grad_probs - row_delta[:, :, None])).astype(bf16)
    grad_value = jnp.einsum(
        "hqk,qhd->khd", probs_low, grad_attended, preferred_element_type=f32
    ).astype(bf16)
    grad_query = (
        jnp.einsum("hqk,khd->qhd", grad_scores, key, preferred_element_type=f32) * scale
    )
    grad_key = (
        jnp.einsum("hqk,qhd->khd", grad_scores, query, preferred_element_type=f32)
        * scale
    )
    grad_query = rope(grad_query, cosine, -sine).reshape(seq, head_cols)
    grad_key = rope(grad_key, cosine, -sine).reshape(seq, head_cols)
    means = jnp.stack(
        [
            jnp.sum(query_pre * own_q_gain * grad_query, axis=-1),
            jnp.sum(key_pre * own_k_gain * grad_key, axis=-1),
        ]
    )
    means = lax.psum(means, "blk") / width
    grad_q_gain = jnp.sum(grad_query * query_pre * r_q, axis=0)
    grad_k_gain = jnp.sum(grad_key * key_pre * r_k, axis=0)
    grad_query_pre = norm_back(query_pre, r_q, own_q_gain, grad_query, means[0][:, None])
    grad_key_pre = norm_back(key_pre, r_k, own_k_gain, grad_key, means[1][:, None])
    grad_qkv = jnp.concatenate(
        [
            grad_query_pre.astype(bf16),
            grad_key_pre.astype(bf16),
            grad_value.reshape(seq, head_cols),
        ],
        axis=1,
    )
    grad_w = mm_tn(normed_row, grad_qkv).astype(bf16)
    grad_w = lax.psum_scatter(grad_w, "row", scatter_dimension=0, tiled=True)
    grad_w = grad_w.reshape(blocks, wrows, 3 * head_cols)
    grad_w = lax.all_to_all(grad_w, "blk", split_axis=0, concat_axis=0, tiled=True)
    grad_w = grad_w.reshape(blocks, wrows, 3, head_cols).transpose(2, 1, 0, 3)
    grad_w = grad_w.reshape(3, wrows, width).astype(f32)
    grad_normed = mm_nt(grad_qkv, qkv_cols).astype(bf16)
    grad_normed = lax.psum_scatter(
        grad_normed, "blk", scatter_dimension=0, tiled=True
    ).astype(f32)
    grad_gain_attn = jnp.sum(grad_normed * x * r_attn, axis=0)
    input_grad = grad_mid + norm_back(
        x,
        r_attn,
        gain_attn,
        grad_normed,
        jnp.mean(x * gain_attn * grad_normed, axis=-1, keepdims=True),
    )

    def placed(vector):
        return lax.dynamic_update_slice_in_dim(
            jnp.zeros((width,), f32), vector, blk * head_cols, axis=0
        )

    small_grads = jnp.concatenate(
        [
            grad_router,
            grad_gain_attn[:, None],
            placed(grad_q_gain)[:, None],
            placed(grad_k_gain)[:, None],
            grad_gain_expert[:, None],
        ],
        axis=1,
    )
    small_grads = lax.psum_scatter(small_grads, BOTH, scatter_dimension=0, tiled=True)
    return (
        layer_out[None],
        input_grad[None],
        small_grads[:, experts],
        small_grads[:, experts + 1],
        small_grads[:, experts + 2],
        small_grads[:, experts + 3],
        grad_w[0],
        grad_w[1],
        grad_w[2],
        grad_output_w,
        small_grads[:, :experts],
        grad_gate_local[None],
        grad_up_local[None],
        grad_down_local[None],
    )


def solution(mesh):
    tokens3 = P("row", "blk", None)
    vector, matrix, cube = P(BOTH), P(BOTH, None), P(BOTH, None, None)
    return jax.shard_map(
        body,
        mesh=mesh,
        in_specs=(
            tokens3,
            P("row", "blk"),
            tokens3,
            vector,
            vector,
            vector,
            vector,
            matrix,
            matrix,
            matrix,
            matrix,
            matrix,
            cube,
            cube,
            cube,
            tokens3,
        ),
        out_specs=(
            tokens3,
            tokens3,
            vector,
            vector,
            vector,
            vector,
            matrix,
            matrix,
            matrix,
            matrix,
            matrix,
            cube,
            cube,
            cube,
        ),
        check_vma=False,
    )
```

```python
import functools
import math

import jax
import jax.numpy as jnp
from jax import lax
from jax.experimental import pallas as pl
from jax.experimental.pallas import tpu as pltpu
from jax.sharding import PartitionSpec as P

HEADS = 16
HEAD_DIM = 128
TOP_K = 8

epsilon = 1e-05
masked_score = -1e30
BOTH = ("row", "blk")
MESH = pl.DeviceIdType.MESH
bf16 = jnp.bfloat16
f32 = jnp.float32
EXTRA = 128


def dot(a, b):
    return jnp.dot(a, b, preferred_element_type=f32)


def dot_nt(a, b):
    return lax.dot_general(a, b, (((1,), (1,)), ((), ())), preferred_element_type=f32)


def dot_tn(a, b):
    return lax.dot_general(a, b, (((0,), (0,)), ((), ())), preferred_element_type=f32)


def place():
    row, blk = lax.axis_index("row"), lax.axis_index("blk")
    return row, blk // 2, blk % 2


def partners():
    row, z, c = place()
    blk = z * 2 + c
    return {
        "sib": (row, z * 2 + (1 - c)),
        "x": (row ^ 1, blk),
        "y": (row ^ 2, blk),
        "z1": (row, ((z + 1) % 4) * 2 + c),
        "z2": (row, ((z + 2) % 4) * 2 + c),
        "z3": (row, ((z + 3) % 4) * 2 + c),
    }


def remote(src, dst, send, recv, to):
    return pltpu.make_async_remote_copy(
        src_ref=src,
        dst_ref=dst,
        send_sem=send,
        recv_sem=recv,
        device_id=to,
        device_id_type=MESH,
    )


def greet(targets):
    barrier = pltpu.get_barrier_semaphore()
    for to in targets:
        pl.semaphore_signal(barrier, inc=1, device_id=to, device_id_type=MESH)
    pl.semaphore_wait(barrier, len(targets))


def moe_kernel(
    steps,
    x_ref,
    c_ref,
    mask_ref,
    router_ref,
    wgu_ref,
    wd_ref,
    xall,
    out_ref,
    back_ref,
    dwg_ref,
    dwu_ref,
    dwd_ref,
    xbuf,
    cbuf,
    hbuf,
    gbuf,
    po,
    pb,
    ro,
    rb,
    so,
    sb,
    p1ao,
    p1bo,
    p1ab,
    p1bb,
    p2o,
    p2b,
    zo,
    zb,
    ag_send,
    ag_recv,
    rs_send,
    rs_recv,
    load_sem,
):
    row, z, c = place()
    to = partners()
    width = x_ref.shape[-1]
    half = width // 2
    hidden = wd_ref.shape[0]
    me = row * 8 + z * 2 + c
    expert = me // 2

    greet(list(to.values()))

    def ag(j, k, src, dst, who):
        return remote(src, dst, ag_send.at[j, k], ag_recv.at[j, k], to[who])

    def own_copy(j):
        return pltpu.make_async_copy(
            x_ref.at[j], xall.at[j, row, z, c], load_sem.at[2 + j % 4]
        )

    def z_copies(j):
        slot = xall.at[j, row, z, c]
        return [ag(j, k, x_ref.at[j], slot, "z%d" % (k + 1)) for k in range(3)]

    def line_copies(j):
        line = xall.at[j, row, :, c]
        return [
            ag(j, 3, line, line, "x"),
            ag(j, 4, line, line, "y"),
            ag(j, 5, line, line, "sib"),
        ]

    def relay_copies(j):
        a = xall.at[j, row ^ 1, :, c, :, pl.ds(0, half)]
        b = xall.at[j, row ^ 2, :, c, :, pl.ds(half, half)]
        s1 = xall.at[j, row ^ 1, :, c]
        s2 = xall.at[j, row ^ 2, :, c]
        return [
            ag(j, 6, a, a, "y"),
            ag(j, 7, b, b, "x"),
            ag(j, 8, s1, s1, "sib"),
            ag(j, 9, s2, s2, "sib"),
        ]

    def last_copies(j):
        s3 = xall.at[j, row ^ 3, :, c]
        return [ag(j, 10, s3, s3, "sib")]

    def ag_z(j):
        own_copy(j).start()
        for cp in z_copies(j):
            cp.start()

    def ag_xy(j):
        own_copy(j).wait()
        for cp in z_copies(j):
            cp.wait_recv()
        for cp in line_copies(j):
            cp.start()

    def ag_rel(j):
        for cp in line_copies(j)[:2]:
            cp.wait_recv()
        for cp in relay_copies(j):
            cp.start()

    def ag_fin(j):
        for cp in relay_copies(j)[:2]:
            cp.wait_recv()
        for cp in last_copies(j):
            cp.start()

    def loads(j):
        return [
            pltpu.make_async_copy(xall.at[j], xbuf.at[j % 2], load_sem.at[0]),
            pltpu.make_async_copy(
                c_ref.at[:, :, :, j], cbuf.at[j % 2], load_sem.at[1]
            ),
        ]

    def ag_done(j):
        line_copies(j)[2].wait_recv()
        for cp in relay_copies(j)[2:] + last_copies(j):
            cp.wait_recv()
        for cp in loads(j):
            cp.start()

    def ag_sent(j):
        for cp in z_copies(j) + line_copies(j) + relay_copies(j) + last_copies(j):
            cp.wait_send()

    arrays = (
        (po, ro, so, p1ao, p1bo, p2o, zo, out_ref),
        (pb, rb, sb, p1ab, p1bb, p2b, zb, back_ref),
    )

    def rs(i, q, k, src, dst, who):
        s = i % 2
        return remote(src, dst, rs_send.at[q, s, k], rs_recv.at[q, s, k], to[who])

    def rs_sib_copy(q, i):
        p, r = arrays[q][:2]
        return rs(i, q, 0, p.at[:, :, 1 - c], r.at[i % 2], "sib")

    def p1_copies(q, i):
        p, r, s, p1a, p1b, p2, zz, out = arrays[q]
        part = s.at[i % 2, row ^ 3]
        rest = p.shape[-1] - half
        return [
            rs(i, q, 1, part.at[:, :, pl.ds(0, half)], p1a.at[i % 2], "y"),
            rs(i, q, 2, part.at[:, :, pl.ds(half, rest)], p1b.at[i % 2], "x"),
        ]

    def p2_copies(q, i):
        p, r, s, p1a, p1b, p2, zz, out = arrays[q]
        return [
            rs(i, q, 3, s.at[i % 2, row ^ 1], p2.at[i % 2, 0], "x"),
            rs(i, q, 4, s.at[i % 2, row ^ 2], p2.at[i % 2, 1], "y"),
        ]

    def rsz_copies(q, i):
        p, r, s, p1a, p1b, p2, zz, out = arrays[q]
        return [
            rs(
                i,
                q,
                5 + k,
                s.at[i % 2, row, (z + k + 1) % 4],
                zz.at[i % 2, k],
                "z%d" % (k + 1),
            )
            for k in range(3)
        ]

    def rs_sib(q, i):
        rs_sib_copy(q, i).start()

    def rs_p1(q, i):
        p, r, s, p1a, p1b, p2, zz, out = arrays[q]
        cp = rs_sib_copy(q, i)
        cp.wait_recv()

        @pl.loop(0, 4)
        def _(a):
            s[i % 2, a] = (
                p[a, :, c].astype(f32) + r[i % 2, a].astype(f32)
            ).astype(bf16)

        cp.wait_send()
        for cp in p1_copies(q, i):
            cp.start()

    def rs_p2(q, i):
        p, r, s, p1a, p1b, p2, zz, out = arrays[q]
        rest = p.shape[-1] - half
        copies = p1_copies(q, i)
        copies[0].wait_recv()
        at = s.at[i % 2, row ^ 1]
        at[:, :, pl.ds(0, half)] = (
            at[:, :, pl.ds(0, half)].astype(f32) + p1a[i % 2].astype(f32)
        ).astype(bf16)
        out_copies = p2_copies(q, i)
        out_copies[0].start()
        copies[1].wait_recv()
        at = s.at[i % 2, row ^ 2]
        at[:, :, pl.ds(half, rest)] = (
            at[:, :, pl.ds(half, rest)].astype(f32) + p1b[i % 2].astype(f32)
        ).astype(bf16)
        out_copies[1].start()

    def rs_z(q, i):
        p, r, s, p1a, p1b, p2, zz, out = arrays[q]
        for cp in p2_copies(q, i):
            cp.wait_recv()
        s[i % 2, row] = (
            s[i % 2, row].astype(f32)
            + p2[i % 2, 0].astype(f32)
            + p2[i % 2, 1].astype(f32)
        ).astype(bf16)
        for cp in rsz_copies(q, i):
            cp.start()

    def rs_fin(q, i):
        p, r, s, p1a, p1b, p2, zz, out = arrays[q]
        copies = rsz_copies(q, i)
        for cp in copies:
            cp.wait_recv()
        total = s[i % 2, row, z].astype(f32)
        for k in range(3):
            total = total + zz[i % 2, k].astype(f32)
        out[i] = total
        for cp in copies + p2_copies(q, i) + p1_copies(q, i):
            cp.wait_send()

    lanes = po.shape[3]
    rows_here = 16 * lanes
    cut = 512

    def tile(i, t):
        s = i % 2
        xt = xbuf[s, 2 * t : 2 * t + 2].reshape(rows_here, width)
        mask = mask_ref[i, t * rows_here : (t + 1) * rows_here, :]
        logits = dot(xt, router_ref[...])[:, : mask.shape[-1]]
        logits = jnp.where(mask > 0, logits, masked_score)
        top = jnp.max(logits, axis=-1, keepdims=True)
        raised = jnp.where(mask > 0, jnp.exp(logits - top), 0.0)
        lane = lax.broadcasted_iota(jnp.int32, raised.shape, 1)
        gate = jnp.sum(
            jnp.where(lane == expert, raised, 0.0), axis=-1, keepdims=True
        ) / jnp.sum(raised, axis=-1, keepdims=True)
        both = dot(xt, wgu_ref[...])
        gp, up = both[:, :hidden], both[:, hidden:]
        sig = jax.nn.sigmoid(gp)
        silu = gp * sig
        hid = (silu * up).astype(bf16)
        hbuf[t * rows_here : (t + 1) * rows_here, :] = hid
        slope = up * sig * (1.0 + gp * (1.0 - sig))
        dots = jnp.zeros((rows_here, 1), f32)
        ghid = jnp.zeros((rows_here, hidden), f32)
        for n in range(width // cut):
            cols = slice(n * cut, (n + 1) * cut)
            wd = wd_ref[:, cols]
            part = dot(hid, wd).astype(bf16).astype(f32)
            cf = cbuf[s, 2 * t : 2 * t + 2, :, :, :, cols]
            shape = cf.shape
            cf = cf.reshape(rows_here, cut).astype(f32)
            dots = dots + jnp.sum(part * cf, axis=-1, keepdims=True)
            po[2 * t : 2 * t + 2, :, :, :, cols] = (
                (gate * part).astype(bf16).reshape(shape)
            )
            gpart = (gate * cf).astype(bf16)
            cbuf[s, 2 * t : 2 * t + 2, :, :, :, cols] = gpart.reshape(shape)
            ghid = ghid + dot_nt(gpart, wd)
        dgp = (ghid * slope).astype(bf16)
        dup = (ghid * silu).astype(bf16)
        grads = jnp.concatenate([dgp, dup], axis=1)
        gbuf[t * rows_here : (t + 1) * rows_here, :] = grads
        for n in range(width // cut):
            cols = slice(n * cut, (n + 1) * cut)
            bk = dot_nt(grads, wgu_ref[cols, :]).astype(bf16)
            pb[2 * t : 2 * t + 2, :, :, :, cols] = bk.reshape(shape)
        high = dots.astype(bf16).astype(f32)
        low = dots - high
        lane = lax.broadcasted_iota(jnp.int32, (rows_here, EXTRA), 1)
        extra = jnp.where(lane == me, high, jnp.where(lane == me + 64, low, 0.0))
        pb[2 * t : 2 * t + 2, :, :, :, width:] = extra.astype(bf16).reshape(
            shape[:-1] + (EXTRA,)
        )

    def weight_grads(i):
        s = i % 2
        every = 2 * rows_here

        @pl.loop(0, width // 256)
        def _(n):
            cols = pl.ds(pl.multiple_of(n * 256, 256), 256)
            xt = xbuf[s, :, :, :, :, cols].reshape(every, 256)
            r = dot_tn(xt, gbuf[...])
            dwg_ref[cols, :] += r[:, :hidden]
            dwu_ref[cols, :] += r[:, hidden:]

        @pl.loop(0, width // cut)
        def _(n):
            cols = pl.ds(pl.multiple_of(n * cut, cut), cut)
            gpart = cbuf[s, :, :, :, :, cols].reshape(every, cut)
            dwd_ref[:, cols] += dot_tn(hbuf[...], gpart)

    dwg_ref[...] = jnp.zeros_like(dwg_ref)
    dwu_ref[...] = jnp.zeros_like(dwu_ref)
    dwd_ref[...] = jnp.zeros_like(dwd_ref)
    for j in range(3):
        ag_z(j)
    ag_xy(0)
    ag_xy(1)
    ag_rel(0)
    ag_rel(1)
    ag_fin(0)
    ag_done(0)
    ag_fin(1)

    @pl.loop(0, steps + 2)
    def _(i):
        def when(low, high, *work):
            @pl.when((i >= low) & (i < high))
            def _():
                for f in work:
                    f()

        @pl.when(i + 3 < steps)
        def _():
            ag_z(i + 3)

        @pl.when(i + 2 < steps)
        def _():
            ag_xy(i + 2)

        when(1, steps + 1, lambda: rs_p2(0, i - 1))
        when(2, steps + 2, lambda: rs_z(1, i - 2))

        @pl.when(i < steps)
        def _():
            for cp in loads(i):
                cp.wait()
            tile(i, 0)

        @pl.when(i + 2 < steps)
        def _():
            ag_rel(i + 2)

        when(1, steps + 1, lambda: rs_p2(1, i - 1))
        when(2, steps + 2, lambda: rs_fin(0, i - 2))

        @pl.when(i < steps)
        def _():
            tile(i, 1)
            rs_sib(0, i)
            rs_sib(1, i)

        @pl.when(i + 2 < steps)
        def _():
            ag_fin(i + 2)

        when(0, steps, lambda: rs_p1(0, i))
        when(1, steps + 1, lambda: rs_z(0, i - 1))
        when(2, steps + 2, lambda: rs_fin(1, i - 2))
        when(0, steps, lambda: rs_p1(1, i))

        @pl.when(i < steps)
        def _():
            weight_grads(i)

        @pl.when(i + 1 < steps)
        def _():
            ag_done(i + 1)

    @pl.loop(0, steps)
    def _(j):
        ag_sent(j)


def moe(expert_in, upstream_all, mask, router, gate_up, down):
    tokens, width = expert_in.shape
    hidden = down.shape[0]
    steps = tokens // 16
    wide = width + EXTRA
    half = width // 2
    any_, vm = pl.BlockSpec(memory_space=pl.ANY), pl.BlockSpec(memory_space=pltpu.VMEM)
    dma = pltpu.SemaphoreType.DMA
    router = jnp.pad(router, ((0, 0), (0, 128 - router.shape[1])))
    results = pl.pallas_call(
        functools.partial(moe_kernel, steps),
        out_shape=(
            jax.ShapeDtypeStruct((steps, 4, 4, 2, 16, width), bf16),
            jax.ShapeDtypeStruct((steps, 16, width), f32),
            jax.ShapeDtypeStruct((steps, 16, wide), f32),
            jax.ShapeDtypeStruct((width, hidden), f32),
            jax.ShapeDtypeStruct((width, hidden), f32),
            jax.ShapeDtypeStruct((hidden, width), f32),
        ),
        in_specs=[any_, any_, vm, vm, vm, vm],
        out_specs=(any_, vm, vm, vm, vm, vm),
        scratch_shapes=[
            pltpu.VMEM((2, 4, 4, 2, 16, width), bf16),
            pltpu.VMEM((2, 4, 4, 2, 16, width), bf16),
            pltpu.VMEM((512, hidden), bf16),
            pltpu.VMEM((512, 2 * hidden), bf16),
            pltpu.VMEM((4, 4, 2, 16, width), bf16),
            pltpu.VMEM((4, 4, 2, 16, wide), bf16),
            pltpu.VMEM((2, 4, 4, 16, width), bf16),
            pltpu.VMEM((2, 4, 4, 16, wide), bf16),
            pltpu.VMEM((2, 4, 4, 16, width), bf16),
            pltpu.VMEM((2, 4, 4, 16, wide), bf16),
            pltpu.VMEM((2, 4, 16, half), bf16),
            pltpu.VMEM((2, 4, 16, half), bf16),
            pltpu.VMEM((2, 4, 16, half), bf16),
            pltpu.VMEM((2, 4, 16, wide - half), bf16),
            pltpu.VMEM((2, 2, 4, 16, width), bf16),
            pltpu.VMEM((2, 2, 4, 16, wide), bf16),
            pltpu.VMEM((2, 3, 16, width), bf16),
            pltpu.VMEM((2, 3, 16, wide), bf16),
            dma((steps, 11)),
            dma((steps, 11)),
            dma((2, 2, 8)),
            dma((2, 2, 8)),
            dma((6,)),
        ],
        compiler_params=pltpu.CompilerParams(
            collective_id=1, has_side_effects=True, vmem_limit_bytes=60 * 2**20
        ),
        cost_estimate=pl.CostEstimate(
            flops=78 * 10**9, bytes_accessed=10**8, transcendentals=0
        ),
    )(
        expert_in.reshape(steps, 16, width),
        upstream_all.reshape(4, 4, 2, steps, 16, width),
        mask,
        router,
        gate_up,
        down,
    )
    return results[1:]


def rope_tables(count):
    half = HEAD_DIM // 2
    frequency = jnp.exp(
        -math.log(10000.0) * 2.0 * jnp.arange(half, dtype=f32) / HEAD_DIM
    )
    angles = jnp.arange(count, dtype=f32)[:, None] * frequency[None, :]
    return jnp.cos(angles)[:, None, :], jnp.sin(angles)[:, None, :]


def rope(values, cosine, sine):
    half = HEAD_DIM // 2
    a, b = values[..., :half], values[..., half:]
    return jnp.concatenate([a * cosine - b * sine, b * cosine + a * sine], axis=-1)


def norm_back(v, r, g, c, mean_vgc):
    return r * g * c - v * (r * r * r) * mean_vgc


def experts_by_scan(expert_in, upstream, gates, gate_local, up_local, down_local):
    tokens, width = expert_in.shape
    experts = gates.shape[1]
    rows, blocks = lax.axis_size("row"), lax.axis_size("blk")
    devices = rows * blocks
    me = lax.axis_index("row") * blocks + lax.axis_index("blk")
    parts = devices * tokens // 2048
    step = tokens // parts
    all_gates = lax.all_gather(gates, BOTH, axis=0, tiled=False)
    own_gate = jnp.sum(
        jnp.where(
            jnp.arange(experts, dtype=jnp.int32)[None, None, :] == me // 2,
            all_gates,
            0.0,
        ),
        axis=-1,
    )

    def expert_part(sums, items):
        own_rows, own_upstream, gate_col = items
        got = lax.all_gather(own_rows, BOTH, axis=0, tiled=True)
        up_stream = lax.all_gather(own_upstream, BOTH, axis=0, tiled=True)
        gate_col = gate_col.reshape(devices * step, 1)
        gate_pre = dot(got, gate_local)
        up_pre = dot(got, up_local)
        sig = jax.nn.sigmoid(gate_pre)
        silu = gate_pre * sig
        hidden = (silu * up_pre).astype(bf16)
        part_f = dot(hidden, down_local).astype(bf16).astype(f32)
        up_f = up_stream.astype(f32)
        dots = jnp.sum(part_f * up_f, axis=-1).reshape(devices, step)
        mixed = (gate_col * part_f).astype(bf16)
        out = lax.psum_scatter(mixed, BOTH, scatter_dimension=0, tiled=True)
        grad_part = (gate_col * up_f).astype(bf16)
        grad_hidden = dot_nt(grad_part, down_local)
        grad_gate_pre = (
            grad_hidden * up_pre * sig * (1.0 + gate_pre * (1.0 - sig))
        ).astype(bf16)
        grad_up_pre = (grad_hidden * silu).astype(bf16)
        grad_rows = (
            dot_nt(grad_gate_pre, gate_local) + dot_nt(grad_up_pre, up_local)
        ).astype(bf16)
        back = lax.psum_scatter(grad_rows, BOTH, scatter_dimension=0, tiled=True)
        sums = (
            sums[0] + dot_tn(got, grad_gate_pre),
            sums[1] + dot_tn(got, grad_up_pre),
            sums[2] + dot_tn(hidden, grad_part),
        )
        return sums, (out, back, dots)

    sums = (
        jnp.zeros(gate_local.shape, f32),
        jnp.zeros(up_local.shape, f32),
        jnp.zeros(down_local.shape, f32),
    )
    items = (
        expert_in.reshape(parts, step, width),
        upstream.reshape(parts, step, width),
        own_gate.reshape(devices, parts, step).transpose(1, 0, 2),
    )
    if parts > 2:
        sums, (outs, backs, dots) = lax.scan(expert_part, sums, items)
    else:
        made = []
        for part in range(parts):
            sums, result = expert_part(sums, tuple(item[part] for item in items))
            made.append(result)
        outs, backs, dots = (jnp.stack(some) for some in zip(*made))
    dots = dots.transpose(1, 0, 2).reshape(devices, tokens)
    outs = outs.reshape(tokens, width)
    backs = backs.reshape(tokens, width)
    dots = lax.all_to_all(dots, BOTH, split_axis=0, concat_axis=0, tiled=True)
    grad_gates = jnp.sum(dots.reshape(experts, 2, tokens), axis=1).T
    return outs.astype(f32), backs.astype(f32), grad_gates, sums


def experts_in_kernel(
    expert_in, upstream, routed, router, gate_local, up_local, down_local
):
    tokens, width = expert_in.shape
    experts = router.shape[1]
    steps = tokens // 16
    upstream_all = lax.all_gather(upstream, BOTH, axis=0, tiled=False)
    mask = lax.all_gather(routed.astype(bf16), BOTH, axis=0, tiled=False).astype(f32)
    mask = mask.reshape(-1, steps, 16, experts).transpose(1, 0, 2, 3)
    mask = mask.reshape(steps, -1, experts)
    gate_up = jnp.concatenate([gate_local, up_local], axis=1)
    outs, backs, *sums = moe(
        expert_in, upstream_all, mask, router, gate_up, down_local
    )
    outs = outs.reshape(tokens, width)
    backs = backs.reshape(tokens, width + EXTRA)
    dots = backs[:, width : width + 2 * experts]
    dots = dots + backs[:, width + 64 : width + 64 + 2 * experts]
    grad_gates = jnp.sum(dots.reshape(tokens, experts, 2), axis=2)
    return outs, backs[:, :width], grad_gates, sums


def body(
    hidden_in,
    segment_ids,
    expert_ids,
    attention_gain,
    query_gain,
    key_gain,
    expert_gain,
    query_weight,
    key_weight,
    value_weight,
    output_weight,
    router_weight,
    gate_weight,
    up_weight,
    down_weight,
    grad_out,
):
    tokens = hidden_in.shape[1]
    width = hidden_in.shape[2]
    experts = router_weight.shape[1]
    rows, blocks = lax.axis_size("row"), lax.axis_size("blk")
    devices = rows * blocks
    seq = tokens * blocks
    head_cols = width // blocks
    heads_here = HEADS // blocks
    blk = lax.axis_index("blk")
    me = lax.axis_index("row") * blocks + blk
    scale = HEAD_DIM**-0.5

    small = jnp.concatenate(
        [
            router_weight,
            attention_gain[:, None],
            query_gain[:, None],
            key_gain[:, None],
            expert_gain[:, None],
        ],
        axis=1,
    )
    small = lax.all_gather(small, BOTH, axis=0, tiled=True)
    router = small[:, :experts]
    gains = small[:, experts:].astype(f32)
    gain_attn, gain_expert = gains[:, 0], gains[:, 3]
    own_q_gain = lax.dynamic_slice_in_dim(gains[:, 1], blk * head_cols, head_cols)
    own_k_gain = lax.dynamic_slice_in_dim(gains[:, 2], blk * head_cols, head_cols)

    x = hidden_in[0].astype(f32)
    r_attn = lax.rsqrt(jnp.mean(x * x, axis=-1, keepdims=True) + epsilon)
    normed = (x * r_attn * gain_attn).astype(bf16)
    normed_row = lax.all_gather(normed, "blk", axis=0, tiled=True)
    segments = lax.all_gather(segment_ids[0], "blk", axis=0, tiled=True)

    stacked = jnp.stack([query_weight, key_weight, value_weight], axis=0)
    wrows = stacked.shape[1]
    stacked = stacked.reshape(3, wrows, blocks, head_cols).transpose(2, 1, 0, 3)
    stacked = stacked.reshape(blocks, wrows, 3 * head_cols)
    cols = lax.all_to_all(stacked, "blk", split_axis=0, concat_axis=0, tiled=True)
    cols = cols.reshape(blocks * wrows, 3 * head_cols)
    qkv_cols = lax.all_gather(cols, "row", axis=0, tiled=True)
    full_output = lax.all_gather(output_weight, BOTH, axis=0, tiled=True)

    qkv = dot(normed_row, qkv_cols)
    query_pre = qkv[:, :head_cols]
    key_pre = qkv[:, head_cols : 2 * head_cols]
    value = qkv[:, 2 * head_cols :].astype(bf16)
    squares = jnp.stack(
        [jnp.sum(query_pre * query_pre, axis=-1), jnp.sum(key_pre * key_pre, axis=-1)]
    )
    squares = lax.psum(squares, "blk") / width
    r_q = lax.rsqrt(squares[0] + epsilon)[:, None]
    r_k = lax.rsqrt(squares[1] + epsilon)[:, None]
    cosine, sine = rope_tables(seq)

    def heads(v):
        return v.reshape(seq, heads_here, HEAD_DIM)

    query = rope(heads(query_pre * r_q * own_q_gain), cosine, sine).astype(bf16)
    key = rope(heads(key_pre * r_k * own_k_gain), cosine, sine).astype(bf16)
    value = heads(value)
    places = jnp.arange(seq, dtype=jnp.int32)
    allowed = (places[None, :] <= places[:, None]) & (
        segments[None, :] == segments[:, None]
    )
    scores = jnp.einsum("qhd,khd->hqk", query, key, preferred_element_type=f32) * scale
    scores = jnp.where(allowed[None], scores, masked_score)
    top = jnp.max(scores, axis=-1, keepdims=True)
    weights = jnp.where(allowed[None], jnp.exp(scores - top), 0.0)
    total = jnp.sum(weights, axis=-1, keepdims=True)
    probs = weights / total
    probs_low = probs.astype(bf16)
    attended = jnp.einsum("hqk,khd->qhd", probs_low, value, preferred_element_type=f32)
    attended_low_cols = attended.astype(bf16).reshape(blocks, tokens, head_cols)
    attended_low = lax.all_to_all(
        attended_low_cols, "blk", split_axis=0, concat_axis=0, tiled=True
    )
    attended_low = attended_low.transpose(1, 0, 2).reshape(tokens, width)

    residual_mid = x + dot(attended_low, full_output)
    r_exp = lax.rsqrt(
        jnp.mean(residual_mid * residual_mid, axis=-1, keepdims=True) + epsilon
    )
    expert_in = (residual_mid * r_exp * gain_expert).astype(bf16)
    logits = dot(expert_in, router)
    routes = expert_ids[0]
    routed = jnp.any(
        routes[:, :, None] == jnp.arange(experts, dtype=jnp.int32)[None, None, :],
        axis=1,
    )
    top_logit = jnp.max(
        jnp.where(routed, logits, masked_score), axis=-1, keepdims=True
    )
    gates = jnp.where(routed, jnp.exp(logits - top_logit), 0.0)
    gates = gates / jnp.sum(gates, axis=-1, keepdims=True)

    gate_local, up_local, down_local = gate_weight[0], up_weight[0], down_weight[0]
    if (rows, blocks, 2 * experts, heads_here) == (4, 8, 32, 2):
        outs, backs, grad_gates, sums = experts_in_kernel(
            expert_in, grad_out[0], routed, router, gate_local, up_local, down_local
        )
    else:
        outs, backs, grad_gates, sums = experts_by_scan(
            expert_in, grad_out[0], gates, gate_local, up_local, down_local
        )
    grad_gate_local, grad_up_local, grad_down_local = sums
    layer_out = (residual_mid + outs).astype(bf16)
    upstream = grad_out[0].astype(f32)
    grad_picked = gates * (
        grad_gates - jnp.sum(gates * grad_gates, axis=-1, keepdims=True)
    )
    grad_logits = jnp.where(routed, grad_picked, 0.0).astype(bf16)
    grad_expert_in = backs + dot_nt(
        grad_logits, router
    )
    grad_router = dot_tn(expert_in, grad_logits)
    grad_gain_expert = jnp.sum(grad_expert_in * residual_mid * r_exp, axis=0)
    grad_mid = upstream + norm_back(
        residual_mid,
        r_exp,
        gain_expert,
        grad_expert_in,
        jnp.mean(residual_mid * gain_expert * grad_expert_in, axis=-1, keepdims=True),
    )
    grad_proj = grad_mid.astype(bf16)
    grad_output_w = dot_tn(attended_low, grad_proj).astype(bf16)
    grad_output_w = lax.psum_scatter(
        grad_output_w, BOTH, scatter_dimension=0, tiled=True
    ).astype(f32)
    grad_attended = dot_nt(grad_proj, full_output).astype(bf16)
    grad_attended = grad_attended.reshape(tokens, blocks, head_cols).transpose(1, 0, 2)
    grad_attended = lax.all_to_all(
        grad_attended, "blk", split_axis=0, concat_axis=0, tiled=True
    )
    grad_attended = grad_attended.reshape(seq, heads_here, HEAD_DIM)
    row_delta = jnp.sum(grad_attended.astype(f32) * attended, axis=-1).T
    grad_probs = jnp.einsum(
        "qhd,khd->hqk", grad_attended, value, preferred_element_type=f32
    )
    grad_scores = (probs * (grad_probs - row_delta[:, :, None])).astype(bf16)
    grad_value = jnp.einsum(
        "hqk,qhd->khd", probs_low, grad_attended, preferred_element_type=f32
    ).astype(bf16)
    grad_query = (
        jnp.einsum("hqk,khd->qhd", grad_scores, key, preferred_element_type=f32) * scale
    )
    grad_key = (
        jnp.einsum("hqk,qhd->khd", grad_scores, query, preferred_element_type=f32)
        * scale
    )
    grad_query = rope(grad_query, cosine, -sine).reshape(seq, head_cols)
    grad_key = rope(grad_key, cosine, -sine).reshape(seq, head_cols)
    means = jnp.stack(
        [
            jnp.sum(query_pre * own_q_gain * grad_query, axis=-1),
            jnp.sum(key_pre * own_k_gain * grad_key, axis=-1),
        ]
    )
    means = lax.psum(means, "blk") / width
    grad_q_gain = jnp.sum(grad_query * query_pre * r_q, axis=0)
    grad_k_gain = jnp.sum(grad_key * key_pre * r_k, axis=0)
    grad_query_pre = norm_back(query_pre, r_q, own_q_gain, grad_query, means[0][:, None])
    grad_key_pre = norm_back(key_pre, r_k, own_k_gain, grad_key, means[1][:, None])
    grad_qkv = jnp.concatenate(
        [
            grad_query_pre.astype(bf16),
            grad_key_pre.astype(bf16),
            grad_value.reshape(seq, head_cols),
        ],
        axis=1,
    )
    grad_w = dot_tn(normed_row, grad_qkv).astype(bf16)
    grad_w = lax.psum_scatter(grad_w, "row", scatter_dimension=0, tiled=True)
    grad_w = grad_w.reshape(blocks, wrows, 3 * head_cols)
    grad_w = lax.all_to_all(grad_w, "blk", split_axis=0, concat_axis=0, tiled=True)
    grad_w = grad_w.reshape(blocks, wrows, 3, head_cols).transpose(2, 1, 0, 3)
    grad_w = grad_w.reshape(3, wrows, width).astype(f32)
    grad_normed = dot_nt(grad_qkv, qkv_cols).astype(bf16)
    grad_normed = lax.psum_scatter(
        grad_normed, "blk", scatter_dimension=0, tiled=True
    ).astype(f32)
    grad_gain_attn = jnp.sum(grad_normed * x * r_attn, axis=0)
    input_grad = grad_mid + norm_back(
        x,
        r_attn,
        gain_attn,
        grad_normed,
        jnp.mean(x * gain_attn * grad_normed, axis=-1, keepdims=True),
    )

    def placed(vector):
        return lax.dynamic_update_slice_in_dim(
            jnp.zeros((width,), f32), vector, blk * head_cols, axis=0
        )

    small_grads = jnp.concatenate(
        [
            grad_router,
            grad_gain_attn[:, None],
            placed(grad_q_gain)[:, None],
            placed(grad_k_gain)[:, None],
            grad_gain_expert[:, None],
        ],
        axis=1,
    )
    small_grads = lax.psum_scatter(small_grads, BOTH, scatter_dimension=0, tiled=True)
    return (
        layer_out[None],
        input_grad[None],
        small_grads[:, experts],
        small_grads[:, experts + 1],
        small_grads[:, experts + 2],
        small_grads[:, experts + 3],
        grad_w[0],
        grad_w[1],
        grad_w[2],
        grad_output_w,
        small_grads[:, :experts],
        grad_gate_local[None],
        grad_up_local[None],
        grad_down_local[None],
    )


def solution(mesh):
    tokens3 = P("row", "blk", None)
    vector, matrix, cube = P(BOTH), P(BOTH, None), P(BOTH, None, None)
    return jax.shard_map(
        body,
        mesh=mesh,
        in_specs=(
            tokens3,
            P("row", "blk"),
            tokens3,
            vector,
            vector,
            vector,
            vector,
            matrix,
            matrix,
            matrix,
            matrix,
            matrix,
            cube,
            cube,
            cube,
            tokens3,
        ),
        out_specs=(
            tokens3,
            tokens3,
            vector,
            vector,
            vector,
            vector,
            matrix,
            matrix,
            matrix,
            matrix,
            matrix,
            cube,
            cube,
            cube,
        ),
        check_vma=False,
    )
```

```python
import functools
import math

import jax
import jax.numpy as jnp
import numpy as np
from jax import lax
from jax.experimental import pallas as pl
from jax.experimental.pallas import tpu as pltpu
from jax.sharding import PartitionSpec as P

HEADS = 16
HEAD_DIM = 128
TOP_K = 8

epsilon = 1e-05
masked_score = -1e30
BOTH = ("row", "blk")
MESH = pl.DeviceIdType.MESH
bf16 = jnp.bfloat16
f32 = jnp.float32
EXTRA = 128


def dot(a, b):
    return jnp.dot(a, b, preferred_element_type=f32)


def dot_nt(a, b):
    return lax.dot_general(a, b, (((1,), (1,)), ((), ())), preferred_element_type=f32)


def dot_tn(a, b):
    return lax.dot_general(a, b, (((0,), (0,)), ((), ())), preferred_element_type=f32)


def place():
    row, blk = lax.axis_index("row"), lax.axis_index("blk")
    return row, blk // 2, blk % 2


def partners():
    row, z, c = place()
    blk = z * 2 + c
    return {
        "sib": (row, z * 2 + (1 - c)),
        "x": (row ^ 1, blk),
        "y": (row ^ 2, blk),
        "z1": (row, ((z + 1) % 4) * 2 + c),
        "z2": (row, ((z + 2) % 4) * 2 + c),
        "z3": (row, ((z + 3) % 4) * 2 + c),
    }


def remote(src, dst, send, recv, to):
    return pltpu.make_async_remote_copy(
        src_ref=src,
        dst_ref=dst,
        send_sem=send,
        recv_sem=recv,
        device_id=to,
        device_id_type=MESH,
    )


def greet(targets):
    barrier = pltpu.get_barrier_semaphore()
    for to in targets:
        pl.semaphore_signal(barrier, inc=1, device_id=to, device_id_type=MESH)
    pl.semaphore_wait(barrier, len(targets))


def moe_kernel(
    steps,
    x_ref,
    c_ref,
    mask_ref,
    router_ref,
    gate_ref,
    up_ref,
    down_ref,
    xall,
    out_ref,
    back_ref,
    dwg_out,
    dwu_out,
    dwd_out,
    wgu_ref,
    wd_ref,
    dwg_ref,
    dwu_ref,
    dwd_ref,
    xbuf,
    cbuf,
    hbuf,
    gbuf,
    po,
    pb,
    ro,
    rb,
    so,
    sb,
    p1ao,
    p1bo,
    p1ab,
    p1bb,
    p2o,
    p2b,
    zo,
    zb,
    ag_send,
    ag_recv,
    rs_send,
    rs_recv,
    load_sem,
    weight_sem,
):
    row, z, c = place()
    to = partners()
    width = x_ref.shape[-1]
    half = width // 2
    hidden = wd_ref.shape[0]
    me = row * 8 + z * 2 + c
    expert = me // 2

    weights = [
        pltpu.make_async_copy(src, dst, weight_sem.at[k])
        for k, (src, dst) in enumerate(
            (
                (gate_ref, wgu_ref.at[:, pl.ds(0, hidden)]),
                (up_ref, wgu_ref.at[:, pl.ds(hidden, hidden)]),
                (down_ref, wd_ref),
            )
        )
    ]
    sums = [
        pltpu.make_async_copy(src, dst, weight_sem.at[3 + k])
        for k, (src, dst) in enumerate(
            ((dwg_ref, dwg_out), (dwu_ref, dwu_out), (dwd_ref, dwd_out))
        )
    ]
    for cp in weights:
        cp.start()
    greet(list(to.values()))

    def ag(j, k, src, dst, who):
        return remote(src, dst, ag_send.at[j, k], ag_recv.at[j, k], to[who])

    def own_copy(j):
        return pltpu.make_async_copy(
            x_ref.at[j], xall.at[j, row, z, c], load_sem.at[2 + j % 4]
        )

    def z_copies(j):
        slot = xall.at[j, row, z, c]
        return [ag(j, k, x_ref.at[j], slot, "z%d" % (k + 1)) for k in range(3)]

    def line_copies(j):
        line = xall.at[j, row, :, c]
        return [
            ag(j, 3, line, line, "x"),
            ag(j, 4, line, line, "y"),
            ag(j, 5, line, line, "sib"),
        ]

    def relay_copies(j):
        a = xall.at[j, row ^ 1, :, c, :, pl.ds(0, half)]
        b = xall.at[j, row ^ 2, :, c, :, pl.ds(half, half)]
        s1 = xall.at[j, row ^ 1, :, c]
        s2 = xall.at[j, row ^ 2, :, c]
        return [
            ag(j, 6, a, a, "y"),
            ag(j, 7, b, b, "x"),
            ag(j, 8, s1, s1, "sib"),
            ag(j, 9, s2, s2, "sib"),
        ]

    def last_copies(j):
        s3 = xall.at[j, row ^ 3, :, c]
        return [ag(j, 10, s3, s3, "sib")]

    def ag_z(j):
        own_copy(j).start()
        for cp in z_copies(j):
            cp.start()

    def ag_xy(j):
        own_copy(j).wait()
        for cp in z_copies(j):
            cp.wait_recv()
        for cp in line_copies(j):
            cp.start()

    def ag_rel(j):
        for cp in line_copies(j)[:2]:
            cp.wait_recv()
        for cp in relay_copies(j):
            cp.start()

    def ag_fin(j):
        for cp in relay_copies(j)[:2]:
            cp.wait_recv()
        for cp in last_copies(j):
            cp.start()

    def loads(j):
        return [
            pltpu.make_async_copy(xall.at[j], xbuf.at[j % 2], load_sem.at[0]),
            pltpu.make_async_copy(c_ref.at[j], cbuf.at[j % 2], load_sem.at[1]),
        ]

    def ag_done(j):
        line_copies(j)[2].wait_recv()
        for cp in relay_copies(j)[2:] + last_copies(j):
            cp.wait_recv()
        for cp in loads(j):
            cp.start()

    def ag_sent(j):
        for cp in z_copies(j) + line_copies(j) + relay_copies(j) + last_copies(j):
            cp.wait_send()

    arrays = (
        (po, ro, so, p1ao, p1bo, p2o, zo, out_ref),
        (pb, rb, sb, p1ab, p1bb, p2b, zb, back_ref),
    )

    def rs(i, q, k, src, dst, who):
        s = i % 2
        return remote(src, dst, rs_send.at[q, s, k], rs_recv.at[q, s, k], to[who])

    def rs_sib_copy(q, i):
        p, r = arrays[q][:2]
        return rs(i, q, 0, p.at[:, :, 1 - c], r.at[i % 2], "sib")

    def p1_copies(q, i):
        p, r, s, p1a, p1b, p2, zz, out = arrays[q]
        part = s.at[i % 2, row ^ 3]
        rest = p.shape[-1] - half
        return [
            rs(i, q, 1, part.at[:, :, pl.ds(0, half)], p1a.at[i % 2], "y"),
            rs(i, q, 2, part.at[:, :, pl.ds(half, rest)], p1b.at[i % 2], "x"),
        ]

    def p2_copies(q, i):
        p, r, s, p1a, p1b, p2, zz, out = arrays[q]
        return [
            rs(i, q, 3, s.at[i % 2, row ^ 1], p2.at[i % 2, 0], "x"),
            rs(i, q, 4, s.at[i % 2, row ^ 2], p2.at[i % 2, 1], "y"),
        ]

    def rsz_copies(q, i):
        p, r, s, p1a, p1b, p2, zz, out = arrays[q]
        return [
            rs(
                i,
                q,
                5 + k,
                s.at[i % 2, row, (z + k + 1) % 4],
                zz.at[i % 2, k],
                "z%d" % (k + 1),
            )
            for k in range(3)
        ]

    def rs_sib(q, i):
        rs_sib_copy(q, i).start()

    def rs_p1(q, i):
        p, r, s, p1a, p1b, p2, zz, out = arrays[q]
        cp = rs_sib_copy(q, i)
        cp.wait_recv()

        @pl.loop(0, 4)
        def _(a):
            s[i % 2, a] = (
                p[a, :, c].astype(f32) + r[i % 2, a].astype(f32)
            ).astype(bf16)

        cp.wait_send()
        for cp in p1_copies(q, i):
            cp.start()

    def rs_p2(q, i):
        p, r, s, p1a, p1b, p2, zz, out = arrays[q]
        rest = p.shape[-1] - half
        copies = p1_copies(q, i)
        copies[0].wait_recv()
        at = s.at[i % 2, row ^ 1]
        at[:, :, pl.ds(0, half)] = (
            at[:, :, pl.ds(0, half)].astype(f32) + p1a[i % 2].astype(f32)
        ).astype(bf16)
        out_copies = p2_copies(q, i)
        out_copies[0].start()
        copies[1].wait_recv()
        at = s.at[i % 2, row ^ 2]
        at[:, :, pl.ds(half, rest)] = (
            at[:, :, pl.ds(half, rest)].astype(f32) + p1b[i % 2].astype(f32)
        ).astype(bf16)
        out_copies[1].start()

    def rs_z(q, i):
        p, r, s, p1a, p1b, p2, zz, out = arrays[q]
        for cp in p2_copies(q, i):
            cp.wait_recv()
        s[i % 2, row] = (
            s[i % 2, row].astype(f32)
            + p2[i % 2, 0].astype(f32)
            + p2[i % 2, 1].astype(f32)
        ).astype(bf16)
        for cp in rsz_copies(q, i):
            cp.start()

    def rs_fin(q, i):
        p, r, s, p1a, p1b, p2, zz, out = arrays[q]
        copies = rsz_copies(q, i)
        for cp in copies:
            cp.wait_recv()
        total = s[i % 2, row, z].astype(f32)
        for k in range(3):
            total = total + zz[i % 2, k].astype(f32)
        out[i] = total
        for cp in copies + p2_copies(q, i) + p1_copies(q, i):
            cp.wait_send()

    lanes = po.shape[3]
    rows_here = 16 * lanes
    cut = 512

    def tile(i, t):
        s = i % 2
        xt = xbuf[s, 2 * t : 2 * t + 2].reshape(rows_here, width)
        mask = mask_ref[i, t * rows_here : (t + 1) * rows_here, :]
        logits = dot(xt, router_ref[...])[:, : mask.shape[-1]]
        logits = jnp.where(mask > 0, logits, masked_score)
        top = jnp.max(logits, axis=-1, keepdims=True)
        raised = jnp.where(mask > 0, jnp.exp(logits - top), 0.0)
        lane = lax.broadcasted_iota(jnp.int32, raised.shape, 1)
        gate = jnp.sum(
            jnp.where(lane == expert, raised, 0.0), axis=-1, keepdims=True
        ) / jnp.sum(raised, axis=-1, keepdims=True)
        both = dot(xt, wgu_ref[...])
        gp, up = both[:, :hidden], both[:, hidden:]
        sig = jax.nn.sigmoid(gp)
        silu = gp * sig
        hid = (silu * up).astype(bf16)
        hbuf[t * rows_here : (t + 1) * rows_here, :] = hid
        slope = up * sig * (1.0 + gp * (1.0 - sig))
        dots = jnp.zeros((rows_here, 1), f32)
        ghid = jnp.zeros((rows_here, hidden), f32)
        for n in range(width // cut):
            cols = slice(n * cut, (n + 1) * cut)
            wd = wd_ref[:, cols]
            part = dot(hid, wd).astype(bf16).astype(f32)
            cf = cbuf[s, 2 * t : 2 * t + 2, :, :, :, cols]
            shape = cf.shape
            cf = cf.reshape(rows_here, cut).astype(f32)
            dots = dots + jnp.sum(part * cf, axis=-1, keepdims=True)
            po[2 * t : 2 * t + 2, :, :, :, cols] = (
                (gate * part).astype(bf16).reshape(shape)
            )
            gpart = (gate * cf).astype(bf16)
            cbuf[s, 2 * t : 2 * t + 2, :, :, :, cols] = gpart.reshape(shape)
            ghid = ghid + dot_nt(gpart, wd)
        dgp = (ghid * slope).astype(bf16)
        dup = (ghid * silu).astype(bf16)
        grads = jnp.concatenate([dgp, dup], axis=1)
        gbuf[t * rows_here : (t + 1) * rows_here, :] = grads
        for n in range(width // cut):
            cols = slice(n * cut, (n + 1) * cut)
            bk = dot_nt(grads, wgu_ref[cols, :]).astype(bf16)
            pb[2 * t : 2 * t + 2, :, :, :, cols] = bk.reshape(shape)
        high = dots.astype(bf16).astype(f32)
        low = dots - high
        lane = lax.broadcasted_iota(jnp.int32, (rows_here, EXTRA), 1)
        extra = jnp.where(lane == me, high, jnp.where(lane == me + 64, low, 0.0))
        pb[2 * t : 2 * t + 2, :, :, :, width:] = extra.astype(bf16).reshape(
            shape[:-1] + (EXTRA,)
        )

    def weight_grads(i):
        s = i % 2
        every = 2 * rows_here

        @pl.loop(0, width // 256)
        def _(n):
            cols = pl.ds(pl.multiple_of(n * 256, 256), 256)
            xt = xbuf[s, :, :, :, :, cols].reshape(every, 256)
            r = dot_tn(xt, gbuf[...])
            dwg_ref[cols, :] += r[:, :hidden]
            dwu_ref[cols, :] += r[:, hidden:]

        @pl.loop(0, width // cut)
        def _(n):
            cols = pl.ds(pl.multiple_of(n * cut, cut), cut)
            gpart = cbuf[s, :, :, :, :, cols].reshape(every, cut)
            dwd_ref[:, cols] += dot_tn(hbuf[...], gpart)

    for j in range(3):
        ag_z(j)
    ag_xy(0)
    ag_xy(1)
    dwg_ref[...] = jnp.zeros_like(dwg_ref)
    dwu_ref[...] = jnp.zeros_like(dwu_ref)
    dwd_ref[...] = jnp.zeros_like(dwd_ref)
    for cp in weights:
        cp.wait()
    ag_rel(0)
    ag_rel(1)
    ag_fin(0)
    ag_done(0)
    ag_fin(1)

    @pl.loop(0, steps + 2)
    def _(i):
        def when(low, high, *work):
            @pl.when((i >= low) & (i < high))
            def _():
                for f in work:
                    f()

        @pl.when(i + 3 < steps)
        def _():
            ag_z(i + 3)

        @pl.when(i + 2 < steps)
        def _():
            ag_xy(i + 2)

        when(1, steps + 1, lambda: rs_p2(0, i - 1))
        when(2, steps + 2, lambda: rs_z(1, i - 2))

        @pl.when(i < steps)
        def _():
            for cp in loads(i):
                cp.wait()
            tile(i, 0)

        @pl.when(i + 2 < steps)
        def _():
            ag_rel(i + 2)

        when(1, steps + 1, lambda: rs_p2(1, i - 1))
        when(2, steps + 2, lambda: rs_fin(0, i - 2))

        @pl.when(i < steps)
        def _():
            tile(i, 1)
            rs_sib(0, i)
            rs_sib(1, i)

        @pl.when(i + 2 < steps)
        def _():
            ag_fin(i + 2)

        when(0, steps, lambda: rs_p1(0, i))
        when(1, steps + 1, lambda: rs_z(0, i - 1))
        when(2, steps + 2, lambda: rs_fin(1, i - 2))
        when(0, steps, lambda: rs_p1(1, i))

        @pl.when(i < steps)
        def _():
            weight_grads(i)

        @pl.when(i == steps - 1)
        def _():
            for cp in sums:
                cp.start()

        @pl.when(i + 1 < steps)
        def _():
            ag_done(i + 1)

    @pl.loop(0, steps)
    def _(j):
        ag_sent(j)

    for cp in sums:
        cp.wait()


def moe(expert_in, upstream_all, mask, router, gate, up, down):
    tokens, width = expert_in.shape
    hidden = down.shape[0]
    steps = tokens // 16
    wide = width + EXTRA
    half = width // 2
    any_, vm = pl.BlockSpec(memory_space=pl.ANY), pl.BlockSpec(memory_space=pltpu.VMEM)
    dma = pltpu.SemaphoreType.DMA
    router = jnp.pad(router, ((0, 0), (0, 128 - router.shape[1])))
    results = pl.pallas_call(
        functools.partial(moe_kernel, steps),
        out_shape=(
            jax.ShapeDtypeStruct((steps, 4, 4, 2, 16, width), bf16),
            jax.ShapeDtypeStruct((steps, 16, width), f32),
            jax.ShapeDtypeStruct((steps, 16, wide), f32),
            jax.ShapeDtypeStruct((width, hidden), f32),
            jax.ShapeDtypeStruct((width, hidden), f32),
            jax.ShapeDtypeStruct((hidden, width), f32),
        ),
        in_specs=[any_, any_, vm, vm, any_, any_, any_],
        out_specs=(any_, vm, vm, any_, any_, any_),
        scratch_shapes=[
            pltpu.VMEM((width, 2 * hidden), bf16),
            pltpu.VMEM((hidden, width), bf16),
            pltpu.VMEM((width, hidden), f32),
            pltpu.VMEM((width, hidden), f32),
            pltpu.VMEM((hidden, width), f32),
            pltpu.VMEM((2, 4, 4, 2, 16, width), bf16),
            pltpu.VMEM((2, 4, 4, 2, 16, width), bf16),
            pltpu.VMEM((512, hidden), bf16),
            pltpu.VMEM((512, 2 * hidden), bf16),
            pltpu.VMEM((4, 4, 2, 16, width), bf16),
            pltpu.VMEM((4, 4, 2, 16, wide), bf16),
            pltpu.VMEM((2, 4, 4, 16, width), bf16),
            pltpu.VMEM((2, 4, 4, 16, wide), bf16),
            pltpu.VMEM((2, 4, 4, 16, width), bf16),
            pltpu.VMEM((2, 4, 4, 16, wide), bf16),
            pltpu.VMEM((2, 4, 16, half), bf16),
            pltpu.VMEM((2, 4, 16, half), bf16),
            pltpu.VMEM((2, 4, 16, half), bf16),
            pltpu.VMEM((2, 4, 16, wide - half), bf16),
            pltpu.VMEM((2, 2, 4, 16, width), bf16),
            pltpu.VMEM((2, 2, 4, 16, wide), bf16),
            pltpu.VMEM((2, 3, 16, width), bf16),
            pltpu.VMEM((2, 3, 16, wide), bf16),
            dma((steps, 11)),
            dma((steps, 11)),
            dma((2, 2, 8)),
            dma((2, 2, 8)),
            dma((6,)),
            dma((6,)),
        ],
        compiler_params=pltpu.CompilerParams(
            collective_id=1, has_side_effects=True, vmem_limit_bytes=60 * 2**20
        ),
        cost_estimate=pl.CostEstimate(
            flops=78 * 10**9, bytes_accessed=10**8, transcendentals=0
        ),
    )(
        expert_in.reshape(steps, 16, width),
        upstream_all,
        mask,
        router,
        gate,
        up,
        down,
    )
    return results[1:]


class Copies:
    def __init__(self, send, recv):
        self.send, self.recv, self.count, self.made = send, recv, 0, []

    def __call__(self, src, dst, who):
        k = self.count
        self.count += 1
        return remote(src, dst, self.send.at[k], self.recv.at[k], who)


def row_mates():
    row, z, c = place()
    mates = [(row, z * 2 + (1 - c))]
    for k in (1, 3, 2):
        for flip in (0, 1):
            mates.append((row, ((z + k) % 4) * 2 + (c ^ flip)))
    return mates


def gather_stages(copy, src, slots, cut, own_sem):
    row, z, c = place()
    to = partners()
    own = slots.at[row, z, c]
    line = slots.at[row, :, c]
    width = src.shape[-1]
    if cut:
        a = slots.at[row ^ 1, :, c, :, pl.ds(0, cut)]
        b = slots.at[row ^ 2, :, c, :, pl.ds(cut, width - cut)]
    else:
        a = slots.at[row ^ 1, pl.ds(0, 2), c]
        b = slots.at[row ^ 2, pl.ds(2, 2), c]
    s1, s2, s3 = (slots.at[row ^ k, :, c] for k in (1, 2, 3))
    local = pltpu.make_async_copy(src, own, own_sem)
    along_z = [copy(src, own, to["z%d" % k]) for k in (1, 3, 2)]
    over = [copy(line, line, to[k]) for k in ("x", "y", "sib")]
    relay = [copy(a, a, to["y"]), copy(b, b, to["x"])]
    inside = [copy(s1, s1, to["sib"]), copy(s2, s2, to["sib"])]
    last = [copy(s3, s3, to["sib"])]

    def start(some):
        for cp in some:
            cp.start()

    def arrived(some):
        for cp in some:
            cp.wait_recv()

    def first():
        local.start()
        start(along_z)

    def second():
        local.wait()
        arrived(along_z)
        start(over)

    def third():
        arrived(over[:2])
        start(relay + inside)

    def fourth():
        arrived(relay)
        start(last)

    def fifth():
        arrived(over[2:] + inside + last)
        for cp in along_z + over + relay + inside + last:
            cp.wait_send()

    return first, second, third, fourth, fifth


def norm_rows(v):
    return lax.rsqrt(jnp.mean(v * v, axis=-1, keepdims=True) + epsilon)


def turned(v, cosine, sine):
    heads = []
    for h in range(v.shape[1] // HEAD_DIM):
        one = v[:, h * HEAD_DIM : (h + 1) * HEAD_DIM]
        heads.append(one * cosine + pltpu.roll(one, HEAD_DIM // 2, 1) * sine)
    return jnp.concatenate(heads, axis=1)


def row_pairs(cols):
    row = lax.broadcasted_iota(jnp.int32, (8, 2 * cols), 0)
    lane = lax.broadcasted_iota(jnp.int32, (8, 2 * cols), 1)
    return jnp.where((lane // cols) == row, 1.0, 0.0).astype(f32)


def sums_by_row(pairs, v):
    return lax.dot_general(
        pairs,
        v,
        (((1,), (1,)), ((), ())),
        precision=lax.Precision.HIGHEST,
        preferred_element_type=f32,
    )


def slot_stages(copy, src, slot, k, cut, own_sem):
    row, z, c = place()
    to = partners()
    there = (z + k) % 4
    own = slot(row, z)
    s0, s1, s2, s3 = (slot(row ^ r, there) for r in range(4))
    width = src.shape[-1]
    a = slot(row ^ 1, there).at[:, :, pl.ds(0, cut)]
    b = slot(row ^ 2, there).at[:, :, pl.ds(cut, width - cut)]
    if k:
        along_z = [copy(src, own, to["z%d" % (4 - k)])]
        over = [copy(s0, s0, to[w]) for w in ("x", "y", "sib")]
    else:
        along_z = []
        local = pltpu.make_async_copy(src, own, own_sem)
        over = [copy(src, own, to[w]) for w in ("x", "y", "sib")]
    relay = [copy(a, a, to["y"]), copy(b, b, to["x"])]
    inside = [copy(s1, s1, to["sib"]), copy(s2, s2, to["sib"])]
    last = [copy(s3, s3, to["sib"])]

    def start(some):
        for cp in some:
            cp.start()

    def arrived(some):
        for cp in some:
            cp.wait_recv()

    def first():
        if k:
            start(along_z)
        else:
            local.start()

    def second():
        arrived(along_z)
        start(over)

    def third():
        arrived(over[:2])
        start(relay + inside)

    def fourth():
        arrived(relay)
        start(last)

    def fifth():
        if not k:
            local.wait()
        arrived(over[2:] + inside + last)
        for cp in along_z + over + relay + inside + last:
            cp.wait_send()

    return first, second, third, fourth, fifth


def front_kernel(
    h_ref,
    wq_ref,
    wk_ref,
    wv_ref,
    wo_ref,
    up_ref,
    pack_ref,
    cos_ref,
    sin_ref,
    woall,
    call,
    packs,
    normed_out,
    wcols_out,
    low_out,
    pre_out,
    att_out,
    stat_ref,
    home_ref,
    mid_ref,
    expert_ref,
    hrow,
    normed_ref,
    wcols,
    low_ref,
    pre_ref,
    att_ref,
    wo_buf,
    gains_ref,
    sums_ref,
    sums_land,
    att_low,
    send,
    recv,
    local_sem,
):
    row, z, c = place()
    blk = z * 2 + c
    to = partners()
    mates = row_mates()
    greet(mates + [to["x"], to["y"]])
    copy = Copies(send, recv)
    cols_here = wcols.shape[3] // 3
    tokens, width = h_ref.shape
    seq = 8 * tokens
    wrows = wq_ref.shape[0]

    pack_stages = gather_stages(copy, pack_ref, packs, 0, local_sem.at[0])
    parts = up_ref.shape[0] // 4
    streams = []
    for k in (0, 1, 3, 2):
        streams.append(
            slot_stages(
                copy,
                wo_ref,
                lambda r, q: woall.at[r, q, c],
                k,
                width // 2,
                local_sem.at[9 + len(streams)],
            )
        )
        for j in range(parts):
            part = pl.ds(j * 4, 4)
            streams.append(
                slot_stages(
                    copy,
                    up_ref.at[part],
                    lambda r, q, part=part: call.at[part, r, q, c],
                    k,
                    width // 2,
                    local_sem.at[9 + len(streams)],
                )
            )
    for_output = streams[:: parts + 1]
    for_upstream = [one for one in streams if one not in for_output]
    saves = [
        pltpu.make_async_copy(src, dst, local_sem.at[9 + len(streams) + k])
        for k, (src, dst) in enumerate(
            (
                (wcols, wcols_out),
                (normed_ref, normed_out),
                (pre_ref, pre_out),
                (low_ref, low_out),
                (att_ref, att_out),
            )
        )
    ]
    wo_load = pltpu.make_async_copy(woall, wo_buf, local_sem.at[9 + len(streams) + 5])
    ticks = [0]

    def tick():
        t = ticks[0]
        ticks[0] += 1
        for stage, lag in ((0, 0), (1, 1), (2, 2), (3, 3)):
            if 0 <= t - lag < len(streams):
                streams[t - lag][stage]()

    own_rows = pltpu.make_async_copy(h_ref, hrow.at[blk], local_sem.at[5])
    up_to, down_to = (row, blk + 2), (row, blk - 2)
    sib = to["sib"]
    own_sib = copy(h_ref, hrow.at[blk], sib)
    ups, downs = [], []
    for t in range(3):
        src = h_ref if t == 0 else hrow.at[blk - 2 * t]
        up = copy(src, hrow.at[blk - 2 * t], up_to)
        got = hrow.at[blk - 2 - 2 * t]
        ups.append((up, copy(got, got, sib), (z < 3) & (z >= t), z >= t + 1))
        src = h_ref if t == 0 else hrow.at[blk + 2 * t]
        down = copy(src, hrow.at[blk + 2 * t], down_to)
        got = hrow.at[blk + 2 + 2 * t]
        downs.append((down, copy(got, got, sib), (z > 0) & (z + t <= 3), z + t + 1 <= 3))

    def line_start(t):
        for cp, hand, sends, gets in (ups[t], downs[t]):
            pl.when(sends)(cp.start)

    def line_arrived(t):
        for cp, hand, sends, gets in (ups[t], downs[t]):

            @pl.when(gets)
            def _():
                cp.wait_recv()
                hand.start()

    def line_done():
        own_rows.wait()
        own_sib.wait()
        for t in range(3):
            for cp, hand, sends, gets in (ups[t], downs[t]):
                pl.when(sends)(cp.wait_send)
                pl.when(gets)(hand.wait)

    def columns(b):
        return pl.ds(pl.multiple_of(b * cols_here, cols_here), cols_here)

    own_cols, col_copies = [], []
    for j, w in enumerate((wq_ref, wk_ref, wv_ref)):
        there = pl.ds(j * cols_here, cols_here)
        own_cols.append(
            pltpu.make_async_copy(
                w.at[:, columns(blk)], wcols.at[row, blk, :, there], local_sem.at[6 + j]
            )
        )
        for mate in mates:
            col_copies.append(
                copy(w.at[:, columns(mate[1])], wcols.at[row, blk, :, there], mate)
            )
    half = wcols.shape[1] // 2
    col_over = [copy(wcols.at[row], wcols.at[row], to[k]) for k in ("x", "y")]
    a = wcols.at[row ^ 1, pl.ds(0, half)]
    b = wcols.at[row ^ 2, pl.ds(half, half)]
    col_relay = [copy(a, a, to["y"]), copy(b, b, to["x"])]
    sum_copies = [
        copy(sums_ref, sums_land.at[k], mate) for k, mate in enumerate(mates)
    ]
    home_copies = [
        copy(att_low.at[mate[1]], home_ref.at[:, columns(blk)], mate) for mate in mates
    ]

    def start(some):
        for cp in some:
            cp.start()

    def arrived(some):
        for cp in some:
            cp.wait_recv()

    own_rows.start()
    start(own_cols)
    line_start(0)
    own_sib.start()
    tick()
    tick()
    pack_stages[0]()
    start(col_copies)
    tick()
    pack_stages[1]()
    tick()
    line_arrived(0)
    line_start(1)
    tick()
    pack_stages[2]()
    for cp in own_cols:
        cp.wait()
    arrived(col_copies)
    start(col_over)
    pack_stages[3]()
    line_arrived(1)
    line_start(2)
    tick()
    arrived(col_over)
    start(col_relay)
    tick()
    line_arrived(2)
    pack_stages[4]()
    arrived(col_relay)
    line_done()
    tick()
    start(saves[:1])

    pieces = []
    for r in range(4):
        for q in range(4):
            pieces.append(
                packs[r, q, 0, 48:64, :].astype(f32) + packs[r, q, 1, 48:64, :].astype(f32)
            )
    gains_ref[...] = jnp.concatenate(pieces, axis=1)[0:8]
    gain_attn = gains_ref[0:1, :]
    segments = jnp.concatenate(
        [
            packs[row, q, k, 16:32, :].astype(f32)[0:1]
            for q in range(4)
            for k in range(2)
        ],
        axis=1,
    )
    pairs = row_pairs(cols_here)
    block = 256
    blocks = seq // block

    for t in range(blocks):
        rows = slice(t * block, (t + 1) * block)
        per = block // tokens
        v = hrow[t * per : (t + 1) * per].reshape(block, width).astype(f32)
        normed = (v * norm_rows(v) * gain_attn).astype(bf16)
        normed_ref[rows, :] = normed
        pre = dot(normed, wcols[...].reshape(width, 3 * cols_here))
        pre_ref[rows, :] = pre[:, : 2 * cols_here]
        low_ref[rows, 2 * cols_here :] = pre[:, 2 * cols_here :].astype(bf16)
        both = pre[:, : 2 * cols_here]
        squares = sums_by_row(pairs, both * both)
        sums_ref[2 * t : 2 * t + 2, :] = squares[0:2]
        if t % 2:
            tick()
    start(saves[1:3])
    start(sum_copies)
    tick()
    total = sums_ref[...]
    for k, cp in enumerate(sum_copies):
        cp.wait_recv()
        total = total + sums_land[k]
    scales = lax.rsqrt(total * (1.0 / width) + epsilon)
    gain_q = gains_ref[1:2, columns(blk)]
    gain_k = gains_ref[2:3, columns(blk)]
    for t in range(blocks):
        rows = slice(t * block, (t + 1) * block)
        turned_scales = jnp.concatenate(
            [scales[2 * t : 2 * t + 2], segments[:, rows], jnp.zeros((5, block), f32)],
            axis=0,
        ).T
        stat_ref[rows, :] = jnp.concatenate(
            [turned_scales, jnp.zeros((block, 120), f32)], axis=1
        )
        cosine, sine = cos_ref[rows, :], sin_ref[rows, :]
        q = pre_ref[rows, :cols_here] * turned_scales[:, 0:1] * gain_q
        low_ref[rows, :cols_here] = turned(q, cosine, sine).astype(bf16)
        k = pre_ref[rows, cols_here : 2 * cols_here] * turned_scales[:, 1:2] * gain_k
        low_ref[rows, cols_here : 2 * cols_here] = turned(k, cosine, sine).astype(bf16)
    tick()

    for t in range(blocks):
        rows = slice(t * block, (t + 1) * block)
        keys = (t + 1) * block
        stat = stat_ref[rows, :]
        place_q = lax.broadcasted_iota(jnp.int32, (block, keys), 0) + t * block
        place_k = lax.broadcasted_iota(jnp.int32, (block, keys), 1)
        allowed = (place_k <= place_q) & (segments[:, :keys] == stat[:, 2:3])
        lane = lax.broadcasted_iota(jnp.int32, stat.shape, 1)
        for h in range(cols_here // HEAD_DIM):
            cols = slice(h * HEAD_DIM, (h + 1) * HEAD_DIM)
            q = low_ref[rows, cols]
            k = low_ref[0:keys, cols_here + h * HEAD_DIM : cols_here + (h + 1) * HEAD_DIM]
            v = low_ref[
                0:keys, 2 * cols_here + h * HEAD_DIM : 2 * cols_here + (h + 1) * HEAD_DIM
            ]
            scores = jnp.where(allowed, dot_nt(q, k) * HEAD_DIM**-0.5, masked_score)
            top = jnp.max(scores, axis=-1, keepdims=True)
            raised = jnp.where(allowed, jnp.exp(scores - top), 0.0)
            share = 1.0 / jnp.sum(raised, axis=-1, keepdims=True)
            out = dot((raised * share).astype(bf16), v)
            att_ref[rows, cols] = out
            per = block // tokens
            att_low[t * per : (t + 1) * per, :, cols] = out.astype(bf16).reshape(
                per, tokens, HEAD_DIM
            )
            stat = jnp.where(lane == 3 + h, top, jnp.where(lane == 5 + h, share, stat))
        stat_ref[rows, :] = stat
        if t % 2:
            tick()
    start(saves[3:])
    home_ref[:, columns(blk)] = att_low[blk]
    start(home_copies)
    tick()
    while ticks[0] < len(streams) - parts + 3:
        tick()
    for stages in for_output:
        stages[4]()
    wo_load.start()
    arrived(home_copies)
    wo_load.wait()
    mid = hrow[blk].astype(f32)
    cut = 512
    for n in range(width // cut):
        cols = slice(n * cut, (n + 1) * cut)
        mid_ref[:, cols] = mid[:, cols] + dot(
            home_ref[...], wo_buf[:, :, :, :, :, cols].reshape(width, cut)
        )
    mid = mid_ref[...]
    expert_ref[...] = (mid * norm_rows(mid) * gains_ref[3:4, :]).astype(bf16)
    while ticks[0] < len(streams) + 3:
        tick()
    for stages in for_upstream:
        stages[4]()
    for cp in col_copies + col_over + col_relay + sum_copies + home_copies:
        cp.wait_send()
    for cp in saves:
        cp.wait()


def front(hidden, wq, wk, wv, wo, upstream, pack, cosine, sine):
    any_, vm = pl.BlockSpec(memory_space=pl.ANY), pl.BlockSpec(memory_space=pltpu.VMEM)
    tokens, width = hidden.shape
    wrows = wq.shape[0]
    seq, cols = 8 * tokens, width // 8
    dma = pltpu.SemaphoreType.DMA
    streams = 4 * (1 + tokens // 64)
    count = 11 + 9 * streams + 13 + 21 + 4 + 14
    shape = jax.ShapeDtypeStruct
    return pl.pallas_call(
        front_kernel,
        out_shape=(
            shape((4, 4, 2, wrows // 16, 16, width), bf16),
            shape((tokens // 16, 4, 4, 2, 16, width), bf16),
            shape((4, 4, 2) + pack.shape, bf16),
            shape((seq, width), bf16),
            shape((4, 8, wrows, 3 * cols), bf16),
            shape((seq, 3 * cols), bf16),
            shape((seq, 2 * cols), f32),
            shape((seq, cols), f32),
            shape((seq, 128), f32),
            shape((tokens, width), bf16),
            shape((tokens, width), f32),
            shape((tokens, width), bf16),
        ),
        in_specs=[any_] * 7 + [vm] * 2,
        out_specs=(any_, any_, vm) + (any_,) * 5 + (vm,) * 4,
        scratch_shapes=[
            pltpu.VMEM((8, tokens, width), bf16),
            pltpu.VMEM((seq, width), bf16),
            pltpu.VMEM((4, 8, wrows, 3 * cols), bf16),
            pltpu.VMEM((seq, 3 * cols), bf16),
            pltpu.VMEM((seq, 2 * cols), f32),
            pltpu.VMEM((seq, cols), f32),
            pltpu.VMEM((4, 4, 2, wrows // 16, 16, width), bf16),
            pltpu.VMEM((8, width), f32),
            pltpu.VMEM((8, seq // 4), f32),
            pltpu.VMEM((7, 8, seq // 4), f32),
            pltpu.VMEM((8, tokens, cols), bf16),
            dma((count,)),
            dma((count,)),
            dma((16 + streams,)),
        ],
        compiler_params=pltpu.CompilerParams(
            collective_id=2, has_side_effects=True, vmem_limit_bytes=56 * 2**20
        ),
        cost_estimate=pl.CostEstimate(
            flops=10**10, bytes_accessed=2 * 10**8, transcendentals=0
        ),
    )(
        hidden,
        wq,
        wk,
        wv,
        wo.reshape(-1, 16, width),
        upstream.reshape(-1, 16, width),
        pack,
        cosine,
        sine,
    )


def added(total, *extra):
    total = total.astype(f32)
    for one in extra:
        total = total + one.astype(f32)
    return total.astype(bf16)


def reduce_stages(copy, src, got, p1a, p1b, p2, land, out):
    row, z, c = place()
    to = partners()
    half = src.shape[-1] // 2

    def own(r):
        return src.at[r, :, c]

    inside = copy(src.at[:, :, 1 - c], got, to["sib"])
    far = [
        copy(own(row ^ 3).at[:, :, pl.ds(0, half)], p1a, to["y"]),
        copy(own(row ^ 3).at[:, :, pl.ds(half, half)], p1b, to["x"]),
    ]
    near = [
        copy(own(row ^ 1), p2.at[0], to["x"]),
        copy(own(row ^ 2), p2.at[1], to["y"]),
    ]
    home = [
        copy(src.at[row, (z + k) % 4, c], land.at[k - 1], to["z%d" % k])
        for k in (1, 3, 2)
    ]

    def first():
        inside.start()

    def second():
        inside.wait_recv()
        for k in (3, 1, 2, 0):
            at = own(row ^ k)
            at[...] = added(at[...], got[row ^ k])
            if k == 3:
                for cp in far:
                    cp.start()

    def third():
        far[0].wait_recv()
        at = own(row ^ 1).at[:, :, pl.ds(0, half)]
        at[...] = added(at[...], p1a[...])
        near[0].start()
        far[1].wait_recv()
        at = own(row ^ 2).at[:, :, pl.ds(half, half)]
        at[...] = added(at[...], p1b[...])
        near[1].start()

    def fourth():
        for cp in near:
            cp.wait_recv()
        at = own(row)
        at[...] = added(at[...], p2[0], p2[1])
        for cp in home:
            cp.start()

    def fifth():
        for cp in home:
            cp.wait_recv()
        total = src[row, z, c].astype(f32)
        for k in range(3):
            total = total + land[k].astype(f32)
        out[...] = total
        for cp in [inside] + far + near + home:
            cp.wait_send()

    return first, second, third, fourth, fifth


def back_kernel(
    ga_home,
    attended_ref,
    proj_ref,
    low_ref,
    pre_ref,
    att_ref,
    stat_ref,
    seg_ref,
    gain_ref,
    cos_ref,
    sin_ref,
    normed_in,
    wcols_in,
    small_ref,
    gn_out,
    q_out,
    k_out,
    v_out,
    wo_out,
    small_out,
    normed_ref,
    wcols,
    ga,
    dq_ref,
    dk_ref,
    dv_ref,
    grads_ref,
    sums_ref,
    sums_land,
    gn,
    gn_sib,
    gn_land,
    gw,
    gw_p1,
    gw_p2,
    gw_land,
    small,
    sm_sib,
    sm_p1a,
    sm_p1b,
    sm_p2,
    sm_land,
    dwo_ref,
    wo_got,
    wo_p1a,
    wo_p1b,
    wo_p2,
    wo_land,
    send,
    recv,
    local_sem,
):
    row, z, c = place()
    blk = z * 2 + c
    to = partners()
    mates = row_mates()
    greet(mates + [to["x"], to["y"]])
    copy = Copies(send, recv)
    tokens, width = ga_home.shape
    seq = 8 * tokens
    cols_here = att_ref.shape[1]
    wrows = wo_out.shape[0]
    scale = HEAD_DIM**-0.5
    block = 256
    blocks = seq // block
    per = block // tokens

    def start(some):
        for cp in some:
            cp.start()

    def arrived(some):
        for cp in some:
            cp.wait_recv()

    def columns(b):
        return pl.ds(pl.multiple_of(b * cols_here, cols_here), cols_here)

    streams = []
    for j in range(wrows // 16):
        part = pl.ds(j * 16, 16)
        streams.append(
            reduce_stages(
                copy,
                dwo_ref.at[:, :, :, part],
                wo_got.at[j],
                wo_p1a.at[j],
                wo_p1b.at[j],
                wo_p2.at[j],
                wo_land.at[j],
                wo_out.at[part],
            )
        )
    ticks = [0]

    def tick():
        t = ticks[0]
        ticks[0] += 1
        for stage in range(5):
            if 0 <= t - stage < len(streams):
                streams[t - stage][stage]()

    own_ga = pltpu.make_async_copy(
        ga_home.at[:, columns(blk)], ga.at[blk], local_sem.at[0]
    )
    ga_copies = [copy(ga_home.at[:, columns(mate[1])], ga.at[blk], mate) for mate in mates]
    sum_copies = [
        copy(sums_ref, sums_land.at[k], mate) for k, mate in enumerate(mates)
    ]
    half = gw.shape[1] // 2
    w_far = [
        copy(gw.at[row ^ 3, pl.ds(0, half)], gw_p1.at[0], to["y"]),
        copy(gw.at[row ^ 3, pl.ds(half, half)], gw_p1.at[1], to["x"]),
    ]
    w_near = [
        copy(gw.at[row ^ 1], gw_p2.at[0], to["x"]),
        copy(gw.at[row ^ 2], gw_p2.at[1], to["y"]),
    ]
    w_home = [copy(gw.at[row, mate[1]], gw_land.at[blk], mate) for mate in mates]
    d0, d1 = 3 - z, (3 * z + 2) % 5
    d2 = 3 - d1
    inner, outer = (z == 1) | (z == 2), (z == 0) | (z == 3)
    n_sib = [
        copy(gn.at[chip, 1 - c], gn_sib.at[chip], to["sib"]) for chip in (d0, d1, d2, z)
    ]
    n_relay = copy(gn.at[d0, c], gn_land.at[0], (row, (1 + z // 2) * 2 + c))
    n_inner = copy(gn.at[d0, c], gn_land.at[1], (row, (2 - z // 2) * 2 + c))
    n_home = [
        copy(gn.at[d1, c], gn_land.at[2], (row, d1 * 2 + c)),
        copy(gn.at[d2, c], gn_land.at[3], (row, d2 * 2 + c)),
    ]
    s_sib = copy(small.at[0], sm_sib, to["sib"])
    s_far = [
        copy(small.at[1, row ^ 3, 0:2], sm_p1a, to["y"]),
        copy(small.at[1, row ^ 3, 2:4], sm_p1b, to["x"]),
    ]
    s_near = [
        copy(small.at[1, row ^ 1], sm_p2.at[0], to["x"]),
        copy(small.at[1, row ^ 2], sm_p2.at[1], to["y"]),
    ]
    s_home = [
        copy(small.at[1, row, (z + k) % 4], sm_land.at[k - 1], to["z%d" % k])
        for k in (1, 3, 2)
    ]

    late = [
        pltpu.make_async_copy(src, dst, local_sem.at[1 + len(streams) + k])
        for k, (src, dst) in enumerate(
            ((normed_in, normed_ref), (wcols_in, wcols))
        )
    ]
    own_ga.start()
    start(ga_copies)
    start(late)

    @pl.loop(0, 8)
    def _(n):
        some = attended_ref[:, pl.ds(pl.multiple_of(n * block, block), block)]
        made = dot_tn(some, proj_ref[...]).astype(bf16)
        dwo_ref[n // 2, pl.ds(2 * (n % 2), 2)] = made.reshape(2, 2, wrows, width)

    tick()
    dk_ref[...] = jnp.zeros_like(dk_ref)
    dv_ref[...] = jnp.zeros_like(dv_ref)
    small[0] = small_ref[...]
    own_ga.wait()
    arrived(ga_copies)

    segments = seg_ref[0:1, :]
    for t in range(blocks):
        rows = slice(t * block, (t + 1) * block)
        keys = (t + 1) * block
        stat = stat_ref[rows, :]
        place_q = lax.broadcasted_iota(jnp.int32, (block, keys), 0) + t * block
        place_k = lax.broadcasted_iota(jnp.int32, (block, keys), 1)
        allowed = (place_k <= place_q) & (segments[:, :keys] == stat[:, 2:3])
        for h in range(cols_here // HEAD_DIM):
            cols = slice(h * HEAD_DIM, (h + 1) * HEAD_DIM)
            q = low_ref[rows, cols]
            k = low_ref[0:keys, cols_here + h * HEAD_DIM : cols_here + (h + 1) * HEAD_DIM]
            v = low_ref[
                0:keys, 2 * cols_here + h * HEAD_DIM : 2 * cols_here + (h + 1) * HEAD_DIM
            ]
            g = ga[t * per : (t + 1) * per, :, cols].reshape(block, HEAD_DIM)
            scores = jnp.where(allowed, dot_nt(q, k) * scale, masked_score)
            raised = jnp.exp(scores - stat[:, 3 + h : 4 + h])
            probs = jnp.where(allowed, raised, 0.0) * stat[:, 5 + h : 6 + h]
            delta = jnp.sum(g.astype(f32) * att_ref[rows, cols], axis=-1, keepdims=True)
            ds = (probs * (dot_nt(g, v) - delta)).astype(bf16)
            dq_ref[rows, cols] = dot(ds, k) * scale
            dk_ref[0:keys, cols] += dot_tn(ds, q) * scale
            dv_ref[0:keys, cols] += dot_tn(probs.astype(bf16), g)
        tick()

    pairs = row_pairs(cols_here)
    gain_q, gain_k = gain_ref[0:1, :], gain_ref[1:2, :]
    for_q = jnp.zeros((1, cols_here), f32)
    for_k = jnp.zeros((1, cols_here), f32)
    for t in range(blocks):
        rows = slice(t * block, (t + 1) * block)
        cosine, sine = cos_ref[rows, :], -sin_ref[rows, :]
        q_pre, k_pre = pre_ref[rows, :cols_here], pre_ref[rows, cols_here:]
        dq = turned(dq_ref[rows, :], cosine, sine)
        dk = turned(dk_ref[rows, :], cosine, sine)
        dq_ref[rows, :] = dq
        dk_ref[rows, :] = dk
        vq, vk = dq * q_pre, dk * k_pre
        for_q = for_q + jnp.sum(vq * stat_ref[rows, 0:1], axis=0, keepdims=True)
        for_k = for_k + jnp.sum(vk * stat_ref[rows, 1:2], axis=0, keepdims=True)
        sums = sums_by_row(pairs, jnp.concatenate([vq * gain_q, vk * gain_k], axis=1))
        sums_ref[2 * t : 2 * t + 2, :] = sums[0:2]
    start(sum_copies)
    tick()
    total = sums_ref[...]
    for k, cp in enumerate(sum_copies):
        cp.wait_recv()
        total = total + sums_land[k]
    means = total * (1.0 / width)
    for t in range(blocks):
        rows = slice(t * block, (t + 1) * block)
        mean = jnp.concatenate(
            [means[2 * t : 2 * t + 2], jnp.zeros((6, block), f32)], axis=0
        ).T
        for j, (d_ref, gain) in enumerate(((dq_ref, gain_q), (dk_ref, gain_k))):
            cols = slice(j * cols_here, (j + 1) * cols_here)
            r = stat_ref[rows, j : j + 1]
            grads_ref[rows, cols] = (
                r * gain * d_ref[rows, :]
                - pre_ref[rows, cols] * (r * r * r) * mean[:, j : j + 1]
            ).astype(bf16)
        grads_ref[rows, 2 * cols_here :] = dv_ref[rows, :].astype(bf16)

    deep = 8 * wrows
    for cp in late:
        cp.wait()

    def weight_rows(k):
        there = row ^ k
        some = normed_ref[:, pl.ds(pl.multiple_of(there * deep, deep), deep)]
        gw[there] = (
            dot_tn(some, grads_ref[...]).astype(bf16).reshape(8, wrows, 3 * cols_here)
        )

    weight_rows(3)
    start(w_far)
    weights = wcols[...].reshape(width, 3 * cols_here)
    for_attn = jnp.zeros((1, width), f32)
    chips = (d0, d1, d2, z)
    for n, chip in enumerate(chips):
        tok = pl.ds(pl.multiple_of(chip * block, block), block)
        made = dot_nt(grads_ref[tok, :], weights)
        gn[chip] = made.astype(bf16).reshape(per, tokens, width)
        n_sib[n].start()
        for_attn = for_attn + jnp.sum(
            made * normed_ref[tok, :].astype(f32), axis=0, keepdims=True
        )
        if n:
            before = chips[n - 1]
            n_sib[n - 1].wait_recv()
            n_sib[n - 1].wait_send()
            gn[before, c] = added(gn[before, c], gn_sib[before])
            if n == 1:
                pl.when(outer)(n_relay.start)
                pl.when(inner)(n_inner.start)
            elif n == 2:
                n_home[0].start()
    weight_rows(1)
    weight_rows(2)

    @pl.when(inner)
    def _():
        n_relay.wait_recv()
        gn[d2, c] = added(gn[d2, c], gn_land[0])

    n_home[1].start()
    weight_rows(0)
    tick()
    for r in range(4):
        for q in range(4):
            at = (r * 4 + q) * 128
            small[0, r, q, 16:17, :] = for_attn[:, at : at + 128]
    for j in range(cols_here // 128):
        at = blk * (cols_here // 128) + j
        small[0, at // 4, at % 4, 17:18, :] = for_q[:, j * 128 : (j + 1) * 128]
        small[0, at // 4, at % 4, 18:19, :] = for_k[:, j * 128 : (j + 1) * 128]
    s_sib.start()

    arrived(w_far[:1])
    gw[row ^ 1, 0:half] = added(gw[row ^ 1, 0:half], gw_p1[0])
    w_near[0].start()
    arrived(w_far[1:])
    gw[row ^ 2, half:] = added(gw[row ^ 2, half:], gw_p1[1])
    w_near[1].start()
    s_sib.wait_recv()
    small[1] = small[0] + sm_sib[...]
    start(s_far)
    tick()
    arrived(s_far)
    small[1, row ^ 1, 0:2] = small[1, row ^ 1, 0:2] + sm_p1a[...]
    small[1, row ^ 2, 2:4] = small[1, row ^ 2, 2:4] + sm_p1b[...]
    start(s_near)
    arrived(w_near)
    for b in range(8):
        gw[row, b] = added(gw[row, b], gw_p2[0, b], gw_p2[1, b])
    start(w_home)
    arrived(s_near)
    small[1, row] = small[1, row] + sm_p2[0] + sm_p2[1]
    start(s_home)
    while ticks[0] < len(streams) + 4:
        tick()

    n_sib[3].wait_recv()
    gn_out[...] = gn[z, c].astype(f32) + gn_sib[z].astype(f32)
    arrived(n_home)
    gn_out[...] += gn_land[2].astype(f32) + gn_land[3].astype(f32)

    @pl.when(inner)
    def _():
        n_inner.wait_recv()
        n_inner.wait_send()
        gn_out[...] += gn_land[1].astype(f32)

    @pl.when(outer)
    def _():
        n_relay.wait_send()

    arrived(s_home)
    small_out[...] = small[1, row, z] + sm_land[0] + sm_land[1] + sm_land[2]
    gw_land[blk] = gw[row, blk]
    arrived(w_home)
    for b in range(8):
        for j, out in enumerate((q_out, k_out, v_out)):
            out[:, b * cols_here : (b + 1) * cols_here] = gw_land[
                b, :, j * cols_here : (j + 1) * cols_here
            ].astype(f32)
    n_sib[3].wait_send()
    for cp in ga_copies + sum_copies + w_far + w_near + w_home + n_home:
        cp.wait_send()
    for cp in [s_sib] + s_far + s_near + s_home:
        cp.wait_send()


def back(ga, att_low, proj, low, pre, att, stat, seg, gain, cosine, sine, normed, wcols, small):
    any_, vm = pl.BlockSpec(memory_space=pl.ANY), pl.BlockSpec(memory_space=pltpu.VMEM)
    tokens, width = ga.shape
    seq, cols = 8 * tokens, width // 8
    wrows = wcols.shape[2]
    fields = small.shape[2:]
    dma = pltpu.SemaphoreType.DMA
    streams = wrows // 16
    count = 8 * streams + 7 + 7 + 2 + 2 + 7 + 4 + 4 + 1 + 2 + 2 + 3
    shape, vmem = jax.ShapeDtypeStruct, pltpu.VMEM
    weight = shape((wrows, width), f32)
    return pl.pallas_call(
        back_kernel,
        out_shape=(
            shape((tokens, width), f32),
            weight,
            weight,
            weight,
            weight,
            shape(fields, f32),
        ),
        in_specs=[any_] + [vm] * 10 + [any_] * 2 + [vm],
        out_specs=(vm,) * 6,
        scratch_shapes=[
            vmem((seq, width), bf16),
            vmem((4, 8, wrows, 3 * cols), bf16),
            vmem((8, tokens, cols), bf16),
            vmem((seq, cols), f32),
            vmem((seq, cols), f32),
            vmem((seq, cols), f32),
            vmem((seq, 3 * cols), bf16),
            vmem((8, seq // 4), f32),
            vmem((7, 8, seq // 4), f32),
            vmem((4, 2, tokens, width), bf16),
            vmem((4, tokens, width), bf16),
            vmem((4, tokens, width), bf16),
            vmem((4, 8, wrows, 3 * cols), bf16),
            vmem((2, 4, wrows, 3 * cols), bf16),
            vmem((2, 8, wrows, 3 * cols), bf16),
            vmem((8, wrows, 3 * cols), bf16),
            vmem((2, 4, 4) + fields, f32),
            vmem((4, 4) + fields, f32),
            vmem((2,) + fields, f32),
            vmem((2,) + fields, f32),
            vmem((2, 4) + fields, f32),
            vmem((3,) + fields, f32),
            vmem((4, 4, 2, wrows, width), bf16),
            vmem((streams, 4, 4, 16, width), bf16),
            vmem((streams, 4, 16, width // 2), bf16),
            vmem((streams, 4, 16, width // 2), bf16),
            vmem((streams, 2, 4, 16, width), bf16),
            vmem((streams, 3, 16, width), bf16),
            dma((count,)),
            dma((count,)),
            dma((4 + streams,)),
        ],
        compiler_params=pltpu.CompilerParams(
            collective_id=7, has_side_effects=True, vmem_limit_bytes=60 * 2**20
        ),
        cost_estimate=pl.CostEstimate(
            flops=10**10, bytes_accessed=2 * 10**8, transcendentals=0
        ),
    )(
        ga,
        att_low,
        proj,
        low,
        pre,
        att,
        stat,
        seg,
        gain,
        cosine,
        sine,
        normed,
        wcols,
        small,
    )


def rope_tables(count):
    half = HEAD_DIM // 2
    frequency = jnp.exp(
        -math.log(10000.0) * 2.0 * jnp.arange(half, dtype=f32) / HEAD_DIM
    )
    angles = jnp.arange(count, dtype=f32)[:, None] * frequency[None, :]
    return jnp.cos(angles), jnp.sin(angles)


def rope(values, cosine, sine):
    half = HEAD_DIM // 2
    a, b = values[..., :half], values[..., half:]
    return jnp.concatenate([a * cosine - b * sine, b * cosine + a * sine], axis=-1)


def norm_back(v, r, g, c, mean_vgc):
    return r * g * c - v * (r * r * r) * mean_vgc


def experts_by_scan(expert_in, upstream, gates, gate_local, up_local, down_local):
    tokens, width = expert_in.shape
    experts = gates.shape[1]
    rows, blocks = lax.axis_size("row"), lax.axis_size("blk")
    devices = rows * blocks
    me = lax.axis_index("row") * blocks + lax.axis_index("blk")
    parts = devices * tokens // 2048
    step = tokens // parts
    all_gates = lax.all_gather(gates, BOTH, axis=0, tiled=False)
    own_gate = jnp.sum(
        jnp.where(
            jnp.arange(experts, dtype=jnp.int32)[None, None, :] == me // 2,
            all_gates,
            0.0,
        ),
        axis=-1,
    )

    def expert_part(sums, items):
        own_rows, own_upstream, gate_col = items
        got = lax.all_gather(own_rows, BOTH, axis=0, tiled=True)
        up_stream = lax.all_gather(own_upstream, BOTH, axis=0, tiled=True)
        gate_col = gate_col.reshape(devices * step, 1)
        gate_pre = dot(got, gate_local)
        up_pre = dot(got, up_local)
        sig = jax.nn.sigmoid(gate_pre)
        silu = gate_pre * sig
        hidden = (silu * up_pre).astype(bf16)
        part_f = dot(hidden, down_local).astype(bf16).astype(f32)
        up_f = up_stream.astype(f32)
        dots = jnp.sum(part_f * up_f, axis=-1).reshape(devices, step)
        mixed = (gate_col * part_f).astype(bf16)
        out = lax.psum_scatter(mixed, BOTH, scatter_dimension=0, tiled=True)
        grad_part = (gate_col * up_f).astype(bf16)
        grad_hidden = dot_nt(grad_part, down_local)
        grad_gate_pre = (
            grad_hidden * up_pre * sig * (1.0 + gate_pre * (1.0 - sig))
        ).astype(bf16)
        grad_up_pre = (grad_hidden * silu).astype(bf16)
        grad_rows = (
            dot_nt(grad_gate_pre, gate_local) + dot_nt(grad_up_pre, up_local)
        ).astype(bf16)
        back = lax.psum_scatter(grad_rows, BOTH, scatter_dimension=0, tiled=True)
        sums = (
            sums[0] + dot_tn(got, grad_gate_pre),
            sums[1] + dot_tn(got, grad_up_pre),
            sums[2] + dot_tn(hidden, grad_part),
        )
        return sums, (out, back, dots)

    sums = (
        jnp.zeros(gate_local.shape, f32),
        jnp.zeros(up_local.shape, f32),
        jnp.zeros(down_local.shape, f32),
    )
    items = (
        expert_in.reshape(parts, step, width),
        upstream.reshape(parts, step, width),
        own_gate.reshape(devices, parts, step).transpose(1, 0, 2),
    )
    if parts > 2:
        sums, (outs, backs, dots) = lax.scan(expert_part, sums, items)
    else:
        made = []
        for part in range(parts):
            sums, result = expert_part(sums, tuple(item[part] for item in items))
            made.append(result)
        outs, backs, dots = (jnp.stack(some) for some in zip(*made))
    dots = dots.transpose(1, 0, 2).reshape(devices, tokens)
    outs = outs.reshape(tokens, width)
    backs = backs.reshape(tokens, width)
    dots = lax.all_to_all(dots, BOTH, split_axis=0, concat_axis=0, tiled=True)
    grad_gates = jnp.sum(dots.reshape(experts, 2, tokens), axis=1).T
    return outs.astype(f32), backs.astype(f32), grad_gates, sums


def own_mesh_body(
    hidden_in,
    segment_ids,
    expert_ids,
    attention_gain,
    query_gain,
    key_gain,
    expert_gain,
    query_weight,
    key_weight,
    value_weight,
    output_weight,
    router_weight,
    gate_weight,
    up_weight,
    down_weight,
    grad_out,
):
    tokens, width = hidden_in.shape[1:]
    wrows = query_weight.shape[0]
    experts = router_weight.shape[1]
    blocks = lax.axis_size("blk")
    seq = tokens * blocks
    head_cols = width // blocks
    blk = lax.axis_index("blk")
    upstream_low = grad_out[0]

    experts_in_order = jnp.arange(experts, dtype=jnp.int32)
    routed = jnp.any(
        expert_ids[0][:, :, None] == experts_in_order[None, None, :], axis=1
    )
    routed_t = jnp.any(
        expert_ids[0].T[None, :, :] == experts_in_order[:, None, None], axis=1
    )
    gains = jnp.stack([attention_gain, query_gain, key_gain, expert_gain])
    spare = tokens - wrows
    gains = jnp.concatenate([gains, gains], axis=1)
    lane = jnp.arange(2 * wrows, dtype=jnp.int32)[None]
    gains = jnp.where(lane // wrows == blk % 2, gains, 0)

    def rows_at(first, values, lanes):
        return jnp.pad(values.astype(f32), ((first, 64 - first - values.shape[0]), (0, lanes)))

    pack = (
        rows_at(0, routed_t, 0)
        + rows_at(16, segment_ids, 0)
        + rows_at(32, router_weight.T, spare)
        + rows_at(32 + experts, gains, 0)
    ).astype(bf16)
    half = HEAD_DIM // 2
    frequency = np.exp(-math.log(10000.0) * 2.0 * np.arange(half) / HEAD_DIM)
    angles = np.arange(seq)[:, None] * frequency.astype(np.float32)[None, :]
    angles = angles.astype(np.float32)
    cosine, sine = np.cos(angles), np.sin(angles)
    cosine = jnp.asarray(np.concatenate([cosine, cosine], axis=1), f32)
    sine = jnp.asarray(np.concatenate([-sine, sine], axis=1), f32)
    (
        full_output,
        upstream_all,
        packs,
        normed_row,
        qkv_cols,
        low,
        pre,
        attended,
        stats,
        attended_low,
        residual_mid,
        expert_in,
    ) = front(
        hidden_in[0],
        query_weight,
        key_weight,
        value_weight,
        output_weight,
        upstream_low,
        pack,
        cosine,
        sine,
    )
    full_output = full_output.reshape(width, width)
    packs = packs.reshape(-1, pack.shape[0], tokens)
    router = packs[:, 32 : 32 + experts, :wrows].transpose(0, 2, 1).reshape(width, -1)
    gains = packs[:, 32 + experts : 36 + experts].reshape(-1, 2, 4, tokens).sum(axis=1)
    gains = gains.transpose(1, 0, 2).reshape(4, width).astype(f32)
    gain_attn, gain_expert = gains[0], gains[3]
    own_q_gain = lax.dynamic_slice_in_dim(gains[1], blk * head_cols, head_cols)
    own_k_gain = lax.dynamic_slice_in_dim(gains[2], blk * head_cols, head_cols)
    steps = tokens // 16
    mask = packs[:, :experts].astype(f32).reshape(-1, experts, steps, 16)
    mask = mask.transpose(2, 0, 3, 1).reshape(steps, -1, experts)
    x = hidden_in[0].astype(f32)
    r_attn = lax.rsqrt(jnp.mean(x * x, axis=-1, keepdims=True) + epsilon)
    r_exp = lax.rsqrt(
        jnp.mean(residual_mid * residual_mid, axis=-1, keepdims=True) + epsilon
    )
    logits = dot(expert_in, router)
    top_logit = jnp.max(
        jnp.where(routed, logits, masked_score), axis=-1, keepdims=True
    )
    gates = jnp.where(routed, jnp.exp(logits - top_logit), 0.0)
    gates = gates / jnp.sum(gates, axis=-1, keepdims=True)

    outs, backs, grad_gate_local, grad_up_local, grad_down_local = moe(
        expert_in,
        upstream_all,
        mask,
        router,
        gate_weight[0],
        up_weight[0],
        down_weight[0],
    )
    outs = outs.reshape(tokens, width)
    backs = backs.reshape(tokens, width + EXTRA)
    dots = backs[:, width : width + 2 * experts]
    dots = dots + backs[:, width + 64 : width + 64 + 2 * experts]
    grad_gates = jnp.sum(dots.reshape(tokens, experts, 2), axis=2)
    layer_out = (residual_mid + outs).astype(bf16)
    upstream = upstream_low.astype(f32)
    grad_picked = gates * (
        grad_gates - jnp.sum(gates * grad_gates, axis=-1, keepdims=True)
    )
    grad_logits = jnp.where(routed, grad_picked, 0.0).astype(bf16)
    grad_expert_in = backs[:, :width] + dot_nt(grad_logits, router)
    grad_router = dot_tn(grad_logits, expert_in)
    grad_gain_expert = jnp.sum(grad_expert_in * residual_mid * r_exp, axis=0)
    grad_mid = upstream + norm_back(
        residual_mid,
        r_exp,
        gain_expert,
        grad_expert_in,
        jnp.mean(residual_mid * gain_expert * grad_expert_in, axis=-1, keepdims=True),
    )
    grad_proj = grad_mid.astype(bf16)
    grad_attended = dot_nt(grad_proj, full_output).astype(bf16)
    small = jnp.concatenate(
        [
            grad_router,
            jnp.zeros((3, width), f32),
            grad_gain_expert[None],
            jnp.zeros((20 - experts, width), f32),
        ],
        axis=0,
    )
    fields = small.shape[0]
    small = small.reshape(fields, 4, 4, 2 * wrows).transpose(1, 2, 0, 3)
    grad_normed, grad_q, grad_k, grad_v, grad_output_w, small = back(
        grad_attended,
        attended_low,
        grad_proj,
        low,
        pre,
        attended,
        stats,
        jnp.broadcast_to(stats[:, 2][None], (8, seq)),
        jnp.concatenate(
            [own_q_gain[None], own_k_gain[None], jnp.zeros((6, head_cols), f32)], axis=0
        ),
        cosine,
        sine,
        normed_row,
        qkv_cols,
        small,
    )
    input_grad = grad_mid + norm_back(
        x,
        r_attn,
        gain_attn,
        grad_normed,
        jnp.mean(x * gain_attn * grad_normed, axis=-1, keepdims=True),
    )
    small = lax.dynamic_slice_in_dim(small, (blk % 2) * wrows, wrows, axis=1)
    return (
        layer_out[None],
        input_grad[None],
        small[experts] / attention_gain.astype(f32),
        small[experts + 1],
        small[experts + 2],
        small[experts + 3],
        grad_q,
        grad_k,
        grad_v,
        grad_output_w,
        small[:experts].T,
        grad_gate_local[None],
        grad_up_local[None],
        grad_down_local[None],
    )


def any_mesh_body(
    hidden_in,
    segment_ids,
    expert_ids,
    attention_gain,
    query_gain,
    key_gain,
    expert_gain,
    query_weight,
    key_weight,
    value_weight,
    output_weight,
    router_weight,
    gate_weight,
    up_weight,
    down_weight,
    grad_out,
):
    tokens = hidden_in.shape[1]
    width = hidden_in.shape[2]
    experts = router_weight.shape[1]
    rows, blocks = lax.axis_size("row"), lax.axis_size("blk")
    devices = rows * blocks
    seq = tokens * blocks
    head_cols = width // blocks
    heads_here = HEADS // blocks
    blk = lax.axis_index("blk")
    me = lax.axis_index("row") * blocks + blk
    scale = HEAD_DIM**-0.5

    small = jnp.concatenate(
        [
            router_weight,
            attention_gain[:, None],
            query_gain[:, None],
            key_gain[:, None],
            expert_gain[:, None],
        ],
        axis=1,
    )
    small = lax.all_gather(small, BOTH, axis=0, tiled=True)
    router = small[:, :experts]
    gains = small[:, experts:].astype(f32)
    gain_attn, gain_expert = gains[:, 0], gains[:, 3]
    own_q_gain = lax.dynamic_slice_in_dim(gains[:, 1], blk * head_cols, head_cols)
    own_k_gain = lax.dynamic_slice_in_dim(gains[:, 2], blk * head_cols, head_cols)

    x = hidden_in[0].astype(f32)
    r_attn = lax.rsqrt(jnp.mean(x * x, axis=-1, keepdims=True) + epsilon)
    normed = (x * r_attn * gain_attn).astype(bf16)
    normed_row = lax.all_gather(normed, "blk", axis=0, tiled=True)
    segments = lax.all_gather(segment_ids[0], "blk", axis=0, tiled=True)

    stacked = jnp.stack([query_weight, key_weight, value_weight], axis=0)
    wrows = stacked.shape[1]
    stacked = stacked.reshape(3, wrows, blocks, head_cols).transpose(2, 1, 0, 3)
    stacked = stacked.reshape(blocks, wrows, 3 * head_cols)
    cols = lax.all_to_all(stacked, "blk", split_axis=0, concat_axis=0, tiled=True)
    cols = cols.reshape(blocks * wrows, 3 * head_cols)
    qkv_cols = lax.all_gather(cols, "row", axis=0, tiled=True)
    full_output = lax.all_gather(output_weight, BOTH, axis=0, tiled=True)

    qkv = dot(normed_row, qkv_cols)
    query_pre = qkv[:, :head_cols]
    key_pre = qkv[:, head_cols : 2 * head_cols]
    value = qkv[:, 2 * head_cols :].astype(bf16)
    squares = jnp.stack(
        [jnp.sum(query_pre * query_pre, axis=-1), jnp.sum(key_pre * key_pre, axis=-1)]
    )
    squares = lax.psum(squares, "blk") / width
    r_q = lax.rsqrt(squares[0] + epsilon)[:, None]
    r_k = lax.rsqrt(squares[1] + epsilon)[:, None]
    cosine, sine = (table[:, None] for table in rope_tables(seq))

    def heads(v):
        return v.reshape(seq, heads_here, HEAD_DIM)

    query = rope(heads(query_pre * r_q * own_q_gain), cosine, sine).astype(bf16)
    key = rope(heads(key_pre * r_k * own_k_gain), cosine, sine).astype(bf16)
    value = heads(value)
    places = jnp.arange(seq, dtype=jnp.int32)
    allowed = (places[None, :] <= places[:, None]) & (
        segments[None, :] == segments[:, None]
    )
    scores = jnp.einsum("qhd,khd->hqk", query, key, preferred_element_type=f32) * scale
    scores = jnp.where(allowed[None], scores, masked_score)
    top = jnp.max(scores, axis=-1, keepdims=True)
    weights = jnp.where(allowed[None], jnp.exp(scores - top), 0.0)
    total = jnp.sum(weights, axis=-1, keepdims=True)
    probs = weights / total
    probs_low = probs.astype(bf16)
    attended = jnp.einsum("hqk,khd->qhd", probs_low, value, preferred_element_type=f32)
    attended_low_cols = attended.astype(bf16).reshape(blocks, tokens, head_cols)
    attended_low = lax.all_to_all(
        attended_low_cols, "blk", split_axis=0, concat_axis=0, tiled=True
    )
    attended_low = attended_low.transpose(1, 0, 2).reshape(tokens, width)

    residual_mid = x + dot(attended_low, full_output)
    r_exp = lax.rsqrt(
        jnp.mean(residual_mid * residual_mid, axis=-1, keepdims=True) + epsilon
    )
    expert_in = (residual_mid * r_exp * gain_expert).astype(bf16)
    logits = dot(expert_in, router)
    routes = expert_ids[0]
    routed = jnp.any(
        routes[:, :, None] == jnp.arange(experts, dtype=jnp.int32)[None, None, :],
        axis=1,
    )
    top_logit = jnp.max(
        jnp.where(routed, logits, masked_score), axis=-1, keepdims=True
    )
    gates = jnp.where(routed, jnp.exp(logits - top_logit), 0.0)
    gates = gates / jnp.sum(gates, axis=-1, keepdims=True)

    gate_local, up_local, down_local = gate_weight[0], up_weight[0], down_weight[0]
    outs, backs, grad_gates, sums = experts_by_scan(
        expert_in, grad_out[0], gates, gate_local, up_local, down_local
    )
    grad_gate_local, grad_up_local, grad_down_local = sums
    layer_out = (residual_mid + outs).astype(bf16)
    upstream = grad_out[0].astype(f32)
    grad_picked = gates * (
        grad_gates - jnp.sum(gates * grad_gates, axis=-1, keepdims=True)
    )
    grad_logits = jnp.where(routed, grad_picked, 0.0).astype(bf16)
    grad_expert_in = backs + dot_nt(
        grad_logits, router
    )
    grad_router = dot_tn(expert_in, grad_logits)
    grad_gain_expert = jnp.sum(grad_expert_in * residual_mid * r_exp, axis=0)
    grad_mid = upstream + norm_back(
        residual_mid,
        r_exp,
        gain_expert,
        grad_expert_in,
        jnp.mean(residual_mid * gain_expert * grad_expert_in, axis=-1, keepdims=True),
    )
    grad_proj = grad_mid.astype(bf16)
    grad_output_w = dot_tn(attended_low, grad_proj).astype(bf16)
    grad_output_w = lax.psum_scatter(
        grad_output_w, BOTH, scatter_dimension=0, tiled=True
    ).astype(f32)
    grad_attended = dot_nt(grad_proj, full_output).astype(bf16)
    grad_attended = grad_attended.reshape(tokens, blocks, head_cols).transpose(1, 0, 2)
    grad_attended = lax.all_to_all(
        grad_attended, "blk", split_axis=0, concat_axis=0, tiled=True
    )
    grad_attended = grad_attended.reshape(seq, heads_here, HEAD_DIM)
    row_delta = jnp.sum(grad_attended.astype(f32) * attended, axis=-1).T
    grad_probs = jnp.einsum(
        "qhd,khd->hqk", grad_attended, value, preferred_element_type=f32
    )
    grad_scores = (probs * (grad_probs - row_delta[:, :, None])).astype(bf16)
    grad_value = jnp.einsum(
        "hqk,qhd->khd", probs_low, grad_attended, preferred_element_type=f32
    ).astype(bf16)
    grad_query = (
        jnp.einsum("hqk,khd->qhd", grad_scores, key, preferred_element_type=f32) * scale
    )
    grad_key = (
        jnp.einsum("hqk,qhd->khd", grad_scores, query, preferred_element_type=f32)
        * scale
    )
    grad_query = rope(grad_query, cosine, -sine).reshape(seq, head_cols)
    grad_key = rope(grad_key, cosine, -sine).reshape(seq, head_cols)
    means = jnp.stack(
        [
            jnp.sum(query_pre * own_q_gain * grad_query, axis=-1),
            jnp.sum(key_pre * own_k_gain * grad_key, axis=-1),
        ]
    )
    means = lax.psum(means, "blk") / width
    grad_q_gain = jnp.sum(grad_query * query_pre * r_q, axis=0)
    grad_k_gain = jnp.sum(grad_key * key_pre * r_k, axis=0)
    grad_query_pre = norm_back(query_pre, r_q, own_q_gain, grad_query, means[0][:, None])
    grad_key_pre = norm_back(key_pre, r_k, own_k_gain, grad_key, means[1][:, None])
    grad_qkv = jnp.concatenate(
        [
            grad_query_pre.astype(bf16),
            grad_key_pre.astype(bf16),
            grad_value.reshape(seq, head_cols),
        ],
        axis=1,
    )
    grad_w = dot_tn(normed_row, grad_qkv).astype(bf16)
    grad_w = lax.psum_scatter(grad_w, "row", scatter_dimension=0, tiled=True)
    grad_w = grad_w.reshape(blocks, wrows, 3 * head_cols)
    grad_w = lax.all_to_all(grad_w, "blk", split_axis=0, concat_axis=0, tiled=True)
    grad_w = grad_w.reshape(blocks, wrows, 3, head_cols).transpose(2, 1, 0, 3)
    grad_w = grad_w.reshape(3, wrows, width).astype(f32)
    grad_normed = dot_nt(grad_qkv, qkv_cols).astype(bf16)
    grad_normed = lax.psum_scatter(
        grad_normed, "blk", scatter_dimension=0, tiled=True
    ).astype(f32)
    grad_gain_attn = jnp.sum(grad_normed * x * r_attn, axis=0)
    input_grad = grad_mid + norm_back(
        x,
        r_attn,
        gain_attn,
        grad_normed,
        jnp.mean(x * gain_attn * grad_normed, axis=-1, keepdims=True),
    )

    def placed(vector):
        return lax.dynamic_update_slice_in_dim(
            jnp.zeros((width,), f32), vector, blk * head_cols, axis=0
        )

    small_grads = jnp.concatenate(
        [
            grad_router,
            grad_gain_attn[:, None],
            placed(grad_q_gain)[:, None],
            placed(grad_k_gain)[:, None],
            grad_gain_expert[:, None],
        ],
        axis=1,
    )
    small_grads = lax.psum_scatter(small_grads, BOTH, scatter_dimension=0, tiled=True)
    return (
        layer_out[None],
        input_grad[None],
        small_grads[:, experts],
        small_grads[:, experts + 1],
        small_grads[:, experts + 2],
        small_grads[:, experts + 3],
        grad_w[0],
        grad_w[1],
        grad_w[2],
        grad_output_w,
        small_grads[:, :experts],
        grad_gate_local[None],
        grad_up_local[None],
        grad_down_local[None],
    )


def solution(mesh):
    tokens3 = P("row", "blk", None)
    vector, matrix, cube = P(BOTH), P(BOTH, None), P(BOTH, None, None)
    own = (mesh.shape["row"], mesh.shape["blk"]) == (4, 8)
    return jax.shard_map(
        own_mesh_body if own else any_mesh_body,
        mesh=mesh,
        in_specs=(
            tokens3,
            P("row", "blk"),
            tokens3,
            vector,
            vector,
            vector,
            vector,
            matrix,
            matrix,
            matrix,
            matrix,
            matrix,
            cube,
            cube,
            cube,
            tokens3,
        ),
        out_specs=(
            tokens3,
            tokens3,
            vector,
            vector,
            vector,
            vector,
            matrix,
            matrix,
            matrix,
            matrix,
            matrix,
            cube,
            cube,
            cube,
        ),
        check_vma=False,
    )
```

```python
import functools
import math

import jax
import jax.numpy as jnp
from jax import lax
from jax.experimental import pallas as pl
from jax.experimental.pallas import tpu as pltpu
from jax.sharding import PartitionSpec as P

HEADS = 16
HEAD_DIM = 128
TOP_K = 8

epsilon = 1e-05
masked_score = -1e30
BOTH = ("row", "blk")
MESH = pl.DeviceIdType.MESH
bf16 = jnp.bfloat16
f32 = jnp.float32
EXTRA = 128
ZCOLS = 256


def dot(a, b):
    return jnp.dot(a, b, preferred_element_type=f32)


def dot_nt(a, b):
    return lax.dot_general(a, b, (((1,), (1,)), ((), ())), preferred_element_type=f32)


def dot_tn(a, b):
    return lax.dot_general(a, b, (((0,), (0,)), ((), ())), preferred_element_type=f32)


def place():
    row, blk = lax.axis_index("row"), lax.axis_index("blk")
    return row, blk // 2, blk % 2


def partners():
    row, z, c = place()
    blk = z * 2 + c
    return {
        "sib": (row, z * 2 + (1 - c)),
        "x": (row ^ 1, blk),
        "y": (row ^ 2, blk),
        "z1": (row, ((z + 1) % 4) * 2 + c),
        "z2": (row, ((z + 2) % 4) * 2 + c),
        "z3": (row, ((z + 3) % 4) * 2 + c),
    }


def remote(src, dst, send, recv, to):
    return pltpu.make_async_remote_copy(
        src_ref=src,
        dst_ref=dst,
        send_sem=send,
        recv_sem=recv,
        device_id=to,
        device_id_type=MESH,
    )


def greet(targets):
    barrier = pltpu.get_barrier_semaphore()
    for to in targets:
        pl.semaphore_signal(barrier, inc=1, device_id=to, device_id_type=MESH)
    pl.semaphore_wait(barrier, len(targets))


def moe_kernel(
    steps,
    x_ref,
    c_ref,
    mask_ref,
    router_ref,
    gate_ref,
    up_ref,
    down_ref,
    xall,
    out_ref,
    back_ref,
    dwg_out,
    dwu_out,
    dwd_out,
    wgu_ref,
    wd_ref,
    dwg_ref,
    dwu_ref,
    dwd_ref,
    xbuf,
    cbuf,
    hbuf,
    gbuf,
    po,
    pb,
    ro,
    rb,
    so,
    sb,
    p1ao,
    p1bo,
    p1ab,
    p1bb,
    p2o,
    p2b,
    zo,
    zb,
    gz,
    gp1,
    gp2,
    ag_send,
    ag_recv,
    rs_send,
    rs_recv,
    load_sem,
    weight_sem,
):
    row, z, c = place()
    to = partners()
    width = x_ref.shape[-1]
    half = width // 2
    hidden = wd_ref.shape[0]
    me = row * 8 + z * 2 + c
    expert = me // 2

    weights = [
        pltpu.make_async_copy(src, dst, weight_sem.at[k])
        for k, (src, dst) in enumerate(
            (
                (gate_ref, wgu_ref.at[:, pl.ds(0, hidden)]),
                (up_ref, wgu_ref.at[:, pl.ds(hidden, hidden)]),
                (down_ref, wd_ref),
            )
        )
    ]
    sums = [
        pltpu.make_async_copy(src, dst, weight_sem.at[3 + k])
        for k, (src, dst) in enumerate(
            ((dwg_ref, dwg_out), (dwu_ref, dwu_out), (dwd_ref, dwd_out))
        )
    ]
    for cp in weights:
        cp.start()
    greet(list(to.values()))

    def ag(j, k, src, dst, who):
        return remote(src, dst, ag_send.at[j, k], ag_recv.at[j, k], to[who])

    def own_copy(j):
        return pltpu.make_async_copy(
            x_ref.at[j], xall.at[j, row, z, c], load_sem.at[2 + j % 4]
        )

    def z_copies(j):
        slot = xall.at[j, row, z, c]
        return [ag(j, k, x_ref.at[j], slot, "z%d" % (k + 1)) for k in range(3)]

    def line_copies(j):
        line = xall.at[j, row, :, c]
        return [
            ag(j, 3, line, line, "x"),
            ag(j, 4, line, line, "y"),
            ag(j, 5, line, line, "sib"),
        ]

    def relay_copies(j):
        a = xall.at[j, row ^ 1, :, c, :, pl.ds(0, half)]
        b = xall.at[j, row ^ 2, :, c, :, pl.ds(half, half)]
        s1 = xall.at[j, row ^ 1, :, c]
        s2 = xall.at[j, row ^ 2, :, c]
        return [
            ag(j, 6, a, a, "y"),
            ag(j, 7, b, b, "x"),
            ag(j, 8, s1, s1, "sib"),
            ag(j, 9, s2, s2, "sib"),
        ]

    def last_copies(j):
        s3 = xall.at[j, row ^ 3, :, c]
        return [ag(j, 10, s3, s3, "sib")]

    def ag_z(j):
        own_copy(j).start()
        for cp in z_copies(j):
            cp.start()

    def ag_xy(j):
        own_copy(j).wait()
        for cp in z_copies(j):
            cp.wait_recv()
        for cp in line_copies(j):
            cp.start()

    def ag_rel(j):
        for cp in line_copies(j)[:2]:
            cp.wait_recv()
        for cp in relay_copies(j):
            cp.start()

    def ag_fin(j):
        for cp in relay_copies(j)[:2]:
            cp.wait_recv()
        for cp in last_copies(j):
            cp.start()

    def loads(j):
        return [
            pltpu.make_async_copy(xall.at[j], xbuf.at[j % 2], load_sem.at[0]),
            pltpu.make_async_copy(c_ref.at[j], cbuf.at[j % 2], load_sem.at[1]),
        ]

    def ag_done(j):
        line_copies(j)[2].wait_recv()
        for cp in relay_copies(j)[2:] + last_copies(j):
            cp.wait_recv()
        for cp in loads(j):
            cp.start()

    def ag_sent(j):
        for cp in z_copies(j) + line_copies(j) + relay_copies(j) + last_copies(j):
            cp.wait_send()

    arrays = (
        (po, ro, so, p1ao, p1bo, p2o, zo, out_ref),
        (pb, rb, sb, p1ab, p1bb, p2b, zb, back_ref),
    )
    near_z, near_cut = ZCOLS, ZCOLS // 2
    mid = near_z + p1ao.shape[-1]

    def rs(i, q, k, src, dst, who):
        s = i % 2
        return remote(src, dst, rs_send.at[q, s, k], rs_recv.at[q, s, k], to[who])

    def rs_sib_copy(q, i):
        p, r = arrays[q][:2]
        return rs(i, q, 0, p.at[:, :, 1 - c], r.at[i % 2], "sib")

    def p1_copies(q, i):
        p, r, s, p1a, p1b, p2, zz, out = arrays[q]
        part = s.at[i % 2, row ^ 3]
        rest = p.shape[-1] - mid
        return [
            rs(i, q, 1, part.at[:, :, pl.ds(near_z, mid - near_z)], p1a.at[i % 2], "y"),
            rs(i, q, 2, part.at[:, :, pl.ds(mid, rest)], p1b.at[i % 2], "x"),
        ]

    def p2_copies(q, i):
        p, r, s, p1a, p1b, p2, zz, out = arrays[q]
        cols = pl.ds(near_z, p.shape[-1] - near_z)
        return [
            rs(i, q, 3, s.at[i % 2, row ^ 1, :, :, cols], p2.at[i % 2, 0], "x"),
            rs(i, q, 4, s.at[i % 2, row ^ 2, :, :, cols], p2.at[i % 2, 1], "y"),
        ]

    def rsz_copies(q, i):
        p, r, s, p1a, p1b, p2, zz, out = arrays[q]
        cols = pl.ds(near_z, p.shape[-1] - near_z)
        return [
            rs(
                i,
                q,
                5 + k,
                s.at[i % 2, row, (z + k + 1) % 4, :, cols],
                zz.at[i % 2, k],
                "z%d" % (k + 1),
            )
            for k in range(3)
        ]

    def first_z_copies(q, i):
        s = arrays[q][2]
        return [
            rs(
                i,
                q,
                8 + k,
                s.at[i % 2, :, (z + k + 1) % 4, :, pl.ds(0, near_z)],
                gz.at[q, i % 2, k],
                "z%d" % (k + 1),
            )
            for k in range(3)
        ]

    def first_p1_copies(q, i):
        part = arrays[q][2].at[i % 2, row ^ 3, z]
        return [
            rs(i, q, 11, part.at[:, pl.ds(0, near_cut)], gp1.at[q, i % 2, 0], "y"),
            rs(i, q, 12, part.at[:, pl.ds(near_cut, near_cut)], gp1.at[q, i % 2, 1], "x"),
        ]

    def first_p2_copies(q, i):
        s = arrays[q][2]
        cols = pl.ds(0, near_z)
        return [
            rs(i, q, 13, s.at[i % 2, row ^ 1, z, :, cols], gp2.at[q, i % 2, 0], "x"),
            rs(i, q, 14, s.at[i % 2, row ^ 2, z, :, cols], gp2.at[q, i % 2, 1], "y"),
        ]

    def rs_sib(q, i):
        rs_sib_copy(q, i).start()

    def rs_p1(q, i):
        p, r, s, p1a, p1b, p2, zz, out = arrays[q]
        cp = rs_sib_copy(q, i)
        cp.wait_recv()

        @pl.loop(0, 4)
        def _(a):
            s[i % 2, a] = (
                p[a, :, c].astype(f32) + r[i % 2, a].astype(f32)
            ).astype(bf16)

        cp.wait_send()
        for cp in p1_copies(q, i) + first_z_copies(q, i):
            cp.start()

    def rs_p2(q, i):
        p, r, s, p1a, p1b, p2, zz, out = arrays[q]
        rest = p.shape[-1] - mid
        copies = p1_copies(q, i)
        copies[0].wait_recv()
        at = s.at[i % 2, row ^ 1, :, :, pl.ds(near_z, mid - near_z)]
        at[...] = added(at[...], p1a[i % 2])
        out_copies = p2_copies(q, i)
        out_copies[0].start()
        copies[1].wait_recv()
        at = s.at[i % 2, row ^ 2, :, :, pl.ds(mid, rest)]
        at[...] = added(at[...], p1b[i % 2])
        out_copies[1].start()
        for cp in first_z_copies(q, i):
            cp.wait_recv()
        at = s.at[i % 2, :, z, :, pl.ds(0, near_z)]
        at[...] = added(at[...], gz[q, i % 2, 0], gz[q, i % 2, 1], gz[q, i % 2, 2])
        for cp in first_p1_copies(q, i):
            cp.start()

    def rs_z(q, i):
        p, r, s, p1a, p1b, p2, zz, out = arrays[q]
        for cp in p2_copies(q, i):
            cp.wait_recv()
        at = s.at[i % 2, row, :, :, pl.ds(near_z, p.shape[-1] - near_z)]
        at[...] = added(at[...], p2[i % 2, 0], p2[i % 2, 1])
        for cp in rsz_copies(q, i):
            cp.start()
        for cp in first_p1_copies(q, i):
            cp.wait_recv()
        at = s.at[i % 2, row ^ 1, z, :, pl.ds(0, near_cut)]
        at[...] = added(at[...], gp1[q, i % 2, 0])
        at = s.at[i % 2, row ^ 2, z, :, pl.ds(near_cut, near_cut)]
        at[...] = added(at[...], gp1[q, i % 2, 1])
        for cp in first_p2_copies(q, i):
            cp.start()

    def rs_fin(q, i):
        p, r, s, p1a, p1b, p2, zz, out = arrays[q]
        copies = rsz_copies(q, i)
        for cp in copies:
            cp.wait_recv()
        total = s[i % 2, row, z, :, near_z:].astype(f32)
        for k in range(3):
            total = total + zz[i % 2, k].astype(f32)
        out[i, :, near_z:] = total
        first = first_p2_copies(q, i)
        for cp in first:
            cp.wait_recv()
        total = s[i % 2, row, z, :, :near_z].astype(f32)
        for k in range(2):
            total = total + gp2[q, i % 2, k].astype(f32)
        out[i, :, :near_z] = total
        for cp in copies + p2_copies(q, i) + p1_copies(q, i):
            cp.wait_send()
        for cp in first + first_p1_copies(q, i) + first_z_copies(q, i):
            cp.wait_send()

    lanes = po.shape[3]
    rows_here = 16 * lanes
    cut = 512

    def tile(i, t):
        s = i % 2
        xt = xbuf[s, 2 * t : 2 * t + 2].reshape(rows_here, width)
        mask = mask_ref[i, t * rows_here : (t + 1) * rows_here, :]
        logits = dot(xt, router_ref[...])[:, : mask.shape[-1]]
        logits = jnp.where(mask > 0, logits, masked_score)
        top = jnp.max(logits, axis=-1, keepdims=True)
        raised = jnp.where(mask > 0, jnp.exp(logits - top), 0.0)
        lane = lax.broadcasted_iota(jnp.int32, raised.shape, 1)
        gate = jnp.sum(
            jnp.where(lane == expert, raised, 0.0), axis=-1, keepdims=True
        ) / jnp.sum(raised, axis=-1, keepdims=True)
        both = dot(xt, wgu_ref[...])
        gp, up = both[:, :hidden], both[:, hidden:]
        sig = jax.nn.sigmoid(gp)
        silu = gp * sig
        hid = (silu * up).astype(bf16)
        hbuf[t * rows_here : (t + 1) * rows_here, :] = hid
        slope = up * sig * (1.0 + gp * (1.0 - sig))
        dots = jnp.zeros((rows_here, 1), f32)
        ghid = jnp.zeros((rows_here, hidden), f32)
        for n in range(width // cut):
            cols = slice(n * cut, (n + 1) * cut)
            wd = wd_ref[:, cols]
            part = dot(hid, wd).astype(bf16).astype(f32)
            cf = cbuf[s, 2 * t : 2 * t + 2, :, :, :, cols]
            shape = cf.shape
            cf = cf.reshape(rows_here, cut).astype(f32)
            dots = dots + jnp.sum(part * cf, axis=-1, keepdims=True)
            po[2 * t : 2 * t + 2, :, :, :, cols] = (
                (gate * part).astype(bf16).reshape(shape)
            )
            gpart = (gate * cf).astype(bf16)
            cbuf[s, 2 * t : 2 * t + 2, :, :, :, cols] = gpart.reshape(shape)
            ghid = ghid + dot_nt(gpart, wd)
        dgp = (ghid * slope).astype(bf16)
        dup = (ghid * silu).astype(bf16)
        grads = jnp.concatenate([dgp, dup], axis=1)
        gbuf[t * rows_here : (t + 1) * rows_here, :] = grads
        for n in range(width // cut):
            cols = slice(n * cut, (n + 1) * cut)
            bk = dot_nt(grads, wgu_ref[cols, :]).astype(bf16)
            pb[2 * t : 2 * t + 2, :, :, :, cols] = bk.reshape(shape)
        high = dots.astype(bf16).astype(f32)
        low = dots - high
        lane = lax.broadcasted_iota(jnp.int32, (rows_here, EXTRA), 1)
        extra = jnp.where(lane == me, high, jnp.where(lane == me + 64, low, 0.0))
        pb[2 * t : 2 * t + 2, :, :, :, width:] = extra.astype(bf16).reshape(
            shape[:-1] + (EXTRA,)
        )

    def weight_grads(i):
        s = i % 2
        every = 2 * rows_here

        @pl.loop(0, width // 256)
        def _(n):
            cols = pl.ds(pl.multiple_of(n * 256, 256), 256)
            xt = xbuf[s, :, :, :, :, cols].reshape(every, 256)
            r = dot_tn(xt, gbuf[...])
            dwg_ref[cols, :] += r[:, :hidden]
            dwu_ref[cols, :] += r[:, hidden:]

        @pl.loop(0, width // cut)
        def _(n):
            cols = pl.ds(pl.multiple_of(n * cut, cut), cut)
            gpart = cbuf[s, :, :, :, :, cols].reshape(every, cut)
            dwd_ref[:, cols] += dot_tn(hbuf[...], gpart)

    for j in range(3):
        ag_z(j)
    ag_xy(0)
    ag_xy(1)
    dwg_ref[...] = jnp.zeros_like(dwg_ref)
    dwu_ref[...] = jnp.zeros_like(dwu_ref)
    dwd_ref[...] = jnp.zeros_like(dwd_ref)
    for cp in weights:
        cp.wait()
    ag_rel(0)
    ag_rel(1)
    ag_fin(0)
    ag_done(0)
    ag_fin(1)

    @pl.loop(0, steps + 2)
    def _(i):
        def when(low, high, *work):
            @pl.when((i >= low) & (i < high))
            def _():
                for f in work:
                    f()

        @pl.when(i + 3 < steps)
        def _():
            ag_z(i + 3)

        @pl.when(i + 2 < steps)
        def _():
            ag_xy(i + 2)

        when(1, steps + 1, lambda: rs_p2(0, i - 1))
        when(2, steps + 2, lambda: rs_z(1, i - 2))

        @pl.when(i < steps)
        def _():
            for cp in loads(i):
                cp.wait()
            tile(i, 0)

        @pl.when(i + 2 < steps)
        def _():
            ag_rel(i + 2)

        when(1, steps + 1, lambda: rs_p2(1, i - 1))
        when(2, steps + 2, lambda: rs_fin(0, i - 2))

        @pl.when(i < steps)
        def _():
            tile(i, 1)
            rs_sib(0, i)
            rs_sib(1, i)

        @pl.when(i + 2 < steps)
        def _():
            ag_fin(i + 2)

        when(0, steps, lambda: rs_p1(0, i))
        when(1, steps + 1, lambda: rs_z(0, i - 1))
        when(2, steps + 2, lambda: rs_fin(1, i - 2))
        when(0, steps, lambda: rs_p1(1, i))

        @pl.when(i < steps)
        def _():
            weight_grads(i)

        @pl.when(i == steps - 1)
        def _():
            for cp in sums:
                cp.start()

        @pl.when(i + 1 < steps)
        def _():
            ag_done(i + 1)

    @pl.loop(0, steps)
    def _(j):
        ag_sent(j)

    for cp in sums:
        cp.wait()


def moe(expert_in, upstream_all, mask, router, gate, up, down):
    tokens, width = expert_in.shape
    hidden = down.shape[0]
    steps = tokens // 16
    wide = width + EXTRA
    mid = ZCOLS + (width - ZCOLS) // 2
    any_, vm = pl.BlockSpec(memory_space=pl.ANY), pl.BlockSpec(memory_space=pltpu.VMEM)
    dma = pltpu.SemaphoreType.DMA
    router = jnp.pad(router, ((0, 0), (0, 128 - router.shape[1])))
    results = pl.pallas_call(
        functools.partial(moe_kernel, steps),
        out_shape=(
            jax.ShapeDtypeStruct((steps, 4, 4, 2, 16, width), bf16),
            jax.ShapeDtypeStruct((steps, 16, width), f32),
            jax.ShapeDtypeStruct((steps, 16, wide), f32),
            jax.ShapeDtypeStruct((width, hidden), f32),
            jax.ShapeDtypeStruct((width, hidden), f32),
            jax.ShapeDtypeStruct((hidden, width), f32),
        ),
        in_specs=[any_, any_, vm, vm, any_, any_, any_],
        out_specs=(any_, vm, vm, any_, any_, any_),
        scratch_shapes=[
            pltpu.VMEM((width, 2 * hidden), bf16),
            pltpu.VMEM((hidden, width), bf16),
            pltpu.VMEM((width, hidden), f32),
            pltpu.VMEM((width, hidden), f32),
            pltpu.VMEM((hidden, width), f32),
            pltpu.VMEM((2, 4, 4, 2, 16, width), bf16),
            pltpu.VMEM((2, 4, 4, 2, 16, width), bf16),
            pltpu.VMEM((512, hidden), bf16),
            pltpu.VMEM((512, 2 * hidden), bf16),
            pltpu.VMEM((4, 4, 2, 16, width), bf16),
            pltpu.VMEM((4, 4, 2, 16, wide), bf16),
            pltpu.VMEM((2, 4, 4, 16, width), bf16),
            pltpu.VMEM((2, 4, 4, 16, wide), bf16),
            pltpu.VMEM((2, 4, 4, 16, width), bf16),
            pltpu.VMEM((2, 4, 4, 16, wide), bf16),
            pltpu.VMEM((2, 4, 16, mid - ZCOLS), bf16),
            pltpu.VMEM((2, 4, 16, width - mid), bf16),
            pltpu.VMEM((2, 4, 16, mid - ZCOLS), bf16),
            pltpu.VMEM((2, 4, 16, wide - mid), bf16),
            pltpu.VMEM((2, 2, 4, 16, width - ZCOLS), bf16),
            pltpu.VMEM((2, 2, 4, 16, wide - ZCOLS), bf16),
            pltpu.VMEM((2, 3, 16, width - ZCOLS), bf16),
            pltpu.VMEM((2, 3, 16, wide - ZCOLS), bf16),
            pltpu.VMEM((2, 2, 3, 4, 16, ZCOLS), bf16),
            pltpu.VMEM((2, 2, 2, 16, ZCOLS // 2), bf16),
            pltpu.VMEM((2, 2, 2, 16, ZCOLS), bf16),
            dma((steps, 11)),
            dma((steps, 11)),
            dma((2, 2, 15)),
            dma((2, 2, 15)),
            dma((6,)),
            dma((6,)),
        ],
        compiler_params=pltpu.CompilerParams(
            collective_id=1, has_side_effects=True, vmem_limit_bytes=60 * 2**20
        ),
        cost_estimate=pl.CostEstimate(
            flops=78 * 10**9, bytes_accessed=10**8, transcendentals=0
        ),
    )(
        expert_in.reshape(steps, 16, width),
        upstream_all,
        mask,
        router,
        gate,
        up,
        down,
    )
    return results[1:]


class Copies:
    def __init__(self, send, recv):
        self.send, self.recv, self.count, self.made = send, recv, 0, []

    def __call__(self, src, dst, who):
        k = self.count
        self.count += 1
        return remote(src, dst, self.send.at[k], self.recv.at[k], who)


def row_mates():
    row, z, c = place()
    mates = [(row, z * 2 + (1 - c))]
    for k in (1, 3, 2):
        for flip in (0, 1):
            mates.append((row, ((z + k) % 4) * 2 + (c ^ flip)))
    return mates


def gather_stages(copy, src, slots, cut, own_sem):
    row, z, c = place()
    to = partners()
    own = slots.at[row, z, c]
    line = slots.at[row, :, c]
    width = src.shape[-1]
    if cut:
        a = slots.at[row ^ 1, :, c, :, pl.ds(0, cut)]
        b = slots.at[row ^ 2, :, c, :, pl.ds(cut, width - cut)]
    else:
        a = slots.at[row ^ 1, pl.ds(0, 2), c]
        b = slots.at[row ^ 2, pl.ds(2, 2), c]
    s1, s2, s3 = (slots.at[row ^ k, :, c] for k in (1, 2, 3))
    local = pltpu.make_async_copy(src, own, own_sem)
    along_z = [copy(src, own, to["z%d" % k]) for k in (1, 3, 2)]
    over = [copy(line, line, to[k]) for k in ("x", "y", "sib")]
    relay = [copy(a, a, to["y"]), copy(b, b, to["x"])]
    inside = [copy(s1, s1, to["sib"]), copy(s2, s2, to["sib"])]
    last = [copy(s3, s3, to["sib"])]

    def start(some):
        for cp in some:
            cp.start()

    def arrived(some):
        for cp in some:
            cp.wait_recv()

    def first():
        local.start()
        start(along_z)

    def second():
        local.wait()
        arrived(along_z)
        start(over)

    def third():
        arrived(over[:2])
        start(relay + inside)

    def fourth():
        arrived(relay)
        start(last)

    def fifth():
        arrived(over[2:] + inside + last)
        for cp in along_z + over + relay + inside + last:
            cp.wait_send()

    return first, second, third, fourth, fifth


def norm_rows(v):
    return lax.rsqrt(jnp.mean(v * v, axis=-1, keepdims=True) + epsilon)


def turned(v, cosine, sine):
    heads = []
    for h in range(v.shape[1] // HEAD_DIM):
        one = v[:, h * HEAD_DIM : (h + 1) * HEAD_DIM]
        heads.append(one * cosine + pltpu.roll(one, HEAD_DIM // 2, 1) * sine)
    return jnp.concatenate(heads, axis=1)


def row_pairs(cols):
    row = lax.broadcasted_iota(jnp.int32, (8, 2 * cols), 0)
    lane = lax.broadcasted_iota(jnp.int32, (8, 2 * cols), 1)
    return jnp.where((lane // cols) == row, 1.0, 0.0).astype(f32)


def sums_by_row(pairs, v):
    return lax.dot_general(
        pairs,
        v,
        (((1,), (1,)), ((), ())),
        precision=lax.Precision.HIGHEST,
        preferred_element_type=f32,
    )


def slot_stages(copy, src, slot, k, cut, own_sem):
    row, z, c = place()
    to = partners()
    there = (z + k) % 4
    own = slot(row, z)
    s0, s1, s2, s3 = (slot(row ^ r, there) for r in range(4))
    width = src.shape[-1]
    a = slot(row ^ 1, there).at[:, :, pl.ds(0, cut)]
    b = slot(row ^ 2, there).at[:, :, pl.ds(cut, width - cut)]
    if k:
        along_z = [copy(src, own, to["z%d" % (4 - k)])]
        over = [copy(s0, s0, to[w]) for w in ("x", "y", "sib")]
    else:
        along_z = []
        local = pltpu.make_async_copy(src, own, own_sem)
        over = [copy(src, own, to[w]) for w in ("x", "y", "sib")]
    relay = [copy(a, a, to["y"]), copy(b, b, to["x"])]
    inside = [copy(s1, s1, to["sib"]), copy(s2, s2, to["sib"])]
    last = [copy(s3, s3, to["sib"])]

    def start(some):
        for cp in some:
            cp.start()

    def arrived(some):
        for cp in some:
            cp.wait_recv()

    def first():
        if k:
            start(along_z)
        else:
            local.start()

    def second():
        arrived(along_z)
        start(over)

    def third():
        arrived(over[:2])
        start(relay + inside)

    def fourth():
        arrived(relay)
        start(last)

    def fifth():
        if not k:
            local.wait()
        arrived(over[2:] + inside + last)
        for cp in along_z + over + relay + inside + last:
            cp.wait_send()

    return first, second, third, fourth, fifth


def front_kernel(
    h_ref,
    wq_ref,
    wk_ref,
    wv_ref,
    wo_ref,
    up_ref,
    pack_ref,
    cos_ref,
    sin_ref,
    woall,
    call,
    packs,
    normed_out,
    wcols_out,
    low_out,
    pre_out,
    att_out,
    stat_ref,
    home_ref,
    mid_ref,
    expert_ref,
    hrow,
    normed_ref,
    wcols,
    low_ref,
    pre_ref,
    att_ref,
    wo_buf,
    gains_ref,
    sums_ref,
    sums_land,
    att_low,
    send,
    recv,
    local_sem,
):
    row, z, c = place()
    blk = z * 2 + c
    to = partners()
    mates = row_mates()
    greet(mates + [to["x"], to["y"]])
    copy = Copies(send, recv)
    cols_here = wcols.shape[3] // 3
    tokens, width = h_ref.shape
    seq = 8 * tokens
    wrows = wq_ref.shape[0]

    pack_stages = gather_stages(copy, pack_ref, packs, 0, local_sem.at[0])
    parts = up_ref.shape[0] // 4
    streams = []
    for k in (0, 1, 3, 2):
        streams.append(
            slot_stages(
                copy,
                wo_ref,
                lambda r, q: woall.at[r, q, c],
                k,
                width // 2,
                local_sem.at[9 + len(streams)],
            )
        )
        for j in range(parts):
            part = pl.ds(j * 4, 4)
            streams.append(
                slot_stages(
                    copy,
                    up_ref.at[part],
                    lambda r, q, part=part: call.at[part, r, q, c],
                    k,
                    width // 2,
                    local_sem.at[9 + len(streams)],
                )
            )
    for_output = streams[:: parts + 1]
    for_upstream = [one for one in streams if one not in for_output]
    saves = [
        pltpu.make_async_copy(src, dst, local_sem.at[9 + len(streams) + k])
        for k, (src, dst) in enumerate(
            (
                (wcols, wcols_out),
                (normed_ref, normed_out),
                (pre_ref, pre_out),
                (low_ref, low_out),
                (att_ref, att_out),
            )
        )
    ]
    wo_load = pltpu.make_async_copy(woall, wo_buf, local_sem.at[9 + len(streams) + 5])
    ticks = [0]

    def tick():
        t = ticks[0]
        ticks[0] += 1
        for stage, lag in ((0, 0), (1, 1), (2, 2), (3, 3)):
            if 0 <= t - lag < len(streams):
                streams[t - lag][stage]()

    own_rows = pltpu.make_async_copy(h_ref, hrow.at[blk], local_sem.at[5])
    up_to, down_to = (row, blk + 2), (row, blk - 2)
    sib = to["sib"]
    own_sib = copy(h_ref, hrow.at[blk], sib)
    ups, downs = [], []
    for t in range(3):
        src = h_ref if t == 0 else hrow.at[blk - 2 * t]
        up = copy(src, hrow.at[blk - 2 * t], up_to)
        got = hrow.at[blk - 2 - 2 * t]
        ups.append((up, copy(got, got, sib), (z < 3) & (z >= t), z >= t + 1))
        src = h_ref if t == 0 else hrow.at[blk + 2 * t]
        down = copy(src, hrow.at[blk + 2 * t], down_to)
        got = hrow.at[blk + 2 + 2 * t]
        downs.append((down, copy(got, got, sib), (z > 0) & (z + t <= 3), z + t + 1 <= 3))

    def line_start(t):
        for cp, hand, sends, gets in (ups[t], downs[t]):
            pl.when(sends)(cp.start)

    def line_arrived(t):
        for cp, hand, sends, gets in (ups[t], downs[t]):

            @pl.when(gets)
            def _():
                cp.wait_recv()
                hand.start()

    def line_done():
        own_rows.wait()
        own_sib.wait()
        for t in range(3):
            for cp, hand, sends, gets in (ups[t], downs[t]):
                pl.when(sends)(cp.wait_send)
                pl.when(gets)(hand.wait)

    def columns(b):
        return pl.ds(pl.multiple_of(b * cols_here, cols_here), cols_here)

    own_cols, col_copies = [], []
    for j, w in enumerate((wq_ref, wk_ref, wv_ref)):
        there = pl.ds(j * cols_here, cols_here)
        own_cols.append(
            pltpu.make_async_copy(
                w.at[:, columns(blk)], wcols.at[row, blk, :, there], local_sem.at[6 + j]
            )
        )
        for mate in mates:
            col_copies.append(
                copy(w.at[:, columns(mate[1])], wcols.at[row, blk, :, there], mate)
            )
    half = wcols.shape[1] // 2
    col_over = [copy(wcols.at[row], wcols.at[row], to[k]) for k in ("x", "y")]
    a = wcols.at[row ^ 1, pl.ds(0, half)]
    b = wcols.at[row ^ 2, pl.ds(half, half)]
    col_relay = [copy(a, a, to["y"]), copy(b, b, to["x"])]
    sum_copies = [
        copy(sums_ref, sums_land.at[k], mate) for k, mate in enumerate(mates)
    ]
    home_copies = [
        copy(att_low.at[mate[1]], home_ref.at[:, columns(blk)], mate) for mate in mates
    ]

    def start(some):
        for cp in some:
            cp.start()

    def arrived(some):
        for cp in some:
            cp.wait_recv()

    own_rows.start()
    start(own_cols)
    line_start(0)
    own_sib.start()
    tick()
    tick()
    pack_stages[0]()
    start(col_copies)
    tick()
    pack_stages[1]()
    tick()
    line_arrived(0)
    line_start(1)
    tick()
    pack_stages[2]()
    for cp in own_cols:
        cp.wait()
    arrived(col_copies)
    start(col_over)
    pack_stages[3]()
    line_arrived(1)
    line_start(2)
    tick()
    arrived(col_over)
    start(col_relay)
    tick()
    line_arrived(2)
    pack_stages[4]()
    arrived(col_relay)
    line_done()
    tick()
    start(saves[:1])

    pieces = []
    for r in range(4):
        for q in range(4):
            pieces.append(
                packs[r, q, 0, 48:64, :].astype(f32) + packs[r, q, 1, 48:64, :].astype(f32)
            )
    gains_ref[...] = jnp.concatenate(pieces, axis=1)[0:8]
    gain_attn = gains_ref[0:1, :]
    segments = jnp.concatenate(
        [
            packs[row, q, k, 16:32, :].astype(f32)[0:1]
            for q in range(4)
            for k in range(2)
        ],
        axis=1,
    )
    pairs = row_pairs(cols_here)
    block = 256
    blocks = seq // block

    for t in range(blocks):
        rows = slice(t * block, (t + 1) * block)
        per = block // tokens
        v = hrow[t * per : (t + 1) * per].reshape(block, width).astype(f32)
        normed = (v * norm_rows(v) * gain_attn).astype(bf16)
        normed_ref[rows, :] = normed
        pre = dot(normed, wcols[...].reshape(width, 3 * cols_here))
        pre_ref[rows, :] = pre[:, : 2 * cols_here]
        low_ref[rows, 2 * cols_here :] = pre[:, 2 * cols_here :].astype(bf16)
        both = pre[:, : 2 * cols_here]
        squares = sums_by_row(pairs, both * both)
        sums_ref[2 * t : 2 * t + 2, :] = squares[0:2]
        if t % 2:
            tick()
    start(saves[1:3])
    start(sum_copies)
    tick()
    total = sums_ref[...]
    for k, cp in enumerate(sum_copies):
        cp.wait_recv()
        total = total + sums_land[k]
    scales = lax.rsqrt(total * (1.0 / width) + epsilon)
    gain_q = gains_ref[1:2, columns(blk)]
    gain_k = gains_ref[2:3, columns(blk)]
    for t in range(blocks):
        rows = slice(t * block, (t + 1) * block)
        turned_scales = jnp.concatenate(
            [scales[2 * t : 2 * t + 2], segments[:, rows], jnp.zeros((5, block), f32)],
            axis=0,
        ).T
        stat_ref[rows, :] = jnp.concatenate(
            [turned_scales, jnp.zeros((block, 120), f32)], axis=1
        )
        cosine, sine = cos_ref[rows, :], sin_ref[rows, :]
        q = pre_ref[rows, :cols_here] * turned_scales[:, 0:1] * gain_q
        low_ref[rows, :cols_here] = turned(q, cosine, sine).astype(bf16)
        k = pre_ref[rows, cols_here : 2 * cols_here] * turned_scales[:, 1:2] * gain_k
        low_ref[rows, cols_here : 2 * cols_here] = turned(k, cosine, sine).astype(bf16)
    tick()

    for t in range(blocks):
        rows = slice(t * block, (t + 1) * block)
        keys = (t + 1) * block
        stat = stat_ref[rows, :]
        place_q = lax.broadcasted_iota(jnp.int32, (block, keys), 0) + t * block
        place_k = lax.broadcasted_iota(jnp.int32, (block, keys), 1)
        allowed = (place_k <= place_q) & (segments[:, :keys] == stat[:, 2:3])
        lane = lax.broadcasted_iota(jnp.int32, stat.shape, 1)
        for h in range(cols_here // HEAD_DIM):
            cols = slice(h * HEAD_DIM, (h + 1) * HEAD_DIM)
            q = low_ref[rows, cols]
            k = low_ref[0:keys, cols_here + h * HEAD_DIM : cols_here + (h + 1) * HEAD_DIM]
            v = low_ref[
                0:keys, 2 * cols_here + h * HEAD_DIM : 2 * cols_here + (h + 1) * HEAD_DIM
            ]
            scores = jnp.where(allowed, dot_nt(q, k) * HEAD_DIM**-0.5, masked_score)
            top = jnp.max(scores, axis=-1, keepdims=True)
            raised = jnp.where(allowed, jnp.exp(scores - top), 0.0)
            share = 1.0 / jnp.sum(raised, axis=-1, keepdims=True)
            out = dot((raised * share).astype(bf16), v)
            att_ref[rows, cols] = out
            per = block // tokens
            att_low[t * per : (t + 1) * per, :, cols] = out.astype(bf16).reshape(
                per, tokens, HEAD_DIM
            )
            stat = jnp.where(lane == 3 + h, top, jnp.where(lane == 5 + h, share, stat))
        stat_ref[rows, :] = stat
        if t % 2:
            tick()
    start(saves[3:])
    home_ref[:, columns(blk)] = att_low[blk]
    start(home_copies)
    tick()
    while ticks[0] < len(streams) - parts + 3:
        tick()
    for stages in for_output:
        stages[4]()
    wo_load.start()
    arrived(home_copies)
    wo_load.wait()
    mid = hrow[blk].astype(f32)
    cut = 512
    for n in range(width // cut):
        cols = slice(n * cut, (n + 1) * cut)
        mid_ref[:, cols] = mid[:, cols] + dot(
            home_ref[...], wo_buf[:, :, :, :, :, cols].reshape(width, cut)
        )
    mid = mid_ref[...]
    expert_ref[...] = (mid * norm_rows(mid) * gains_ref[3:4, :]).astype(bf16)
    while ticks[0] < len(streams) + 3:
        tick()
    for stages in for_upstream:
        stages[4]()
    for cp in col_copies + col_over + col_relay + sum_copies + home_copies:
        cp.wait_send()
    for cp in saves:
        cp.wait()


def front(hidden, wq, wk, wv, wo, upstream, pack, cosine, sine):
    any_, vm = pl.BlockSpec(memory_space=pl.ANY), pl.BlockSpec(memory_space=pltpu.VMEM)
    tokens, width = hidden.shape
    wrows = wq.shape[0]
    seq, cols = 8 * tokens, width // 8
    dma = pltpu.SemaphoreType.DMA
    streams = 4 * (1 + tokens // 64)
    count = 11 + 9 * streams + 13 + 21 + 4 + 14
    shape = jax.ShapeDtypeStruct
    return pl.pallas_call(
        front_kernel,
        out_shape=(
            shape((4, 4, 2, wrows // 16, 16, width), bf16),
            shape((tokens // 16, 4, 4, 2, 16, width), bf16),
            shape((4, 4, 2) + pack.shape, bf16),
            shape((seq, width), bf16),
            shape((4, 8, wrows, 3 * cols), bf16),
            shape((seq, 3 * cols), bf16),
            shape((seq, 2 * cols), f32),
            shape((seq, cols), f32),
            shape((seq, 128), f32),
            shape((tokens, width), bf16),
            shape((tokens, width), f32),
            shape((tokens, width), bf16),
        ),
        in_specs=[any_] * 7 + [vm] * 2,
        out_specs=(any_, any_, vm) + (any_,) * 5 + (vm,) * 4,
        scratch_shapes=[
            pltpu.VMEM((8, tokens, width), bf16),
            pltpu.VMEM((seq, width), bf16),
            pltpu.VMEM((4, 8, wrows, 3 * cols), bf16),
            pltpu.VMEM((seq, 3 * cols), bf16),
            pltpu.VMEM((seq, 2 * cols), f32),
            pltpu.VMEM((seq, cols), f32),
            pltpu.VMEM((4, 4, 2, wrows // 16, 16, width), bf16),
            pltpu.VMEM((8, width), f32),
            pltpu.VMEM((8, seq // 4), f32),
            pltpu.VMEM((7, 8, seq // 4), f32),
            pltpu.VMEM((8, tokens, cols), bf16),
            dma((count,)),
            dma((count,)),
            dma((16 + streams,)),
        ],
        compiler_params=pltpu.CompilerParams(
            collective_id=2, has_side_effects=True, vmem_limit_bytes=56 * 2**20
        ),
        cost_estimate=pl.CostEstimate(
            flops=10**10, bytes_accessed=2 * 10**8, transcendentals=0
        ),
    )(
        hidden,
        wq,
        wk,
        wv,
        wo.reshape(-1, 16, width),
        upstream.reshape(-1, 16, width),
        pack,
        cosine,
        sine,
    )


def added(total, *extra):
    total = total.astype(f32)
    for one in extra:
        total = total + one.astype(f32)
    return total.astype(bf16)


def reduce_stages(copy, src, got, p1a, p1b, p2, land, out):
    row, z, c = place()
    to = partners()
    half = src.shape[-1] // 2

    def own(r):
        return src.at[r, :, c]

    inside = copy(src.at[:, :, 1 - c], got, to["sib"])
    far = [
        copy(own(row ^ 3).at[:, :, pl.ds(0, half)], p1a, to["y"]),
        copy(own(row ^ 3).at[:, :, pl.ds(half, half)], p1b, to["x"]),
    ]
    near = [
        copy(own(row ^ 1), p2.at[0], to["x"]),
        copy(own(row ^ 2), p2.at[1], to["y"]),
    ]
    home = [
        copy(src.at[row, (z + k) % 4, c], land.at[k - 1], to["z%d" % k])
        for k in (1, 3, 2)
    ]

    def first():
        inside.start()

    def second():
        inside.wait_recv()
        for k in (3, 1, 2, 0):
            at = own(row ^ k)
            at[...] = added(at[...], got[row ^ k])
            if k == 3:
                for cp in far:
                    cp.start()

    def third():
        far[0].wait_recv()
        at = own(row ^ 1).at[:, :, pl.ds(0, half)]
        at[...] = added(at[...], p1a[...])
        near[0].start()
        far[1].wait_recv()
        at = own(row ^ 2).at[:, :, pl.ds(half, half)]
        at[...] = added(at[...], p1b[...])
        near[1].start()

    def fourth():
        for cp in near:
            cp.wait_recv()
        at = own(row)
        at[...] = added(at[...], p2[0], p2[1])
        for cp in home:
            cp.start()

    def fifth():
        for cp in home:
            cp.wait_recv()
        total = src[row, z, c].astype(f32)
        for k in range(3):
            total = total + land[k].astype(f32)
        out[...] = total
        for cp in [inside] + far + near + home:
            cp.wait_send()

    return first, second, third, fourth, fifth


def back_kernel(
    ga_home,
    attended_ref,
    proj_ref,
    low_ref,
    pre_ref,
    att_ref,
    stat_ref,
    seg_ref,
    gain_ref,
    cos_ref,
    sin_ref,
    normed_in,
    wcols_in,
    small_ref,
    gn_out,
    q_out,
    k_out,
    v_out,
    wo_out,
    small_out,
    normed_ref,
    wcols,
    ga,
    dq_ref,
    dk_ref,
    dv_ref,
    grads_ref,
    sums_ref,
    sums_land,
    gn,
    gn_sib,
    gn_land,
    gw,
    gw_p1,
    gw_p2,
    gw_land,
    small,
    sm_sib,
    sm_p1a,
    sm_p1b,
    sm_p2,
    sm_land,
    dwo_ref,
    wo_got,
    wo_p1a,
    wo_p1b,
    wo_p2,
    wo_land,
    send,
    recv,
    local_sem,
):
    row, z, c = place()
    blk = z * 2 + c
    to = partners()
    mates = row_mates()
    greet(mates + [to["x"], to["y"]])
    copy = Copies(send, recv)
    tokens, width = ga_home.shape
    seq = 8 * tokens
    cols_here = att_ref.shape[1]
    wrows = wo_out.shape[0]
    scale = HEAD_DIM**-0.5
    block = 256
    blocks = seq // block
    per = block // tokens

    def start(some):
        for cp in some:
            cp.start()

    def arrived(some):
        for cp in some:
            cp.wait_recv()

    def columns(b):
        return pl.ds(pl.multiple_of(b * cols_here, cols_here), cols_here)

    streams = []
    for j in range(wrows // 16):
        part = pl.ds(j * 16, 16)
        streams.append(
            reduce_stages(
                copy,
                dwo_ref.at[:, :, :, part],
                wo_got.at[j],
                wo_p1a.at[j],
                wo_p1b.at[j],
                wo_p2.at[j],
                wo_land.at[j],
                wo_out.at[part],
            )
        )
    ticks = [0]

    def tick():
        t = ticks[0]
        ticks[0] += 1
        for stage in range(5):
            if 0 <= t - stage < len(streams):
                streams[t - stage][stage]()

    own_ga = pltpu.make_async_copy(
        ga_home.at[:, columns(blk)], ga.at[blk], local_sem.at[0]
    )
    ga_copies = [copy(ga_home.at[:, columns(mate[1])], ga.at[blk], mate) for mate in mates]
    sum_copies = [
        copy(sums_ref, sums_land.at[k], mate) for k, mate in enumerate(mates)
    ]
    half = gw.shape[1] // 2
    w_far = [
        copy(gw.at[row ^ 3, pl.ds(0, half)], gw_p1.at[0], to["y"]),
        copy(gw.at[row ^ 3, pl.ds(half, half)], gw_p1.at[1], to["x"]),
    ]
    w_near = [
        copy(gw.at[row ^ 1], gw_p2.at[0], to["x"]),
        copy(gw.at[row ^ 2], gw_p2.at[1], to["y"]),
    ]
    w_home = [copy(gw.at[row, mate[1]], gw_land.at[blk], mate) for mate in mates]
    d0, d1 = 3 - z, (3 * z + 2) % 5
    d2 = 3 - d1
    inner, outer = (z == 1) | (z == 2), (z == 0) | (z == 3)
    n_sib = [
        copy(gn.at[chip, 1 - c], gn_sib.at[chip], to["sib"]) for chip in (d0, d1, d2, z)
    ]
    n_relay = copy(gn.at[d0, c], gn_land.at[0], (row, (1 + z // 2) * 2 + c))
    n_inner = copy(gn.at[d0, c], gn_land.at[1], (row, (2 - z // 2) * 2 + c))
    n_home = [
        copy(gn.at[d1, c], gn_land.at[2], (row, d1 * 2 + c)),
        copy(gn.at[d2, c], gn_land.at[3], (row, d2 * 2 + c)),
    ]
    s_sib = copy(small.at[0], sm_sib, to["sib"])
    s_far = [
        copy(small.at[1, row ^ 3, 0:2], sm_p1a, to["y"]),
        copy(small.at[1, row ^ 3, 2:4], sm_p1b, to["x"]),
    ]
    s_near = [
        copy(small.at[1, row ^ 1], sm_p2.at[0], to["x"]),
        copy(small.at[1, row ^ 2], sm_p2.at[1], to["y"]),
    ]
    s_home = [
        copy(small.at[1, row, (z + k) % 4], sm_land.at[k - 1], to["z%d" % k])
        for k in (1, 3, 2)
    ]

    late = [
        pltpu.make_async_copy(src, dst, local_sem.at[1 + len(streams) + k])
        for k, (src, dst) in enumerate(
            ((normed_in, normed_ref), (wcols_in, wcols))
        )
    ]
    own_ga.start()
    start(ga_copies)
    start(late)

    @pl.loop(0, 8)
    def _(n):
        some = attended_ref[:, pl.ds(pl.multiple_of(n * block, block), block)]
        made = dot_tn(some, proj_ref[...]).astype(bf16)
        dwo_ref[n // 2, pl.ds(2 * (n % 2), 2)] = made.reshape(2, 2, wrows, width)

    tick()
    dk_ref[...] = jnp.zeros_like(dk_ref)
    dv_ref[...] = jnp.zeros_like(dv_ref)
    small[0] = small_ref[...]
    own_ga.wait()
    arrived(ga_copies)

    segments = seg_ref[0:1, :]
    for t in range(blocks):
        rows = slice(t * block, (t + 1) * block)
        keys = (t + 1) * block
        stat = stat_ref[rows, :]
        place_q = lax.broadcasted_iota(jnp.int32, (block, keys), 0) + t * block
        place_k = lax.broadcasted_iota(jnp.int32, (block, keys), 1)
        allowed = (place_k <= place_q) & (segments[:, :keys] == stat[:, 2:3])
        for h in range(cols_here // HEAD_DIM):
            cols = slice(h * HEAD_DIM, (h + 1) * HEAD_DIM)
            q = low_ref[rows, cols]
            k = low_ref[0:keys, cols_here + h * HEAD_DIM : cols_here + (h + 1) * HEAD_DIM]
            v = low_ref[
                0:keys, 2 * cols_here + h * HEAD_DIM : 2 * cols_here + (h + 1) * HEAD_DIM
            ]
            g = ga[t * per : (t + 1) * per, :, cols].reshape(block, HEAD_DIM)
            scores = jnp.where(allowed, dot_nt(q, k) * scale, masked_score)
            raised = jnp.exp(scores - stat[:, 3 + h : 4 + h])
            probs = jnp.where(allowed, raised, 0.0) * stat[:, 5 + h : 6 + h]
            delta = jnp.sum(g.astype(f32) * att_ref[rows, cols], axis=-1, keepdims=True)
            ds = (probs * (dot_nt(g, v) - delta)).astype(bf16)
            dq_ref[rows, cols] = dot(ds, k) * scale
            dk_ref[0:keys, cols] += dot_tn(ds, q) * scale
            dv_ref[0:keys, cols] += dot_tn(probs.astype(bf16), g)
        tick()

    pairs = row_pairs(cols_here)
    gain_q, gain_k = gain_ref[0:1, :], gain_ref[1:2, :]
    for_q = jnp.zeros((1, cols_here), f32)
    for_k = jnp.zeros((1, cols_here), f32)
    for t in range(blocks):
        rows = slice(t * block, (t + 1) * block)
        cosine, sine = cos_ref[rows, :], -sin_ref[rows, :]
        q_pre, k_pre = pre_ref[rows, :cols_here], pre_ref[rows, cols_here:]
        dq = turned(dq_ref[rows, :], cosine, sine)
        dk = turned(dk_ref[rows, :], cosine, sine)
        dq_ref[rows, :] = dq
        dk_ref[rows, :] = dk
        vq, vk = dq * q_pre, dk * k_pre
        for_q = for_q + jnp.sum(vq * stat_ref[rows, 0:1], axis=0, keepdims=True)
        for_k = for_k + jnp.sum(vk * stat_ref[rows, 1:2], axis=0, keepdims=True)
        sums = sums_by_row(pairs, jnp.concatenate([vq * gain_q, vk * gain_k], axis=1))
        sums_ref[2 * t : 2 * t + 2, :] = sums[0:2]
    start(sum_copies)
    tick()
    total = sums_ref[...]
    for k, cp in enumerate(sum_copies):
        cp.wait_recv()
        total = total + sums_land[k]
    means = total * (1.0 / width)
    for t in range(blocks):
        rows = slice(t * block, (t + 1) * block)
        mean = jnp.concatenate(
            [means[2 * t : 2 * t + 2], jnp.zeros((6, block), f32)], axis=0
        ).T
        for j, (d_ref, gain) in enumerate(((dq_ref, gain_q), (dk_ref, gain_k))):
            cols = slice(j * cols_here, (j + 1) * cols_here)
            r = stat_ref[rows, j : j + 1]
            grads_ref[rows, cols] = (
                r * gain * d_ref[rows, :]
                - pre_ref[rows, cols] * (r * r * r) * mean[:, j : j + 1]
            ).astype(bf16)
        grads_ref[rows, 2 * cols_here :] = dv_ref[rows, :].astype(bf16)

    deep = 8 * wrows
    for cp in late:
        cp.wait()

    def weight_rows(k):
        there = row ^ k
        some = normed_ref[:, pl.ds(pl.multiple_of(there * deep, deep), deep)]
        gw[there] = (
            dot_tn(some, grads_ref[...]).astype(bf16).reshape(8, wrows, 3 * cols_here)
        )

    weight_rows(3)
    start(w_far)
    weights = wcols[...].reshape(width, 3 * cols_here)
    for_attn = jnp.zeros((1, width), f32)
    chips = (d0, d1, d2, z)
    for n, chip in enumerate(chips):
        tok = pl.ds(pl.multiple_of(chip * block, block), block)
        made = dot_nt(grads_ref[tok, :], weights)
        gn[chip] = made.astype(bf16).reshape(per, tokens, width)
        n_sib[n].start()
        for_attn = for_attn + jnp.sum(
            made * normed_ref[tok, :].astype(f32), axis=0, keepdims=True
        )
        if n:
            before = chips[n - 1]
            n_sib[n - 1].wait_recv()
            n_sib[n - 1].wait_send()
            gn[before, c] = added(gn[before, c], gn_sib[before])
            if n == 1:
                pl.when(outer)(n_relay.start)
                pl.when(inner)(n_inner.start)
            elif n == 2:
                n_home[0].start()
    weight_rows(1)
    weight_rows(2)

    @pl.when(inner)
    def _():
        n_relay.wait_recv()
        gn[d2, c] = added(gn[d2, c], gn_land[0])

    n_home[1].start()
    weight_rows(0)
    tick()
    for r in range(4):
        for q in range(4):
            at = (r * 4 + q) * 128
            small[0, r, q, 16:17, :] = for_attn[:, at : at + 128]
    for j in range(cols_here // 128):
        at = blk * (cols_here // 128) + j
        small[0, at // 4, at % 4, 17:18, :] = for_q[:, j * 128 : (j + 1) * 128]
        small[0, at // 4, at % 4, 18:19, :] = for_k[:, j * 128 : (j + 1) * 128]
    s_sib.start()

    arrived(w_far[:1])
    gw[row ^ 1, 0:half] = added(gw[row ^ 1, 0:half], gw_p1[0])
    w_near[0].start()
    arrived(w_far[1:])
    gw[row ^ 2, half:] = added(gw[row ^ 2, half:], gw_p1[1])
    w_near[1].start()
    s_sib.wait_recv()
    small[1] = small[0] + sm_sib[...]
    start(s_far)
    tick()
    arrived(s_far)
    small[1, row ^ 1, 0:2] = small[1, row ^ 1, 0:2] + sm_p1a[...]
    small[1, row ^ 2, 2:4] = small[1, row ^ 2, 2:4] + sm_p1b[...]
    start(s_near)
    arrived(w_near)
    for b in range(8):
        gw[row, b] = added(gw[row, b], gw_p2[0, b], gw_p2[1, b])
    start(w_home)
    arrived(s_near)
    small[1, row] = small[1, row] + sm_p2[0] + sm_p2[1]
    start(s_home)
    while ticks[0] < len(streams) + 4:
        tick()

    n_sib[3].wait_recv()
    gn_out[...] = gn[z, c].astype(f32) + gn_sib[z].astype(f32)
    arrived(n_home)
    gn_out[...] += gn_land[2].astype(f32) + gn_land[3].astype(f32)

    @pl.when(inner)
    def _():
        n_inner.wait_recv()
        n_inner.wait_send()
        gn_out[...] += gn_land[1].astype(f32)

    @pl.when(outer)
    def _():
        n_relay.wait_send()

    arrived(s_home)
    small_out[...] = small[1, row, z] + sm_land[0] + sm_land[1] + sm_land[2]
    gw_land[blk] = gw[row, blk]
    arrived(w_home)
    for b in range(8):
        for j, out in enumerate((q_out, k_out, v_out)):
            out[:, b * cols_here : (b + 1) * cols_here] = gw_land[
                b, :, j * cols_here : (j + 1) * cols_here
            ].astype(f32)
    n_sib[3].wait_send()
    for cp in ga_copies + sum_copies + w_far + w_near + w_home + n_home:
        cp.wait_send()
    for cp in [s_sib] + s_far + s_near + s_home:
        cp.wait_send()


def back(ga, att_low, proj, low, pre, att, stat, seg, gain, cosine, sine, normed, wcols, small):
    any_, vm = pl.BlockSpec(memory_space=pl.ANY), pl.BlockSpec(memory_space=pltpu.VMEM)
    tokens, width = ga.shape
    seq, cols = 8 * tokens, width // 8
    wrows = wcols.shape[2]
    fields = small.shape[2:]
    dma = pltpu.SemaphoreType.DMA
    streams = wrows // 16
    count = 8 * streams + 7 + 7 + 2 + 2 + 7 + 4 + 4 + 1 + 2 + 2 + 3
    shape, vmem = jax.ShapeDtypeStruct, pltpu.VMEM
    weight = shape((wrows, width), f32)
    return pl.pallas_call(
        back_kernel,
        out_shape=(
            shape((tokens, width), f32),
            weight,
            weight,
            weight,
            weight,
            shape(fields, f32),
        ),
        in_specs=[any_] + [vm] * 10 + [any_] * 2 + [vm],
        out_specs=(vm,) * 6,
        scratch_shapes=[
            vmem((seq, width), bf16),
            vmem((4, 8, wrows, 3 * cols), bf16),
            vmem((8, tokens, cols), bf16),
            vmem((seq, cols), f32),
            vmem((seq, cols), f32),
            vmem((seq, cols), f32),
            vmem((seq, 3 * cols), bf16),
            vmem((8, seq // 4), f32),
            vmem((7, 8, seq // 4), f32),
            vmem((4, 2, tokens, width), bf16),
            vmem((4, tokens, width), bf16),
            vmem((4, tokens, width), bf16),
            vmem((4, 8, wrows, 3 * cols), bf16),
            vmem((2, 4, wrows, 3 * cols), bf16),
            vmem((2, 8, wrows, 3 * cols), bf16),
            vmem((8, wrows, 3 * cols), bf16),
            vmem((2, 4, 4) + fields, f32),
            vmem((4, 4) + fields, f32),
            vmem((2,) + fields, f32),
            vmem((2,) + fields, f32),
            vmem((2, 4) + fields, f32),
            vmem((3,) + fields, f32),
            vmem((4, 4, 2, wrows, width), bf16),
            vmem((streams, 4, 4, 16, width), bf16),
            vmem((streams, 4, 16, width // 2), bf16),
            vmem((streams, 4, 16, width // 2), bf16),
            vmem((streams, 2, 4, 16, width), bf16),
            vmem((streams, 3, 16, width), bf16),
            dma((count,)),
            dma((count,)),
            dma((4 + streams,)),
        ],
        compiler_params=pltpu.CompilerParams(
            collective_id=7, has_side_effects=True, vmem_limit_bytes=60 * 2**20
        ),
        cost_estimate=pl.CostEstimate(
            flops=10**10, bytes_accessed=2 * 10**8, transcendentals=0
        ),
    )(
        ga,
        att_low,
        proj,
        low,
        pre,
        att,
        stat,
        seg,
        gain,
        cosine,
        sine,
        normed,
        wcols,
        small,
    )


def rope_tables(count):
    half = HEAD_DIM // 2
    frequency = jnp.exp(
        -math.log(10000.0) * 2.0 * jnp.arange(half, dtype=f32) / HEAD_DIM
    )
    angles = jnp.arange(count, dtype=f32)[:, None] * frequency[None, :]
    return jnp.cos(angles), jnp.sin(angles)


def rope(values, cosine, sine):
    half = HEAD_DIM // 2
    a, b = values[..., :half], values[..., half:]
    return jnp.concatenate([a * cosine - b * sine, b * cosine + a * sine], axis=-1)


def norm_back(v, r, g, c, mean_vgc):
    return r * g * c - v * (r * r * r) * mean_vgc


def experts_by_scan(expert_in, upstream, gates, gate_local, up_local, down_local):
    tokens, width = expert_in.shape
    experts = gates.shape[1]
    rows, blocks = lax.axis_size("row"), lax.axis_size("blk")
    devices = rows * blocks
    me = lax.axis_index("row") * blocks + lax.axis_index("blk")
    parts = devices * tokens // 2048
    step = tokens // parts
    all_gates = lax.all_gather(gates, BOTH, axis=0, tiled=False)
    own_gate = jnp.sum(
        jnp.where(
            jnp.arange(experts, dtype=jnp.int32)[None, None, :] == me // 2,
            all_gates,
            0.0,
        ),
        axis=-1,
    )

    def expert_part(sums, items):
        own_rows, own_upstream, gate_col = items
        got = lax.all_gather(own_rows, BOTH, axis=0, tiled=True)
        up_stream = lax.all_gather(own_upstream, BOTH, axis=0, tiled=True)
        gate_col = gate_col.reshape(devices * step, 1)
        gate_pre = dot(got, gate_local)
        up_pre = dot(got, up_local)
        sig = jax.nn.sigmoid(gate_pre)
        silu = gate_pre * sig
        hidden = (silu * up_pre).astype(bf16)
        part_f = dot(hidden, down_local).astype(bf16).astype(f32)
        up_f = up_stream.astype(f32)
        dots = jnp.sum(part_f * up_f, axis=-1).reshape(devices, step)
        mixed = (gate_col * part_f).astype(bf16)
        out = lax.psum_scatter(mixed, BOTH, scatter_dimension=0, tiled=True)
        grad_part = (gate_col * up_f).astype(bf16)
        grad_hidden = dot_nt(grad_part, down_local)
        grad_gate_pre = (
            grad_hidden * up_pre * sig * (1.0 + gate_pre * (1.0 - sig))
        ).astype(bf16)
        grad_up_pre = (grad_hidden * silu).astype(bf16)
        grad_rows = (
            dot_nt(grad_gate_pre, gate_local) + dot_nt(grad_up_pre, up_local)
        ).astype(bf16)
        back = lax.psum_scatter(grad_rows, BOTH, scatter_dimension=0, tiled=True)
        sums = (
            sums[0] + dot_tn(got, grad_gate_pre),
            sums[1] + dot_tn(got, grad_up_pre),
            sums[2] + dot_tn(hidden, grad_part),
        )
        return sums, (out, back, dots)

    sums = (
        jnp.zeros(gate_local.shape, f32),
        jnp.zeros(up_local.shape, f32),
        jnp.zeros(down_local.shape, f32),
    )
    items = (
        expert_in.reshape(parts, step, width),
        upstream.reshape(parts, step, width),
        own_gate.reshape(devices, parts, step).transpose(1, 0, 2),
    )
    if parts > 2:
        sums, (outs, backs, dots) = lax.scan(expert_part, sums, items)
    else:
        made = []
        for part in range(parts):
            sums, result = expert_part(sums, tuple(item[part] for item in items))
            made.append(result)
        outs, backs, dots = (jnp.stack(some) for some in zip(*made))
    dots = dots.transpose(1, 0, 2).reshape(devices, tokens)
    outs = outs.reshape(tokens, width)
    backs = backs.reshape(tokens, width)
    dots = lax.all_to_all(dots, BOTH, split_axis=0, concat_axis=0, tiled=True)
    grad_gates = jnp.sum(dots.reshape(experts, 2, tokens), axis=1).T
    return outs.astype(f32), backs.astype(f32), grad_gates, sums


def own_mesh_body(
    hidden_in,
    segment_ids,
    expert_ids,
    attention_gain,
    query_gain,
    key_gain,
    expert_gain,
    query_weight,
    key_weight,
    value_weight,
    output_weight,
    router_weight,
    gate_weight,
    up_weight,
    down_weight,
    grad_out,
):
    tokens, width = hidden_in.shape[1:]
    wrows = query_weight.shape[0]
    experts = router_weight.shape[1]
    blocks = lax.axis_size("blk")
    seq = tokens * blocks
    head_cols = width // blocks
    blk = lax.axis_index("blk")
    upstream_low = grad_out[0]

    experts_in_order = jnp.arange(experts, dtype=jnp.int32)
    routed = jnp.any(
        expert_ids[0][:, :, None] == experts_in_order[None, None, :], axis=1
    )
    routed_t = jnp.any(
        expert_ids[0].T[None, :, :] == experts_in_order[:, None, None], axis=1
    )
    gains = jnp.stack([attention_gain, query_gain, key_gain, expert_gain])
    spare = tokens - wrows
    gains = jnp.concatenate([gains, gains], axis=1)
    lane = jnp.arange(2 * wrows, dtype=jnp.int32)[None]
    gains = jnp.where(lane // wrows == blk % 2, gains, 0)

    def rows_at(first, values, lanes):
        return jnp.pad(values.astype(f32), ((first, 64 - first - values.shape[0]), (0, lanes)))

    pack = (
        rows_at(0, routed_t, 0)
        + rows_at(16, segment_ids, 0)
        + rows_at(32, router_weight.T, spare)
        + rows_at(32 + experts, gains, 0)
    ).astype(bf16)
    cosine, sine = rope_tables(seq)
    cosine = jnp.concatenate([cosine, cosine], axis=1)
    sine = jnp.concatenate([-sine, sine], axis=1)
    (
        full_output,
        upstream_all,
        packs,
        normed_row,
        qkv_cols,
        low,
        pre,
        attended,
        stats,
        attended_low,
        residual_mid,
        expert_in,
    ) = front(
        hidden_in[0],
        query_weight,
        key_weight,
        value_weight,
        output_weight,
        upstream_low,
        pack,
        cosine,
        sine,
    )
    full_output = full_output.reshape(width, width)
    packs = packs.reshape(-1, pack.shape[0], tokens)
    router = packs[:, 32 : 32 + experts, :wrows].transpose(0, 2, 1).reshape(width, -1)
    gains = packs[:, 32 + experts : 36 + experts].reshape(-1, 2, 4, tokens).sum(axis=1)
    gains = gains.transpose(1, 0, 2).reshape(4, width).astype(f32)
    gain_attn, gain_expert = gains[0], gains[3]
    own_q_gain = lax.dynamic_slice_in_dim(gains[1], blk * head_cols, head_cols)
    own_k_gain = lax.dynamic_slice_in_dim(gains[2], blk * head_cols, head_cols)
    steps = tokens // 16
    mask = packs[:, :experts].astype(f32).reshape(-1, experts, steps, 16)
    mask = mask.transpose(2, 0, 3, 1).reshape(steps, -1, experts)
    x = hidden_in[0].astype(f32)
    r_attn = lax.rsqrt(jnp.mean(x * x, axis=-1, keepdims=True) + epsilon)
    r_exp = lax.rsqrt(
        jnp.mean(residual_mid * residual_mid, axis=-1, keepdims=True) + epsilon
    )
    logits = dot(expert_in, router)
    top_logit = jnp.max(
        jnp.where(routed, logits, masked_score), axis=-1, keepdims=True
    )
    gates = jnp.where(routed, jnp.exp(logits - top_logit), 0.0)
    gates = gates / jnp.sum(gates, axis=-1, keepdims=True)

    outs, backs, grad_gate_local, grad_up_local, grad_down_local = moe(
        expert_in,
        upstream_all,
        mask,
        router,
        gate_weight[0],
        up_weight[0],
        down_weight[0],
    )
    outs = outs.reshape(tokens, width)
    backs = backs.reshape(tokens, width + EXTRA)
    dots = backs[:, width : width + 2 * experts]
    dots = dots + backs[:, width + 64 : width + 64 + 2 * experts]
    grad_gates = jnp.sum(dots.reshape(tokens, experts, 2), axis=2)
    layer_out = (residual_mid + outs).astype(bf16)
    upstream = upstream_low.astype(f32)
    grad_picked = gates * (
        grad_gates - jnp.sum(gates * grad_gates, axis=-1, keepdims=True)
    )
    grad_logits = jnp.where(routed, grad_picked, 0.0).astype(bf16)
    grad_expert_in = backs[:, :width] + dot_nt(grad_logits, router)
    grad_router = dot_tn(grad_logits, expert_in)
    grad_gain_expert = jnp.sum(grad_expert_in * residual_mid * r_exp, axis=0)
    grad_mid = upstream + norm_back(
        residual_mid,
        r_exp,
        gain_expert,
        grad_expert_in,
        jnp.mean(residual_mid * gain_expert * grad_expert_in, axis=-1, keepdims=True),
    )
    grad_proj = grad_mid.astype(bf16)
    grad_attended = dot_nt(grad_proj, full_output).astype(bf16)
    small = jnp.concatenate(
        [
            grad_router,
            jnp.zeros((3, width), f32),
            grad_gain_expert[None],
            jnp.zeros((20 - experts, width), f32),
        ],
        axis=0,
    )
    fields = small.shape[0]
    small = small.reshape(fields, 4, 4, 2 * wrows).transpose(1, 2, 0, 3)
    grad_normed, grad_q, grad_k, grad_v, grad_output_w, small = back(
        grad_attended,
        attended_low,
        grad_proj,
        low,
        pre,
        attended,
        stats,
        jnp.broadcast_to(stats[:, 2][None], (8, seq)),
        jnp.concatenate(
            [own_q_gain[None], own_k_gain[None], jnp.zeros((6, head_cols), f32)], axis=0
        ),
        cosine,
        sine,
        normed_row,
        qkv_cols,
        small,
    )
    input_grad = grad_mid + norm_back(
        x,
        r_attn,
        gain_attn,
        grad_normed,
        jnp.mean(x * gain_attn * grad_normed, axis=-1, keepdims=True),
    )
    small = lax.dynamic_slice_in_dim(small, (blk % 2) * wrows, wrows, axis=1)
    return (
        layer_out[None],
        input_grad[None],
        small[experts] / attention_gain.astype(f32),
        small[experts + 1],
        small[experts + 2],
        small[experts + 3],
        grad_q,
        grad_k,
        grad_v,
        grad_output_w,
        small[:experts].T,
        grad_gate_local[None],
        grad_up_local[None],
        grad_down_local[None],
    )


def any_mesh_body(
    hidden_in,
    segment_ids,
    expert_ids,
    attention_gain,
    query_gain,
    key_gain,
    expert_gain,
    query_weight,
    key_weight,
    value_weight,
    output_weight,
    router_weight,
    gate_weight,
    up_weight,
    down_weight,
    grad_out,
):
    tokens = hidden_in.shape[1]
    width = hidden_in.shape[2]
    experts = router_weight.shape[1]
    rows, blocks = lax.axis_size("row"), lax.axis_size("blk")
    devices = rows * blocks
    seq = tokens * blocks
    head_cols = width // blocks
    heads_here = HEADS // blocks
    blk = lax.axis_index("blk")
    me = lax.axis_index("row") * blocks + blk
    scale = HEAD_DIM**-0.5

    small = jnp.concatenate(
        [
            router_weight,
            attention_gain[:, None],
            query_gain[:, None],
            key_gain[:, None],
            expert_gain[:, None],
        ],
        axis=1,
    )
    small = lax.all_gather(small, BOTH, axis=0, tiled=True)
    router = small[:, :experts]
    gains = small[:, experts:].astype(f32)
    gain_attn, gain_expert = gains[:, 0], gains[:, 3]
    own_q_gain = lax.dynamic_slice_in_dim(gains[:, 1], blk * head_cols, head_cols)
    own_k_gain = lax.dynamic_slice_in_dim(gains[:, 2], blk * head_cols, head_cols)

    x = hidden_in[0].astype(f32)
    r_attn = lax.rsqrt(jnp.mean(x * x, axis=-1, keepdims=True) + epsilon)
    normed = (x * r_attn * gain_attn).astype(bf16)
    normed_row = lax.all_gather(normed, "blk", axis=0, tiled=True)
    segments = lax.all_gather(segment_ids[0], "blk", axis=0, tiled=True)

    stacked = jnp.stack([query_weight, key_weight, value_weight], axis=0)
    wrows = stacked.shape[1]
    stacked = stacked.reshape(3, wrows, blocks, head_cols).transpose(2, 1, 0, 3)
    stacked = stacked.reshape(blocks, wrows, 3 * head_cols)
    cols = lax.all_to_all(stacked, "blk", split_axis=0, concat_axis=0, tiled=True)
    cols = cols.reshape(blocks * wrows, 3 * head_cols)
    qkv_cols = lax.all_gather(cols, "row", axis=0, tiled=True)
    full_output = lax.all_gather(output_weight, BOTH, axis=0, tiled=True)

    qkv = dot(normed_row, qkv_cols)
    query_pre = qkv[:, :head_cols]
    key_pre = qkv[:, head_cols : 2 * head_cols]
    value = qkv[:, 2 * head_cols :].astype(bf16)
    squares = jnp.stack(
        [jnp.sum(query_pre * query_pre, axis=-1), jnp.sum(key_pre * key_pre, axis=-1)]
    )
    squares = lax.psum(squares, "blk") / width
    r_q = lax.rsqrt(squares[0] + epsilon)[:, None]
    r_k = lax.rsqrt(squares[1] + epsilon)[:, None]
    cosine, sine = (table[:, None] for table in rope_tables(seq))

    def heads(v):
        return v.reshape(seq, heads_here, HEAD_DIM)

    query = rope(heads(query_pre * r_q * own_q_gain), cosine, sine).astype(bf16)
    key = rope(heads(key_pre * r_k * own_k_gain), cosine, sine).astype(bf16)
    value = heads(value)
    places = jnp.arange(seq, dtype=jnp.int32)
    allowed = (places[None, :] <= places[:, None]) & (
        segments[None, :] == segments[:, None]
    )
    scores = jnp.einsum("qhd,khd->hqk", query, key, preferred_element_type=f32) * scale
    scores = jnp.where(allowed[None], scores, masked_score)
    top = jnp.max(scores, axis=-1, keepdims=True)
    weights = jnp.where(allowed[None], jnp.exp(scores - top), 0.0)
    total = jnp.sum(weights, axis=-1, keepdims=True)
    probs = weights / total
    probs_low = probs.astype(bf16)
    attended = jnp.einsum("hqk,khd->qhd", probs_low, value, preferred_element_type=f32)
    attended_low_cols = attended.astype(bf16).reshape(blocks, tokens, head_cols)
    attended_low = lax.all_to_all(
        attended_low_cols, "blk", split_axis=0, concat_axis=0, tiled=True
    )
    attended_low = attended_low.transpose(1, 0, 2).reshape(tokens, width)

    residual_mid = x + dot(attended_low, full_output)
    r_exp = lax.rsqrt(
        jnp.mean(residual_mid * residual_mid, axis=-1, keepdims=True) + epsilon
    )
    expert_in = (residual_mid * r_exp * gain_expert).astype(bf16)
    logits = dot(expert_in, router)
    routes = expert_ids[0]
    routed = jnp.any(
        routes[:, :, None] == jnp.arange(experts, dtype=jnp.int32)[None, None, :],
        axis=1,
    )
    top_logit = jnp.max(
        jnp.where(routed, logits, masked_score), axis=-1, keepdims=True
    )
    gates = jnp.where(routed, jnp.exp(logits - top_logit), 0.0)
    gates = gates / jnp.sum(gates, axis=-1, keepdims=True)

    gate_local, up_local, down_local = gate_weight[0], up_weight[0], down_weight[0]
    outs, backs, grad_gates, sums = experts_by_scan(
        expert_in, grad_out[0], gates, gate_local, up_local, down_local
    )
    grad_gate_local, grad_up_local, grad_down_local = sums
    layer_out = (residual_mid + outs).astype(bf16)
    upstream = grad_out[0].astype(f32)
    grad_picked = gates * (
        grad_gates - jnp.sum(gates * grad_gates, axis=-1, keepdims=True)
    )
    grad_logits = jnp.where(routed, grad_picked, 0.0).astype(bf16)
    grad_expert_in = backs + dot_nt(
        grad_logits, router
    )
    grad_router = dot_tn(expert_in, grad_logits)
    grad_gain_expert = jnp.sum(grad_expert_in * residual_mid * r_exp, axis=0)
    grad_mid = upstream + norm_back(
        residual_mid,
        r_exp,
        gain_expert,
        grad_expert_in,
        jnp.mean(residual_mid * gain_expert * grad_expert_in, axis=-1, keepdims=True),
    )
    grad_proj = grad_mid.astype(bf16)
    grad_output_w = dot_tn(attended_low, grad_proj).astype(bf16)
    grad_output_w = lax.psum_scatter(
        grad_output_w, BOTH, scatter_dimension=0, tiled=True
    ).astype(f32)
    grad_attended = dot_nt(grad_proj, full_output).astype(bf16)
    grad_attended = grad_attended.reshape(tokens, blocks, head_cols).transpose(1, 0, 2)
    grad_attended = lax.all_to_all(
        grad_attended, "blk", split_axis=0, concat_axis=0, tiled=True
    )
    grad_attended = grad_attended.reshape(seq, heads_here, HEAD_DIM)
    row_delta = jnp.sum(grad_attended.astype(f32) * attended, axis=-1).T
    grad_probs = jnp.einsum(
        "qhd,khd->hqk", grad_attended, value, preferred_element_type=f32
    )
    grad_scores = (probs * (grad_probs - row_delta[:, :, None])).astype(bf16)
    grad_value = jnp.einsum(
        "hqk,qhd->khd", probs_low, grad_attended, preferred_element_type=f32
    ).astype(bf16)
    grad_query = (
        jnp.einsum("hqk,khd->qhd", grad_scores, key, preferred_element_type=f32) * scale
    )
    grad_key = (
        jnp.einsum("hqk,qhd->khd", grad_scores, query, preferred_element_type=f32)
        * scale
    )
    grad_query = rope(grad_query, cosine, -sine).reshape(seq, head_cols)
    grad_key = rope(grad_key, cosine, -sine).reshape(seq, head_cols)
    means = jnp.stack(
        [
            jnp.sum(query_pre * own_q_gain * grad_query, axis=-1),
            jnp.sum(key_pre * own_k_gain * grad_key, axis=-1),
        ]
    )
    means = lax.psum(means, "blk") / width
    grad_q_gain = jnp.sum(grad_query * query_pre * r_q, axis=0)
    grad_k_gain = jnp.sum(grad_key * key_pre * r_k, axis=0)
    grad_query_pre = norm_back(query_pre, r_q, own_q_gain, grad_query, means[0][:, None])
    grad_key_pre = norm_back(key_pre, r_k, own_k_gain, grad_key, means[1][:, None])
    grad_qkv = jnp.concatenate(
        [
            grad_query_pre.astype(bf16),
            grad_key_pre.astype(bf16),
            grad_value.reshape(seq, head_cols),
        ],
        axis=1,
    )
    grad_w = dot_tn(normed_row, grad_qkv).astype(bf16)
    grad_w = lax.psum_scatter(grad_w, "row", scatter_dimension=0, tiled=True)
    grad_w = grad_w.reshape(blocks, wrows, 3 * head_cols)
    grad_w = lax.all_to_all(grad_w, "blk", split_axis=0, concat_axis=0, tiled=True)
    grad_w = grad_w.reshape(blocks, wrows, 3, head_cols).transpose(2, 1, 0, 3)
    grad_w = grad_w.reshape(3, wrows, width).astype(f32)
    grad_normed = dot_nt(grad_qkv, qkv_cols).astype(bf16)
    grad_normed = lax.psum_scatter(
        grad_normed, "blk", scatter_dimension=0, tiled=True
    ).astype(f32)
    grad_gain_attn = jnp.sum(grad_normed * x * r_attn, axis=0)
    input_grad = grad_mid + norm_back(
        x,
        r_attn,
        gain_attn,
        grad_normed,
        jnp.mean(x * gain_attn * grad_normed, axis=-1, keepdims=True),
    )

    def placed(vector):
        return lax.dynamic_update_slice_in_dim(
            jnp.zeros((width,), f32), vector, blk * head_cols, axis=0
        )

    small_grads = jnp.concatenate(
        [
            grad_router,
            grad_gain_attn[:, None],
            placed(grad_q_gain)[:, None],
            placed(grad_k_gain)[:, None],
            grad_gain_expert[:, None],
        ],
        axis=1,
    )
    small_grads = lax.psum_scatter(small_grads, BOTH, scatter_dimension=0, tiled=True)
    return (
        layer_out[None],
        input_grad[None],
        small_grads[:, experts],
        small_grads[:, experts + 1],
        small_grads[:, experts + 2],
        small_grads[:, experts + 3],
        grad_w[0],
        grad_w[1],
        grad_w[2],
        grad_output_w,
        small_grads[:, :experts],
        grad_gate_local[None],
        grad_up_local[None],
        grad_down_local[None],
    )


def solution(mesh):
    tokens3 = P("row", "blk", None)
    vector, matrix, cube = P(BOTH), P(BOTH, None), P(BOTH, None, None)
    own = (mesh.shape["row"], mesh.shape["blk"]) == (4, 8)
    return jax.shard_map(
        own_mesh_body if own else any_mesh_body,
        mesh=mesh,
        in_specs=(
            tokens3,
            P("row", "blk"),
            tokens3,
            vector,
            vector,
            vector,
            vector,
            matrix,
            matrix,
            matrix,
            matrix,
            matrix,
            cube,
            cube,
            cube,
            tokens3,
        ),
        out_specs=(
            tokens3,
            tokens3,
            vector,
            vector,
            vector,
            vector,
            matrix,
            matrix,
            matrix,
            matrix,
            matrix,
            cube,
            cube,
            cube,
        ),
        check_vma=False,
    )
```

```python
import functools
import math

import jax
import jax.numpy as jnp
from jax import lax
from jax.experimental import pallas as pl
from jax.experimental.pallas import tpu as pltpu
from jax.sharding import PartitionSpec as P

HEADS = 16
HEAD_DIM = 128
TOP_K = 8

epsilon = 1e-05
masked_score = -1e30
BOTH = ("row", "blk")
MESH = pl.DeviceIdType.MESH
bf16 = jnp.bfloat16
f32 = jnp.float32
EXTRA = 128
ZCOLS = 256


def dot(a, b):
    return jnp.dot(a, b, preferred_element_type=f32)


def dot_nt(a, b):
    return lax.dot_general(a, b, (((1,), (1,)), ((), ())), preferred_element_type=f32)


def dot_tn(a, b):
    return lax.dot_general(a, b, (((0,), (0,)), ((), ())), preferred_element_type=f32)


def place():
    row, blk = lax.axis_index("row"), lax.axis_index("blk")
    return row, blk // 2, blk % 2


def partners():
    row, z, c = place()
    blk = z * 2 + c
    return {
        "sib": (row, z * 2 + (1 - c)),
        "x": (row ^ 1, blk),
        "y": (row ^ 2, blk),
        "z1": (row, ((z + 1) % 4) * 2 + c),
        "z2": (row, ((z + 2) % 4) * 2 + c),
        "z3": (row, ((z + 3) % 4) * 2 + c),
    }


def remote(src, dst, send, recv, to):
    return pltpu.make_async_remote_copy(
        src_ref=src,
        dst_ref=dst,
        send_sem=send,
        recv_sem=recv,
        device_id=to,
        device_id_type=MESH,
    )


def greet(targets):
    barrier = pltpu.get_barrier_semaphore()
    for to in targets:
        pl.semaphore_signal(barrier, inc=1, device_id=to, device_id_type=MESH)
    pl.semaphore_wait(barrier, len(targets))


def moe_kernel(
    steps,
    x_ref,
    c_ref,
    mask_ref,
    router_ref,
    gate_ref,
    up_ref,
    down_ref,
    xall,
    out_ref,
    back_ref,
    dwg_out,
    dwu_out,
    dwd_out,
    wgu_ref,
    wd_ref,
    dwg_ref,
    dwu_ref,
    dwd_ref,
    xbuf,
    cbuf,
    hbuf,
    gbuf,
    po,
    pb,
    ro,
    rb,
    so,
    sb,
    p1ao,
    p1bo,
    p1ab,
    p1bb,
    p2o,
    p2b,
    zo,
    zb,
    gz,
    gp1,
    gp2,
    ag_send,
    ag_recv,
    rs_send,
    rs_recv,
    load_sem,
    weight_sem,
):
    row, z, c = place()
    to = partners()
    width = x_ref.shape[-1]
    half = width // 2
    hidden = wd_ref.shape[0]
    me = row * 8 + z * 2 + c
    expert = me // 2

    weights = [
        pltpu.make_async_copy(src, dst, weight_sem.at[k])
        for k, (src, dst) in enumerate(
            (
                (gate_ref, wgu_ref.at[:, pl.ds(0, hidden)]),
                (up_ref, wgu_ref.at[:, pl.ds(hidden, hidden)]),
                (down_ref, wd_ref),
            )
        )
    ]
    sums = [
        pltpu.make_async_copy(src, dst, weight_sem.at[3 + k])
        for k, (src, dst) in enumerate(
            ((dwg_ref, dwg_out), (dwu_ref, dwu_out), (dwd_ref, dwd_out))
        )
    ]
    for cp in weights:
        cp.start()
    greet(list(to.values()))

    def ag(j, k, src, dst, who):
        return remote(src, dst, ag_send.at[j, k], ag_recv.at[j, k], to[who])

    def own_copy(j):
        return pltpu.make_async_copy(
            x_ref.at[j], xall.at[j, row, z, c], load_sem.at[2 + j % 4]
        )

    def z_copies(j):
        slot = xall.at[j, row, z, c]
        return [ag(j, k, x_ref.at[j], slot, "z%d" % (k + 1)) for k in range(3)]

    def line_copies(j):
        line = xall.at[j, row, :, c]
        return [
            ag(j, 3, line, line, "x"),
            ag(j, 4, line, line, "y"),
            ag(j, 5, line, line, "sib"),
        ]

    def relay_copies(j):
        a = xall.at[j, row ^ 1, :, c, :, pl.ds(0, half)]
        b = xall.at[j, row ^ 2, :, c, :, pl.ds(half, half)]
        s1 = xall.at[j, row ^ 1, :, c]
        s2 = xall.at[j, row ^ 2, :, c]
        return [
            ag(j, 6, a, a, "y"),
            ag(j, 7, b, b, "x"),
            ag(j, 8, s1, s1, "sib"),
            ag(j, 9, s2, s2, "sib"),
        ]

    def last_copies(j):
        s3 = xall.at[j, row ^ 3, :, c]
        return [ag(j, 10, s3, s3, "sib")]

    def ag_z(j):
        own_copy(j).start()
        for cp in z_copies(j):
            cp.start()

    def ag_xy(j):
        own_copy(j).wait()
        for cp in z_copies(j):
            cp.wait_recv()
        for cp in line_copies(j):
            cp.start()

    def ag_rel(j):
        for cp in line_copies(j)[:2]:
            cp.wait_recv()
        for cp in relay_copies(j):
            cp.start()

    def ag_fin(j):
        for cp in relay_copies(j)[:2]:
            cp.wait_recv()
        for cp in last_copies(j):
            cp.start()

    def loads(j):
        return [
            pltpu.make_async_copy(xall.at[j], xbuf.at[j % 2], load_sem.at[0]),
            pltpu.make_async_copy(c_ref.at[j], cbuf.at[j % 2], load_sem.at[1]),
        ]

    def ag_done(j):
        line_copies(j)[2].wait_recv()
        for cp in relay_copies(j)[2:] + last_copies(j):
            cp.wait_recv()
        for cp in loads(j):
            cp.start()

    def ag_sent(j):
        for cp in z_copies(j) + line_copies(j) + relay_copies(j) + last_copies(j):
            cp.wait_send()

    arrays = (
        (po, ro, so, p1ao, p1bo, p2o, zo, out_ref),
        (pb, rb, sb, p1ab, p1bb, p2b, zb, back_ref),
    )
    near_z, near_cut = ZCOLS, ZCOLS // 2
    mid = near_z + p1ao.shape[-1]

    def rs(i, q, k, src, dst, who):
        s = i % 2
        return remote(src, dst, rs_send.at[q, s, k], rs_recv.at[q, s, k], to[who])

    def rs_sib_copy(q, i):
        p, r = arrays[q][:2]
        return rs(i, q, 0, p.at[:, :, 1 - c], r.at[i % 2], "sib")

    def p1_copies(q, i):
        p, r, s, p1a, p1b, p2, zz, out = arrays[q]
        part = s.at[i % 2, row ^ 3]
        rest = p.shape[-1] - mid
        return [
            rs(i, q, 1, part.at[:, :, pl.ds(near_z, mid - near_z)], p1a.at[i % 2], "y"),
            rs(i, q, 2, part.at[:, :, pl.ds(mid, rest)], p1b.at[i % 2], "x"),
        ]

    def p2_copies(q, i):
        p, r, s, p1a, p1b, p2, zz, out = arrays[q]
        cols = pl.ds(near_z, p.shape[-1] - near_z)
        return [
            rs(i, q, 3, s.at[i % 2, row ^ 1, :, :, cols], p2.at[i % 2, 0], "x"),
            rs(i, q, 4, s.at[i % 2, row ^ 2, :, :, cols], p2.at[i % 2, 1], "y"),
        ]

    def rsz_copies(q, i):
        p, r, s, p1a, p1b, p2, zz, out = arrays[q]
        cols = pl.ds(near_z, p.shape[-1] - near_z)
        return [
            rs(
                i,
                q,
                5 + k,
                s.at[i % 2, row, (z + k + 1) % 4, :, cols],
                zz.at[i % 2, k],
                "z%d" % (k + 1),
            )
            for k in range(3)
        ]

    def first_z_copies(q, i):
        s = arrays[q][2]
        return [
            rs(
                i,
                q,
                8 + k,
                s.at[i % 2, :, (z + k + 1) % 4, :, pl.ds(0, near_z)],
                gz.at[q, i % 2, k],
                "z%d" % (k + 1),
            )
            for k in range(3)
        ]

    def first_p1_copies(q, i):
        part = arrays[q][2].at[i % 2, row ^ 3, z]
        return [
            rs(i, q, 11, part.at[:, pl.ds(0, near_cut)], gp1.at[q, i % 2, 0], "y"),
            rs(i, q, 12, part.at[:, pl.ds(near_cut, near_cut)], gp1.at[q, i % 2, 1], "x"),
        ]

    def first_p2_copies(q, i):
        s = arrays[q][2]
        cols = pl.ds(0, near_z)
        return [
            rs(i, q, 13, s.at[i % 2, row ^ 1, z, :, cols], gp2.at[q, i % 2, 0], "x"),
            rs(i, q, 14, s.at[i % 2, row ^ 2, z, :, cols], gp2.at[q, i % 2, 1], "y"),
        ]

    def rs_sib(q, i):
        rs_sib_copy(q, i).start()

    def rs_p1(q, i):
        p, r, s, p1a, p1b, p2, zz, out = arrays[q]
        cp = rs_sib_copy(q, i)
        cp.wait_recv()

        @pl.loop(0, 4)
        def _(a):
            s[i % 2, a] = (
                p[a, :, c].astype(f32) + r[i % 2, a].astype(f32)
            ).astype(bf16)

        cp.wait_send()
        for cp in p1_copies(q, i) + first_z_copies(q, i):
            cp.start()

    def rs_p2(q, i):
        p, r, s, p1a, p1b, p2, zz, out = arrays[q]
        rest = p.shape[-1] - mid
        copies = p1_copies(q, i)
        copies[0].wait_recv()
        at = s.at[i % 2, row ^ 1, :, :, pl.ds(near_z, mid - near_z)]
        at[...] = added(at[...], p1a[i % 2])
        out_copies = p2_copies(q, i)
        out_copies[0].start()
        copies[1].wait_recv()
        at = s.at[i % 2, row ^ 2, :, :, pl.ds(mid, rest)]
        at[...] = added(at[...], p1b[i % 2])
        out_copies[1].start()
        for cp in first_z_copies(q, i):
            cp.wait_recv()
        at = s.at[i % 2, :, z, :, pl.ds(0, near_z)]
        at[...] = added(at[...], gz[q, i % 2, 0], gz[q, i % 2, 1], gz[q, i % 2, 2])
        for cp in first_p1_copies(q, i):
            cp.start()

    def rs_z(q, i):
        p, r, s, p1a, p1b, p2, zz, out = arrays[q]
        for cp in p2_copies(q, i):
            cp.wait_recv()
        at = s.at[i % 2, row, :, :, pl.ds(near_z, p.shape[-1] - near_z)]
        at[...] = added(at[...], p2[i % 2, 0], p2[i % 2, 1])
        for cp in rsz_copies(q, i):
            cp.start()
        for cp in first_p1_copies(q, i):
            cp.wait_recv()
        at = s.at[i % 2, row ^ 1, z, :, pl.ds(0, near_cut)]
        at[...] = added(at[...], gp1[q, i % 2, 0])
        at = s.at[i % 2, row ^ 2, z, :, pl.ds(near_cut, near_cut)]
        at[...] = added(at[...], gp1[q, i % 2, 1])
        for cp in first_p2_copies(q, i):
            cp.start()

    def rs_fin(q, i):
        p, r, s, p1a, p1b, p2, zz, out = arrays[q]
        copies = rsz_copies(q, i)
        for cp in copies:
            cp.wait_recv()
        total = s[i % 2, row, z, :, near_z:].astype(f32)
        for k in range(3):
            total = total + zz[i % 2, k].astype(f32)
        out[i, :, near_z:] = total
        first = first_p2_copies(q, i)
        for cp in first:
            cp.wait_recv()
        total = s[i % 2, row, z, :, :near_z].astype(f32)
        for k in range(2):
            total = total + gp2[q, i % 2, k].astype(f32)
        out[i, :, :near_z] = total
        for cp in copies + p2_copies(q, i) + p1_copies(q, i):
            cp.wait_send()
        for cp in first + first_p1_copies(q, i) + first_z_copies(q, i):
            cp.wait_send()

    lanes = po.shape[3]
    rows_here = 16 * lanes
    cut = 512

    def tile(i, t):
        s = i % 2
        xt = xbuf[s, 2 * t : 2 * t + 2].reshape(rows_here, width)
        mask = mask_ref[i, t * rows_here : (t + 1) * rows_here, :].astype(f32)
        logits = dot(xt, router_ref[...])[:, : mask.shape[-1]]
        logits = jnp.where(mask > 0, logits, masked_score)
        top = jnp.max(logits, axis=-1, keepdims=True)
        raised = jnp.where(mask > 0, jnp.exp(logits - top), 0.0)
        lane = lax.broadcasted_iota(jnp.int32, raised.shape, 1)
        gate = jnp.sum(
            jnp.where(lane == expert, raised, 0.0), axis=-1, keepdims=True
        ) / jnp.sum(raised, axis=-1, keepdims=True)
        both = dot(xt, wgu_ref[...])
        gp, up = both[:, :hidden], both[:, hidden:]
        sig = jax.nn.sigmoid(gp)
        silu = gp * sig
        hid = (silu * up).astype(bf16)
        hbuf[t * rows_here : (t + 1) * rows_here, :] = hid
        slope = up * sig * (1.0 + gp * (1.0 - sig))
        dots = jnp.zeros((rows_here, 1), f32)
        ghid = jnp.zeros((rows_here, hidden), f32)
        for n in range(width // cut):
            cols = slice(n * cut, (n + 1) * cut)
            wd = wd_ref[:, cols]
            part = dot(hid, wd).astype(bf16).astype(f32)
            cf = cbuf[s, 2 * t : 2 * t + 2, :, :, :, cols]
            shape = cf.shape
            cf = cf.reshape(rows_here, cut).astype(f32)
            dots = dots + jnp.sum(part * cf, axis=-1, keepdims=True)
            po[2 * t : 2 * t + 2, :, :, :, cols] = (
                (gate * part).astype(bf16).reshape(shape)
            )
            gpart = (gate * cf).astype(bf16)
            cbuf[s, 2 * t : 2 * t + 2, :, :, :, cols] = gpart.reshape(shape)
            ghid = ghid + dot_nt(gpart, wd)
        dgp = (ghid * slope).astype(bf16)
        dup = (ghid * silu).astype(bf16)
        grads = jnp.concatenate([dgp, dup], axis=1)
        gbuf[t * rows_here : (t + 1) * rows_here, :] = grads
        for n in range(width // cut):
            cols = slice(n * cut, (n + 1) * cut)
            bk = dot_nt(grads, wgu_ref[cols, :]).astype(bf16)
            pb[2 * t : 2 * t + 2, :, :, :, cols] = bk.reshape(shape)
        high = dots.astype(bf16).astype(f32)
        low = dots - high
        lane = lax.broadcasted_iota(jnp.int32, (rows_here, EXTRA), 1)
        extra = jnp.where(lane == me, high, jnp.where(lane == me + 64, low, 0.0))
        pb[2 * t : 2 * t + 2, :, :, :, width:] = extra.astype(bf16).reshape(
            shape[:-1] + (EXTRA,)
        )

    def weight_grads(i):
        s = i % 2
        every = 2 * rows_here

        @pl.loop(0, width // 256)
        def _(n):
            cols = pl.ds(pl.multiple_of(n * 256, 256), 256)
            xt = xbuf[s, :, :, :, :, cols].reshape(every, 256)
            r = dot_tn(xt, gbuf[...])
            dwg_ref[cols, :] += r[:, :hidden]
            dwu_ref[cols, :] += r[:, hidden:]

        @pl.loop(0, width // cut)
        def _(n):
            cols = pl.ds(pl.multiple_of(n * cut, cut), cut)
            gpart = cbuf[s, :, :, :, :, cols].reshape(every, cut)
            dwd_ref[:, cols] += dot_tn(hbuf[...], gpart)

    ag_z(0)
    ag_z(1)
    dwg_ref[...] = jnp.zeros_like(dwg_ref)
    dwu_ref[...] = jnp.zeros_like(dwu_ref)
    dwd_ref[...] = jnp.zeros_like(dwd_ref)
    for cp in weights:
        cp.wait()
    ag_xy(0)
    ag_z(2)
    ag_xy(1)
    ag_rel(0)
    ag_fin(0)
    ag_rel(1)
    ag_done(0)
    ag_fin(1)

    @pl.loop(0, steps + 2)
    def _(i):
        def when(low, high, *work):
            @pl.when((i >= low) & (i < high))
            def _():
                for f in work:
                    f()

        @pl.when(i + 3 < steps)
        def _():
            ag_z(i + 3)

        @pl.when(i + 2 < steps)
        def _():
            ag_xy(i + 2)

        when(1, steps + 1, lambda: rs_p2(0, i - 1))
        when(2, steps + 2, lambda: rs_z(1, i - 2))

        @pl.when(i < steps)
        def _():
            for cp in loads(i):
                cp.wait()
            tile(i, 0)

        @pl.when(i + 2 < steps)
        def _():
            ag_rel(i + 2)

        when(1, steps + 1, lambda: rs_p2(1, i - 1))
        when(2, steps + 2, lambda: rs_fin(0, i - 2))

        @pl.when(i < steps)
        def _():
            tile(i, 1)
            rs_sib(0, i)
            rs_sib(1, i)

        @pl.when(i + 2 < steps)
        def _():
            ag_fin(i + 2)

        when(0, steps, lambda: rs_p1(0, i))
        when(1, steps + 1, lambda: rs_z(0, i - 1))
        when(2, steps + 2, lambda: rs_fin(1, i - 2))
        when(0, steps, lambda: rs_p1(1, i))

        @pl.when(i < steps)
        def _():
            weight_grads(i)

        @pl.when(i == steps - 1)
        def _():
            for cp in sums:
                cp.start()

        @pl.when(i + 1 < steps)
        def _():
            ag_done(i + 1)

    @pl.loop(0, steps)
    def _(j):
        ag_sent(j)

    for cp in sums:
        cp.wait()


def moe(expert_in, upstream_all, mask, router, gate, up, down):
    tokens, width = expert_in.shape
    hidden = down.shape[0]
    steps = tokens // 16
    wide = width + EXTRA
    mid = ZCOLS + (width - ZCOLS) // 2
    any_, vm = pl.BlockSpec(memory_space=pl.ANY), pl.BlockSpec(memory_space=pltpu.VMEM)
    dma = pltpu.SemaphoreType.DMA
    router = jnp.pad(router, ((0, 0), (0, 128 - router.shape[1])))
    results = pl.pallas_call(
        functools.partial(moe_kernel, steps),
        out_shape=(
            jax.ShapeDtypeStruct((steps, 4, 4, 2, 16, width), bf16),
            jax.ShapeDtypeStruct((steps, 16, width), f32),
            jax.ShapeDtypeStruct((steps, 16, wide), f32),
            jax.ShapeDtypeStruct((width, hidden), f32),
            jax.ShapeDtypeStruct((width, hidden), f32),
            jax.ShapeDtypeStruct((hidden, width), f32),
        ),
        in_specs=[any_, any_, vm, vm, any_, any_, any_],
        out_specs=(any_, vm, vm, any_, any_, any_),
        scratch_shapes=[
            pltpu.VMEM((width, 2 * hidden), bf16),
            pltpu.VMEM((hidden, width), bf16),
            pltpu.VMEM((width, hidden), f32),
            pltpu.VMEM((width, hidden), f32),
            pltpu.VMEM((hidden, width), f32),
            pltpu.VMEM((2, 4, 4, 2, 16, width), bf16),
            pltpu.VMEM((2, 4, 4, 2, 16, width), bf16),
            pltpu.VMEM((512, hidden), bf16),
            pltpu.VMEM((512, 2 * hidden), bf16),
            pltpu.VMEM((4, 4, 2, 16, width), bf16),
            pltpu.VMEM((4, 4, 2, 16, wide), bf16),
            pltpu.VMEM((2, 4, 4, 16, width), bf16),
            pltpu.VMEM((2, 4, 4, 16, wide), bf16),
            pltpu.VMEM((2, 4, 4, 16, width), bf16),
            pltpu.VMEM((2, 4, 4, 16, wide), bf16),
            pltpu.VMEM((2, 4, 16, mid - ZCOLS), bf16),
            pltpu.VMEM((2, 4, 16, width - mid), bf16),
            pltpu.VMEM((2, 4, 16, mid - ZCOLS), bf16),
            pltpu.VMEM((2, 4, 16, wide - mid), bf16),
            pltpu.VMEM((2, 2, 4, 16, width - ZCOLS), bf16),
            pltpu.VMEM((2, 2, 4, 16, wide - ZCOLS), bf16),
            pltpu.VMEM((2, 3, 16, width - ZCOLS), bf16),
            pltpu.VMEM((2, 3, 16, wide - ZCOLS), bf16),
            pltpu.VMEM((2, 2, 3, 4, 16, ZCOLS), bf16),
            pltpu.VMEM((2, 2, 2, 16, ZCOLS // 2), bf16),
            pltpu.VMEM((2, 2, 2, 16, ZCOLS), bf16),
            dma((steps, 11)),
            dma((steps, 11)),
            dma((2, 2, 15)),
            dma((2, 2, 15)),
            dma((6,)),
            dma((6,)),
        ],
        compiler_params=pltpu.CompilerParams(
            collective_id=1, has_side_effects=True, vmem_limit_bytes=60 * 2**20
        ),
        cost_estimate=pl.CostEstimate(
            flops=78 * 10**9, bytes_accessed=10**8, transcendentals=0
        ),
    )(
        expert_in.reshape(steps, 16, width),
        upstream_all,
        mask,
        router,
        gate,
        up,
        down,
    )
    return results[1:]


class Copies:
    def __init__(self, send, recv):
        self.send, self.recv, self.count, self.made = send, recv, 0, []

    def __call__(self, src, dst, who):
        k = self.count
        self.count += 1
        return remote(src, dst, self.send.at[k], self.recv.at[k], who)


def row_mates():
    row, z, c = place()
    mates = [(row, z * 2 + (1 - c))]
    for k in (1, 3, 2):
        for flip in (0, 1):
            mates.append((row, ((z + k) % 4) * 2 + (c ^ flip)))
    return mates


def gather_stages(copy, src, slots, cut, own_sem):
    row, z, c = place()
    to = partners()
    own = slots.at[row, z, c]
    line = slots.at[row, :, c]
    width = src.shape[-1]
    if cut:
        a = slots.at[row ^ 1, :, c, :, pl.ds(0, cut)]
        b = slots.at[row ^ 2, :, c, :, pl.ds(cut, width - cut)]
    else:
        a = slots.at[row ^ 1, pl.ds(0, 2), c]
        b = slots.at[row ^ 2, pl.ds(2, 2), c]
    s1, s2, s3 = (slots.at[row ^ k, :, c] for k in (1, 2, 3))
    local = pltpu.make_async_copy(src, own, own_sem)
    along_z = [copy(src, own, to["z%d" % k]) for k in (1, 3, 2)]
    over = [copy(line, line, to[k]) for k in ("x", "y", "sib")]
    relay = [copy(a, a, to["y"]), copy(b, b, to["x"])]
    inside = [copy(s1, s1, to["sib"]), copy(s2, s2, to["sib"])]
    last = [copy(s3, s3, to["sib"])]

    def start(some):
        for cp in some:
            cp.start()

    def arrived(some):
        for cp in some:
            cp.wait_recv()

    def first():
        local.start()
        start(along_z)

    def second():
        local.wait()
        arrived(along_z)
        start(over)

    def third():
        arrived(over[:2])
        start(relay + inside)

    def fourth():
        arrived(relay)
        start(last)

    def fifth():
        arrived(over[2:] + inside + last)
        for cp in along_z + over + relay + inside + last:
            cp.wait_send()

    return first, second, third, fourth, fifth


def norm_rows(v):
    return lax.rsqrt(jnp.mean(v * v, axis=-1, keepdims=True) + epsilon)


def turned(v, cosine, sine):
    heads = []
    for h in range(v.shape[1] // HEAD_DIM):
        one = v[:, h * HEAD_DIM : (h + 1) * HEAD_DIM]
        heads.append(one * cosine + pltpu.roll(one, HEAD_DIM // 2, 1) * sine)
    return jnp.concatenate(heads, axis=1)


def row_pairs(cols):
    row = lax.broadcasted_iota(jnp.int32, (8, 2 * cols), 0)
    lane = lax.broadcasted_iota(jnp.int32, (8, 2 * cols), 1)
    return jnp.where((lane // cols) == row, 1.0, 0.0).astype(f32)


def sums_by_row(pairs, v):
    return lax.dot_general(
        pairs,
        v,
        (((1,), (1,)), ((), ())),
        precision=lax.Precision.HIGHEST,
        preferred_element_type=f32,
    )


def slot_stages(copy, src, slot, k, cut, own_sem):
    row, z, c = place()
    to = partners()
    there = (z + k) % 4
    own = slot(row, z)
    s0, s1, s2, s3 = (slot(row ^ r, there) for r in range(4))
    width = src.shape[-1]
    a = slot(row ^ 1, there).at[:, :, pl.ds(0, cut)]
    b = slot(row ^ 2, there).at[:, :, pl.ds(cut, width - cut)]
    if k:
        along_z = [copy(src, own, to["z%d" % (4 - k)])]
        over = [copy(s0, s0, to[w]) for w in ("x", "y", "sib")]
    else:
        along_z = []
        local = pltpu.make_async_copy(src, own, own_sem)
        over = [copy(src, own, to[w]) for w in ("x", "y", "sib")]
    relay = [copy(a, a, to["y"]), copy(b, b, to["x"])]
    inside = [copy(s1, s1, to["sib"]), copy(s2, s2, to["sib"])]
    last = [copy(s3, s3, to["sib"])]

    def start(some):
        for cp in some:
            cp.start()

    def arrived(some):
        for cp in some:
            cp.wait_recv()

    def first():
        if k:
            start(along_z)
        else:
            local.start()

    def second():
        arrived(along_z)
        start(over)

    def third():
        arrived(over[:2])
        start(relay + inside)

    def fourth():
        arrived(relay)
        start(last)

    def fifth():
        if not k:
            local.wait()
        arrived(over[2:] + inside + last)
        for cp in along_z + over + relay + inside + last:
            cp.wait_send()

    return first, second, third, fourth, fifth


def front_kernel(
    h_ref,
    wq_ref,
    wk_ref,
    wv_ref,
    wo_ref,
    up_ref,
    pack_ref,
    cos_ref,
    sin_ref,
    woall,
    call,
    packs,
    normed_out,
    wcols_out,
    low_out,
    pre_out,
    att_out,
    stat_ref,
    home_ref,
    mid_ref,
    expert_ref,
    hrow,
    normed_ref,
    wcols,
    low_ref,
    pre_ref,
    att_ref,
    wo_buf,
    gains_ref,
    sums_ref,
    sums_land,
    att_low,
    send,
    recv,
    local_sem,
):
    row, z, c = place()
    blk = z * 2 + c
    to = partners()
    mates = row_mates()
    greet(mates + [to["x"], to["y"]])
    copy = Copies(send, recv)
    cols_here = wcols.shape[3] // 3
    tokens, width = h_ref.shape
    seq = 8 * tokens
    wrows = wq_ref.shape[0]

    pack_stages = gather_stages(copy, pack_ref, packs, 0, local_sem.at[0])
    parts = up_ref.shape[0] // 4
    streams = []
    for k in (0, 1, 3, 2):
        streams.append(
            slot_stages(
                copy,
                wo_ref,
                lambda r, q: woall.at[r, q, c],
                k,
                width // 2,
                local_sem.at[9 + len(streams)],
            )
        )
        for j in range(parts):
            part = pl.ds(j * 4, 4)
            streams.append(
                slot_stages(
                    copy,
                    up_ref.at[part],
                    lambda r, q, part=part: call.at[part, r, q, c],
                    k,
                    width // 2,
                    local_sem.at[9 + len(streams)],
                )
            )
    for_output = streams[:: parts + 1]
    for_upstream = [one for one in streams if one not in for_output]
    saves = [
        pltpu.make_async_copy(src, dst, local_sem.at[9 + len(streams) + k])
        for k, (src, dst) in enumerate(
            (
                (wcols, wcols_out),
                (normed_ref, normed_out),
                (pre_ref, pre_out),
                (low_ref, low_out),
                (att_ref, att_out),
            )
        )
    ]
    wo_load = pltpu.make_async_copy(woall, wo_buf, local_sem.at[9 + len(streams) + 5])
    ticks = [0]

    def tick():
        t = ticks[0]
        ticks[0] += 1
        for stage, lag in ((0, 0), (1, 1), (2, 2), (3, 3)):
            if 0 <= t - lag < len(streams):
                streams[t - lag][stage]()

    own_rows = pltpu.make_async_copy(h_ref, hrow.at[blk], local_sem.at[5])
    up_to, down_to = (row, blk + 2), (row, blk - 2)
    sib = to["sib"]
    own_sib = copy(h_ref, hrow.at[blk], sib)
    ups, downs = [], []
    for t in range(3):
        src = h_ref if t == 0 else hrow.at[blk - 2 * t]
        up = copy(src, hrow.at[blk - 2 * t], up_to)
        got = hrow.at[blk - 2 - 2 * t]
        ups.append((up, copy(got, got, sib), (z < 3) & (z >= t), z >= t + 1))
        src = h_ref if t == 0 else hrow.at[blk + 2 * t]
        down = copy(src, hrow.at[blk + 2 * t], down_to)
        got = hrow.at[blk + 2 + 2 * t]
        downs.append((down, copy(got, got, sib), (z > 0) & (z + t <= 3), z + t + 1 <= 3))

    def line_start(t):
        for cp, hand, sends, gets in (ups[t], downs[t]):
            pl.when(sends)(cp.start)

    def line_arrived(t):
        for cp, hand, sends, gets in (ups[t], downs[t]):

            @pl.when(gets)
            def _():
                cp.wait_recv()
                hand.start()

    def line_done():
        own_rows.wait()
        own_sib.wait()
        for t in range(3):
            for cp, hand, sends, gets in (ups[t], downs[t]):
                pl.when(sends)(cp.wait_send)
                pl.when(gets)(hand.wait)

    def columns(b):
        return pl.ds(pl.multiple_of(b * cols_here, cols_here), cols_here)

    own_cols, col_copies = [], []
    for j, w in enumerate((wq_ref, wk_ref, wv_ref)):
        there = pl.ds(j * cols_here, cols_here)
        own_cols.append(
            pltpu.make_async_copy(
                w.at[:, columns(blk)], wcols.at[row, blk, :, there], local_sem.at[6 + j]
            )
        )
        for mate in mates:
            col_copies.append(
                copy(w.at[:, columns(mate[1])], wcols.at[row, blk, :, there], mate)
            )
    half = wcols.shape[1] // 2
    col_over = [copy(wcols.at[row], wcols.at[row], to[k]) for k in ("x", "y")]
    a = wcols.at[row ^ 1, pl.ds(0, half)]
    b = wcols.at[row ^ 2, pl.ds(half, half)]
    col_relay = [copy(a, a, to["y"]), copy(b, b, to["x"])]
    sum_copies = [
        copy(sums_ref, sums_land.at[k], mate) for k, mate in enumerate(mates)
    ]
    home_copies = [
        copy(att_low.at[mate[1]], home_ref.at[:, columns(blk)], mate) for mate in mates
    ]

    def start(some):
        for cp in some:
            cp.start()

    def arrived(some):
        for cp in some:
            cp.wait_recv()

    own_rows.start()
    start(own_cols)
    line_start(0)
    own_sib.start()
    tick()
    tick()
    pack_stages[0]()
    start(col_copies)
    tick()
    pack_stages[1]()
    tick()
    line_arrived(0)
    line_start(1)
    tick()
    pack_stages[2]()
    for cp in own_cols:
        cp.wait()
    arrived(col_copies)
    start(col_over)
    pack_stages[3]()
    line_arrived(1)
    line_start(2)
    tick()
    arrived(col_over)
    start(col_relay)
    tick()
    line_arrived(2)
    pack_stages[4]()
    arrived(col_relay)
    line_done()
    tick()
    start(saves[:1])

    pieces = []
    for r in range(4):
        for q in range(4):
            pieces.append(
                packs[r, q, 0, 48:64, :].astype(f32) + packs[r, q, 1, 48:64, :].astype(f32)
            )
    gains_ref[...] = jnp.concatenate(pieces, axis=1)[0:8]
    gain_attn = gains_ref[0:1, :]
    segments = jnp.concatenate(
        [
            packs[row, q, k, 16:32, :].astype(f32)[0:1]
            for q in range(4)
            for k in range(2)
        ],
        axis=1,
    )
    pairs = row_pairs(cols_here)
    block = 256
    blocks = seq // block

    for t in range(blocks):
        rows = slice(t * block, (t + 1) * block)
        per = block // tokens
        v = hrow[t * per : (t + 1) * per].reshape(block, width).astype(f32)
        normed = (v * norm_rows(v) * gain_attn).astype(bf16)
        normed_ref[rows, :] = normed
        pre = dot(normed, wcols[...].reshape(width, 3 * cols_here))
        pre_ref[rows, :] = pre[:, : 2 * cols_here]
        low_ref[rows, 2 * cols_here :] = pre[:, 2 * cols_here :].astype(bf16)
        both = pre[:, : 2 * cols_here]
        squares = sums_by_row(pairs, both * both)
        sums_ref[2 * t : 2 * t + 2, :] = squares[0:2]
        if t % 2:
            tick()
    start(saves[1:3])
    start(sum_copies)
    tick()
    total = sums_ref[...]
    for k, cp in enumerate(sum_copies):
        cp.wait_recv()
        total = total + sums_land[k]
    scales = lax.rsqrt(total * (1.0 / width) + epsilon)
    gain_q = gains_ref[1:2, columns(blk)]
    gain_k = gains_ref[2:3, columns(blk)]
    for t in range(blocks):
        rows = slice(t * block, (t + 1) * block)
        turned_scales = jnp.concatenate(
            [scales[2 * t : 2 * t + 2], segments[:, rows], jnp.zeros((5, block), f32)],
            axis=0,
        ).T
        stat_ref[rows, :] = jnp.concatenate(
            [turned_scales, jnp.zeros((block, 120), f32)], axis=1
        )
        cosine, sine = cos_ref[rows, :], sin_ref[rows, :]
        q = pre_ref[rows, :cols_here] * turned_scales[:, 0:1] * gain_q
        low_ref[rows, :cols_here] = turned(q, cosine, sine).astype(bf16)
        k = pre_ref[rows, cols_here : 2 * cols_here] * turned_scales[:, 1:2] * gain_k
        low_ref[rows, cols_here : 2 * cols_here] = turned(k, cosine, sine).astype(bf16)
    tick()

    for t in range(blocks):
        rows = slice(t * block, (t + 1) * block)
        keys = (t + 1) * block
        stat = stat_ref[rows, :]
        place_q = lax.broadcasted_iota(jnp.int32, (block, keys), 0) + t * block
        place_k = lax.broadcasted_iota(jnp.int32, (block, keys), 1)
        allowed = (place_k <= place_q) & (segments[:, :keys] == stat[:, 2:3])
        lane = lax.broadcasted_iota(jnp.int32, stat.shape, 1)
        for h in range(cols_here // HEAD_DIM):
            cols = slice(h * HEAD_DIM, (h + 1) * HEAD_DIM)
            q = low_ref[rows, cols]
            k = low_ref[0:keys, cols_here + h * HEAD_DIM : cols_here + (h + 1) * HEAD_DIM]
            v = low_ref[
                0:keys, 2 * cols_here + h * HEAD_DIM : 2 * cols_here + (h + 1) * HEAD_DIM
            ]
            scores = jnp.where(allowed, dot_nt(q, k) * HEAD_DIM**-0.5, masked_score)
            top = jnp.max(scores, axis=-1, keepdims=True)
            raised = jnp.where(allowed, jnp.exp(scores - top), 0.0)
            share = 1.0 / jnp.sum(raised, axis=-1, keepdims=True)
            out = dot((raised * share).astype(bf16), v)
            att_ref[rows, cols] = out
            per = block // tokens
            att_low[t * per : (t + 1) * per, :, cols] = out.astype(bf16).reshape(
                per, tokens, HEAD_DIM
            )
            stat = jnp.where(lane == 3 + h, top, jnp.where(lane == 5 + h, share, stat))
        stat_ref[rows, :] = stat
        if t % 2:
            tick()
    start(saves[3:])
    home_ref[:, columns(blk)] = att_low[blk]
    start(home_copies)
    tick()
    while ticks[0] < len(streams) - parts + 3:
        tick()
    for stages in for_output:
        stages[4]()
    wo_load.start()
    arrived(home_copies)
    wo_load.wait()
    mid = hrow[blk].astype(f32)
    cut = 512
    for n in range(width // cut):
        cols = slice(n * cut, (n + 1) * cut)
        mid_ref[:, cols] = mid[:, cols] + dot(
            home_ref[...], wo_buf[:, :, :, :, :, cols].reshape(width, cut)
        )
    mid = mid_ref[...]
    expert_ref[...] = (mid * norm_rows(mid) * gains_ref[3:4, :]).astype(bf16)
    while ticks[0] < len(streams) + 3:
        tick()
    for stages in for_upstream:
        stages[4]()
    for cp in col_copies + col_over + col_relay + sum_copies + home_copies:
        cp.wait_send()
    for cp in saves:
        cp.wait()


def front(hidden, wq, wk, wv, wo, upstream, pack, cosine, sine):
    any_, vm = pl.BlockSpec(memory_space=pl.ANY), pl.BlockSpec(memory_space=pltpu.VMEM)
    tokens, width = hidden.shape
    wrows = wq.shape[0]
    seq, cols = 8 * tokens, width // 8
    dma = pltpu.SemaphoreType.DMA
    streams = 4 * (1 + tokens // 64)
    count = 11 + 9 * streams + 13 + 21 + 4 + 14
    shape = jax.ShapeDtypeStruct
    return pl.pallas_call(
        front_kernel,
        out_shape=(
            shape((4, 4, 2, wrows // 16, 16, width), bf16),
            shape((tokens // 16, 4, 4, 2, 16, width), bf16),
            shape((4, 4, 2) + pack.shape, bf16),
            shape((seq, width), bf16),
            shape((4, 8, wrows, 3 * cols), bf16),
            shape((seq, 3 * cols), bf16),
            shape((seq, 2 * cols), f32),
            shape((seq, cols), f32),
            shape((seq, 128), f32),
            shape((tokens, width), bf16),
            shape((tokens, width), f32),
            shape((tokens, width), bf16),
        ),
        in_specs=[any_] * 7 + [vm] * 2,
        out_specs=(any_, any_, vm) + (any_,) * 5 + (vm,) * 4,
        scratch_shapes=[
            pltpu.VMEM((8, tokens, width), bf16),
            pltpu.VMEM((seq, width), bf16),
            pltpu.VMEM((4, 8, wrows, 3 * cols), bf16),
            pltpu.VMEM((seq, 3 * cols), bf16),
            pltpu.VMEM((seq, 2 * cols), f32),
            pltpu.VMEM((seq, cols), f32),
            pltpu.VMEM((4, 4, 2, wrows // 16, 16, width), bf16),
            pltpu.VMEM((8, width), f32),
            pltpu.VMEM((8, seq // 4), f32),
            pltpu.VMEM((7, 8, seq // 4), f32),
            pltpu.VMEM((8, tokens, cols), bf16),
            dma((count,)),
            dma((count,)),
            dma((16 + streams,)),
        ],
        compiler_params=pltpu.CompilerParams(
            collective_id=2, has_side_effects=True, vmem_limit_bytes=56 * 2**20
        ),
        cost_estimate=pl.CostEstimate(
            flops=10**10, bytes_accessed=2 * 10**8, transcendentals=0
        ),
    )(
        hidden,
        wq,
        wk,
        wv,
        wo.reshape(-1, 16, width),
        upstream.reshape(-1, 16, width),
        pack,
        cosine,
        sine,
    )


def added(total, *extra):
    total = total.astype(f32)
    for one in extra:
        total = total + one.astype(f32)
    return total.astype(bf16)


def reduce_stages(copy, src, got, p1a, p1b, p2, land, out):
    row, z, c = place()
    to = partners()
    half = src.shape[-1] // 2

    def own(r):
        return src.at[r, :, c]

    inside = copy(src.at[:, :, 1 - c], got, to["sib"])
    far = [
        copy(own(row ^ 3).at[:, :, pl.ds(0, half)], p1a, to["y"]),
        copy(own(row ^ 3).at[:, :, pl.ds(half, half)], p1b, to["x"]),
    ]
    near = [
        copy(own(row ^ 1), p2.at[0], to["x"]),
        copy(own(row ^ 2), p2.at[1], to["y"]),
    ]
    home = [
        copy(src.at[row, (z + k) % 4, c], land.at[k - 1], to["z%d" % k])
        for k in (1, 3, 2)
    ]

    def first():
        inside.start()

    def second():
        inside.wait_recv()
        for k in (3, 1, 2, 0):
            at = own(row ^ k)
            at[...] = added(at[...], got[row ^ k])
            if k == 3:
                for cp in far:
                    cp.start()

    def third():
        far[0].wait_recv()
        at = own(row ^ 1).at[:, :, pl.ds(0, half)]
        at[...] = added(at[...], p1a[...])
        near[0].start()
        far[1].wait_recv()
        at = own(row ^ 2).at[:, :, pl.ds(half, half)]
        at[...] = added(at[...], p1b[...])
        near[1].start()

    def fourth():
        for cp in near:
            cp.wait_recv()
        at = own(row)
        at[...] = added(at[...], p2[0], p2[1])
        for cp in home:
            cp.start()

    def fifth():
        for cp in home:
            cp.wait_recv()
        total = src[row, z, c].astype(f32)
        for k in range(3):
            total = total + land[k].astype(f32)
        out[...] = total
        for cp in [inside] + far + near + home:
            cp.wait_send()

    return first, second, third, fourth, fifth


def back_kernel(
    ga_home,
    attended_ref,
    proj_ref,
    low_ref,
    pre_ref,
    att_ref,
    stat_ref,
    seg_ref,
    gain_ref,
    cos_ref,
    sin_ref,
    normed_in,
    wcols_in,
    small_ref,
    gn_out,
    q_out,
    k_out,
    v_out,
    wo_out,
    small_out,
    normed_ref,
    wcols,
    ga,
    dq_ref,
    dk_ref,
    dv_ref,
    grads_ref,
    sums_ref,
    sums_land,
    gn,
    gn_sib,
    gn_land,
    gw,
    gw_p1,
    gw_p2,
    gw_land,
    small,
    sm_sib,
    sm_p1a,
    sm_p1b,
    sm_p2,
    sm_land,
    dwo_ref,
    wo_got,
    wo_p1a,
    wo_p1b,
    wo_p2,
    wo_land,
    send,
    recv,
    local_sem,
):
    row, z, c = place()
    blk = z * 2 + c
    to = partners()
    mates = row_mates()
    greet(mates + [to["x"], to["y"]])
    copy = Copies(send, recv)
    tokens, width = ga_home.shape
    seq = 8 * tokens
    cols_here = att_ref.shape[1]
    wrows = wo_out.shape[0]
    scale = HEAD_DIM**-0.5
    block = 256
    blocks = seq // block
    per = block // tokens

    def start(some):
        for cp in some:
            cp.start()

    def arrived(some):
        for cp in some:
            cp.wait_recv()

    def columns(b):
        return pl.ds(pl.multiple_of(b * cols_here, cols_here), cols_here)

    streams = []
    for j in range(wrows // 16):
        part = pl.ds(j * 16, 16)
        streams.append(
            reduce_stages(
                copy,
                dwo_ref.at[:, :, :, part],
                wo_got.at[j],
                wo_p1a.at[j],
                wo_p1b.at[j],
                wo_p2.at[j],
                wo_land.at[j],
                wo_out.at[part],
            )
        )
    ticks = [0]

    def tick():
        t = ticks[0]
        ticks[0] += 1
        for stage in range(5):
            if 0 <= t - stage < len(streams):
                streams[t - stage][stage]()

    own_ga = pltpu.make_async_copy(
        ga_home.at[:, columns(blk)], ga.at[blk], local_sem.at[0]
    )
    ga_copies = [copy(ga_home.at[:, columns(mate[1])], ga.at[blk], mate) for mate in mates]
    sum_copies = [
        copy(sums_ref, sums_land.at[k], mate) for k, mate in enumerate(mates)
    ]
    half = gw.shape[1] // 2
    w_far = [
        copy(gw.at[row ^ 3, pl.ds(0, half)], gw_p1.at[0], to["y"]),
        copy(gw.at[row ^ 3, pl.ds(half, half)], gw_p1.at[1], to["x"]),
    ]
    w_near = [
        copy(gw.at[row ^ 1], gw_p2.at[0], to["x"]),
        copy(gw.at[row ^ 2], gw_p2.at[1], to["y"]),
    ]
    w_home = [copy(gw.at[row, mate[1]], gw_land.at[blk], mate) for mate in mates]
    d0, d1 = 3 - z, (3 * z + 2) % 5
    d2 = 3 - d1
    inner, outer = (z == 1) | (z == 2), (z == 0) | (z == 3)
    n_sib = [
        copy(gn.at[chip, 1 - c], gn_sib.at[chip], to["sib"]) for chip in (d0, d1, d2, z)
    ]
    n_relay = copy(gn.at[d0, c], gn_land.at[0], (row, (1 + z // 2) * 2 + c))
    n_inner = copy(gn.at[d0, c], gn_land.at[1], (row, (2 - z // 2) * 2 + c))
    n_home = [
        copy(gn.at[d1, c], gn_land.at[2], (row, d1 * 2 + c)),
        copy(gn.at[d2, c], gn_land.at[3], (row, d2 * 2 + c)),
    ]
    s_sib = copy(small.at[0], sm_sib, to["sib"])
    s_far = [
        copy(small.at[1, row ^ 3, 0:2], sm_p1a, to["y"]),
        copy(small.at[1, row ^ 3, 2:4], sm_p1b, to["x"]),
    ]
    s_near = [
        copy(small.at[1, row ^ 1], sm_p2.at[0], to["x"]),
        copy(small.at[1, row ^ 2], sm_p2.at[1], to["y"]),
    ]
    s_home = [
        copy(small.at[1, row, (z + k) % 4], sm_land.at[k - 1], to["z%d" % k])
        for k in (1, 3, 2)
    ]

    late = [
        pltpu.make_async_copy(src, dst, local_sem.at[1 + len(streams) + k])
        for k, (src, dst) in enumerate(
            ((normed_in, normed_ref), (wcols_in, wcols))
        )
    ]
    own_ga.start()
    start(ga_copies)
    start(late)

    @pl.loop(0, 8)
    def _(n):
        some = attended_ref[:, pl.ds(pl.multiple_of(n * block, block), block)]
        made = dot_tn(some, proj_ref[...]).astype(bf16)
        dwo_ref[n // 2, pl.ds(2 * (n % 2), 2)] = made.reshape(2, 2, wrows, width)

    tick()
    dk_ref[...] = jnp.zeros_like(dk_ref)
    dv_ref[...] = jnp.zeros_like(dv_ref)
    small[0] = small_ref[...]
    own_ga.wait()
    tick()
    arrived(ga_copies)

    segments = seg_ref[0:1, :]
    for t in range(blocks):
        rows = slice(t * block, (t + 1) * block)
        keys = (t + 1) * block
        stat = stat_ref[rows, :]
        place_q = lax.broadcasted_iota(jnp.int32, (block, keys), 0) + t * block
        place_k = lax.broadcasted_iota(jnp.int32, (block, keys), 1)
        allowed = (place_k <= place_q) & (segments[:, :keys] == stat[:, 2:3])
        for h in range(cols_here // HEAD_DIM):
            cols = slice(h * HEAD_DIM, (h + 1) * HEAD_DIM)
            q = low_ref[rows, cols]
            k = low_ref[0:keys, cols_here + h * HEAD_DIM : cols_here + (h + 1) * HEAD_DIM]
            v = low_ref[
                0:keys, 2 * cols_here + h * HEAD_DIM : 2 * cols_here + (h + 1) * HEAD_DIM
            ]
            g = ga[t * per : (t + 1) * per, :, cols].reshape(block, HEAD_DIM)
            scores = jnp.where(allowed, dot_nt(q, k) * scale, masked_score)
            raised = jnp.exp(scores - stat[:, 3 + h : 4 + h])
            probs = jnp.where(allowed, raised, 0.0) * stat[:, 5 + h : 6 + h]
            delta = jnp.sum(g.astype(f32) * att_ref[rows, cols], axis=-1, keepdims=True)
            ds = (probs * (dot_nt(g, v) - delta)).astype(bf16)
            dq_ref[rows, cols] = dot(ds, k) * scale
            dk_ref[0:keys, cols] += dot_tn(ds, q) * scale
            dv_ref[0:keys, cols] += dot_tn(probs.astype(bf16), g)
        tick()

    pairs = row_pairs(cols_here)
    gain_q, gain_k = gain_ref[0:1, :], gain_ref[1:2, :]
    for_q = jnp.zeros((1, cols_here), f32)
    for_k = jnp.zeros((1, cols_here), f32)
    for t in range(blocks):
        rows = slice(t * block, (t + 1) * block)
        cosine, sine = cos_ref[rows, :], -sin_ref[rows, :]
        q_pre, k_pre = pre_ref[rows, :cols_here], pre_ref[rows, cols_here:]
        dq = turned(dq_ref[rows, :], cosine, sine)
        dk = turned(dk_ref[rows, :], cosine, sine)
        dq_ref[rows, :] = dq
        dk_ref[rows, :] = dk
        vq, vk = dq * q_pre, dk * k_pre
        for_q = for_q + jnp.sum(vq * stat_ref[rows, 0:1], axis=0, keepdims=True)
        for_k = for_k + jnp.sum(vk * stat_ref[rows, 1:2], axis=0, keepdims=True)
        sums = sums_by_row(pairs, jnp.concatenate([vq * gain_q, vk * gain_k], axis=1))
        sums_ref[2 * t : 2 * t + 2, :] = sums[0:2]
    start(sum_copies)
    tick()
    total = sums_ref[...]
    for k, cp in enumerate(sum_copies):
        cp.wait_recv()
        total = total + sums_land[k]
    means = total * (1.0 / width)
    for t in range(blocks):
        rows = slice(t * block, (t + 1) * block)
        mean = jnp.concatenate(
            [means[2 * t : 2 * t + 2], jnp.zeros((6, block), f32)], axis=0
        ).T
        for j, (d_ref, gain) in enumerate(((dq_ref, gain_q), (dk_ref, gain_k))):
            cols = slice(j * cols_here, (j + 1) * cols_here)
            r = stat_ref[rows, j : j + 1]
            grads_ref[rows, cols] = (
                r * gain * d_ref[rows, :]
                - pre_ref[rows, cols] * (r * r * r) * mean[:, j : j + 1]
            ).astype(bf16)
        grads_ref[rows, 2 * cols_here :] = dv_ref[rows, :].astype(bf16)

    deep = 8 * wrows
    for cp in late:
        cp.wait()

    def weight_rows(k):
        there = row ^ k
        some = normed_ref[:, pl.ds(pl.multiple_of(there * deep, deep), deep)]
        gw[there] = (
            dot_tn(some, grads_ref[...]).astype(bf16).reshape(8, wrows, 3 * cols_here)
        )

    weight_rows(3)
    start(w_far)
    weights = wcols[...].reshape(width, 3 * cols_here)
    for_attn = jnp.zeros((1, width), f32)
    chips = (d0, d1, d2, z)
    for n, chip in enumerate(chips):
        tok = pl.ds(pl.multiple_of(chip * block, block), block)
        made = dot_nt(grads_ref[tok, :], weights)
        gn[chip] = made.astype(bf16).reshape(per, tokens, width)
        n_sib[n].start()
        for_attn = for_attn + jnp.sum(
            made * normed_ref[tok, :].astype(f32), axis=0, keepdims=True
        )
        if n:
            before = chips[n - 1]
            n_sib[n - 1].wait_recv()
            n_sib[n - 1].wait_send()
            gn[before, c] = added(gn[before, c], gn_sib[before])
            if n == 1:
                pl.when(outer)(n_relay.start)
                pl.when(inner)(n_inner.start)
            elif n == 2:
                n_home[0].start()
    weight_rows(1)
    weight_rows(2)

    @pl.when(inner)
    def _():
        n_relay.wait_recv()
        gn[d2, c] = added(gn[d2, c], gn_land[0])

    n_home[1].start()
    weight_rows(0)
    tick()
    for r in range(4):
        for q in range(4):
            at = (r * 4 + q) * 128
            small[0, r, q, 16:17, :] = for_attn[:, at : at + 128]
    for j in range(cols_here // 128):
        at = blk * (cols_here // 128) + j
        small[0, at // 4, at % 4, 17:18, :] = for_q[:, j * 128 : (j + 1) * 128]
        small[0, at // 4, at % 4, 18:19, :] = for_k[:, j * 128 : (j + 1) * 128]
    s_sib.start()

    arrived(w_far[:1])
    gw[row ^ 1, 0:half] = added(gw[row ^ 1, 0:half], gw_p1[0])
    w_near[0].start()
    arrived(w_far[1:])
    gw[row ^ 2, half:] = added(gw[row ^ 2, half:], gw_p1[1])
    w_near[1].start()
    s_sib.wait_recv()
    small[1] = small[0] + sm_sib[...]
    start(s_far)
    tick()
    arrived(s_far)
    small[1, row ^ 1, 0:2] = small[1, row ^ 1, 0:2] + sm_p1a[...]
    small[1, row ^ 2, 2:4] = small[1, row ^ 2, 2:4] + sm_p1b[...]
    start(s_near)
    arrived(w_near)
    for b in range(8):
        gw[row, b] = added(gw[row, b], gw_p2[0, b], gw_p2[1, b])
    start(w_home)
    arrived(s_near)
    small[1, row] = small[1, row] + sm_p2[0] + sm_p2[1]
    start(s_home)
    while ticks[0] < len(streams) + 4:
        tick()

    n_sib[3].wait_recv()
    gn_out[...] = gn[z, c].astype(f32) + gn_sib[z].astype(f32)
    arrived(n_home)
    gn_out[...] += gn_land[2].astype(f32) + gn_land[3].astype(f32)

    @pl.when(inner)
    def _():
        n_inner.wait_recv()
        n_inner.wait_send()
        gn_out[...] += gn_land[1].astype(f32)

    @pl.when(outer)
    def _():
        n_relay.wait_send()

    arrived(s_home)
    small_out[...] = small[1, row, z] + sm_land[0] + sm_land[1] + sm_land[2]
    gw_land[blk] = gw[row, blk]
    arrived(w_home)
    for b in range(8):
        for j, out in enumerate((q_out, k_out, v_out)):
            out[:, b * cols_here : (b + 1) * cols_here] = gw_land[
                b, :, j * cols_here : (j + 1) * cols_here
            ].astype(f32)
    n_sib[3].wait_send()
    for cp in ga_copies + sum_copies + w_far + w_near + w_home + n_home:
        cp.wait_send()
    for cp in [s_sib] + s_far + s_near + s_home:
        cp.wait_send()


def back(ga, att_low, proj, low, pre, att, stat, seg, gain, cosine, sine, normed, wcols, small):
    any_, vm = pl.BlockSpec(memory_space=pl.ANY), pl.BlockSpec(memory_space=pltpu.VMEM)
    tokens, width = ga.shape
    seq, cols = 8 * tokens, width // 8
    wrows = wcols.shape[2]
    fields = small.shape[2:]
    dma = pltpu.SemaphoreType.DMA
    streams = wrows // 16
    count = 8 * streams + 7 + 7 + 2 + 2 + 7 + 4 + 4 + 1 + 2 + 2 + 3
    shape, vmem = jax.ShapeDtypeStruct, pltpu.VMEM
    weight = shape((wrows, width), f32)
    return pl.pallas_call(
        back_kernel,
        out_shape=(
            shape((tokens, width), f32),
            weight,
            weight,
            weight,
            weight,
            shape(fields, f32),
        ),
        in_specs=[any_] + [vm] * 10 + [any_] * 2 + [vm],
        out_specs=(vm,) * 6,
        scratch_shapes=[
            vmem((seq, width), bf16),
            vmem((4, 8, wrows, 3 * cols), bf16),
            vmem((8, tokens, cols), bf16),
            vmem((seq, cols), f32),
            vmem((seq, cols), f32),
            vmem((seq, cols), f32),
            vmem((seq, 3 * cols), bf16),
            vmem((8, seq // 4), f32),
            vmem((7, 8, seq // 4), f32),
            vmem((4, 2, tokens, width), bf16),
            vmem((4, tokens, width), bf16),
            vmem((4, tokens, width), bf16),
            vmem((4, 8, wrows, 3 * cols), bf16),
            vmem((2, 4, wrows, 3 * cols), bf16),
            vmem((2, 8, wrows, 3 * cols), bf16),
            vmem((8, wrows, 3 * cols), bf16),
            vmem((2, 4, 4) + fields, f32),
            vmem((4, 4) + fields, f32),
            vmem((2,) + fields, f32),
            vmem((2,) + fields, f32),
            vmem((2, 4) + fields, f32),
            vmem((3,) + fields, f32),
            vmem((4, 4, 2, wrows, width), bf16),
            vmem((streams, 4, 4, 16, width), bf16),
            vmem((streams, 4, 16, width // 2), bf16),
            vmem((streams, 4, 16, width // 2), bf16),
            vmem((streams, 2, 4, 16, width), bf16),
            vmem((streams, 3, 16, width), bf16),
            dma((count,)),
            dma((count,)),
            dma((4 + streams,)),
        ],
        compiler_params=pltpu.CompilerParams(
            collective_id=7, has_side_effects=True, vmem_limit_bytes=60 * 2**20
        ),
        cost_estimate=pl.CostEstimate(
            flops=10**10, bytes_accessed=2 * 10**8, transcendentals=0
        ),
    )(
        ga,
        att_low,
        proj,
        low,
        pre,
        att,
        stat,
        seg,
        gain,
        cosine,
        sine,
        normed,
        wcols,
        small,
    )


def rope_tables(count):
    half = HEAD_DIM // 2
    frequency = jnp.exp(
        -math.log(10000.0) * 2.0 * jnp.arange(half, dtype=f32) / HEAD_DIM
    )
    angles = jnp.arange(count, dtype=f32)[:, None] * frequency[None, :]
    return jnp.cos(angles), jnp.sin(angles)


def rope(values, cosine, sine):
    half = HEAD_DIM // 2
    a, b = values[..., :half], values[..., half:]
    return jnp.concatenate([a * cosine - b * sine, b * cosine + a * sine], axis=-1)


def norm_back(v, r, g, c, mean_vgc):
    return r * g * c - v * (r * r * r) * mean_vgc


def experts_by_scan(expert_in, upstream, gates, gate_local, up_local, down_local):
    tokens, width = expert_in.shape
    experts = gates.shape[1]
    rows, blocks = lax.axis_size("row"), lax.axis_size("blk")
    devices = rows * blocks
    me = lax.axis_index("row") * blocks + lax.axis_index("blk")
    parts = devices * tokens // 2048
    step = tokens // parts
    all_gates = lax.all_gather(gates, BOTH, axis=0, tiled=False)
    own_gate = jnp.sum(
        jnp.where(
            jnp.arange(experts, dtype=jnp.int32)[None, None, :] == me // 2,
            all_gates,
            0.0,
        ),
        axis=-1,
    )

    def expert_part(sums, items):
        own_rows, own_upstream, gate_col = items
        got = lax.all_gather(own_rows, BOTH, axis=0, tiled=True)
        up_stream = lax.all_gather(own_upstream, BOTH, axis=0, tiled=True)
        gate_col = gate_col.reshape(devices * step, 1)
        gate_pre = dot(got, gate_local)
        up_pre = dot(got, up_local)
        sig = jax.nn.sigmoid(gate_pre)
        silu = gate_pre * sig
        hidden = (silu * up_pre).astype(bf16)
        part_f = dot(hidden, down_local).astype(bf16).astype(f32)
        up_f = up_stream.astype(f32)
        dots = jnp.sum(part_f * up_f, axis=-1).reshape(devices, step)
        mixed = (gate_col * part_f).astype(bf16)
        out = lax.psum_scatter(mixed, BOTH, scatter_dimension=0, tiled=True)
        grad_part = (gate_col * up_f).astype(bf16)
        grad_hidden = dot_nt(grad_part, down_local)
        grad_gate_pre = (
            grad_hidden * up_pre * sig * (1.0 + gate_pre * (1.0 - sig))
        ).astype(bf16)
        grad_up_pre = (grad_hidden * silu).astype(bf16)
        grad_rows = (
            dot_nt(grad_gate_pre, gate_local) + dot_nt(grad_up_pre, up_local)
        ).astype(bf16)
        back = lax.psum_scatter(grad_rows, BOTH, scatter_dimension=0, tiled=True)
        sums = (
            sums[0] + dot_tn(got, grad_gate_pre),
            sums[1] + dot_tn(got, grad_up_pre),
            sums[2] + dot_tn(hidden, grad_part),
        )
        return sums, (out, back, dots)

    sums = (
        jnp.zeros(gate_local.shape, f32),
        jnp.zeros(up_local.shape, f32),
        jnp.zeros(down_local.shape, f32),
    )
    items = (
        expert_in.reshape(parts, step, width),
        upstream.reshape(parts, step, width),
        own_gate.reshape(devices, parts, step).transpose(1, 0, 2),
    )
    if parts > 2:
        sums, (outs, backs, dots) = lax.scan(expert_part, sums, items)
    else:
        made = []
        for part in range(parts):
            sums, result = expert_part(sums, tuple(item[part] for item in items))
            made.append(result)
        outs, backs, dots = (jnp.stack(some) for some in zip(*made))
    dots = dots.transpose(1, 0, 2).reshape(devices, tokens)
    outs = outs.reshape(tokens, width)
    backs = backs.reshape(tokens, width)
    dots = lax.all_to_all(dots, BOTH, split_axis=0, concat_axis=0, tiled=True)
    grad_gates = jnp.sum(dots.reshape(experts, 2, tokens), axis=1).T
    return outs.astype(f32), backs.astype(f32), grad_gates, sums


def own_mesh_body(
    hidden_in,
    segment_ids,
    expert_ids,
    attention_gain,
    query_gain,
    key_gain,
    expert_gain,
    query_weight,
    key_weight,
    value_weight,
    output_weight,
    router_weight,
    gate_weight,
    up_weight,
    down_weight,
    grad_out,
):
    tokens, width = hidden_in.shape[1:]
    wrows = query_weight.shape[0]
    experts = router_weight.shape[1]
    blocks = lax.axis_size("blk")
    seq = tokens * blocks
    head_cols = width // blocks
    blk = lax.axis_index("blk")
    upstream_low = grad_out[0]

    experts_in_order = jnp.arange(experts, dtype=jnp.int32)
    routed = jnp.any(
        expert_ids[0][:, :, None] == experts_in_order[None, None, :], axis=1
    )
    routed_t = jnp.any(
        expert_ids[0].T[None, :, :] == experts_in_order[:, None, None], axis=1
    )
    gains = jnp.stack([attention_gain, query_gain, key_gain, expert_gain])
    spare = tokens - wrows
    gains = jnp.concatenate([gains, gains], axis=1)
    lane = jnp.arange(2 * wrows, dtype=jnp.int32)[None]
    gains = jnp.where(lane // wrows == blk % 2, gains, 0)

    def rows_at(first, values, lanes):
        return jnp.pad(values.astype(f32), ((first, 64 - first - values.shape[0]), (0, lanes)))

    pack = (
        rows_at(0, routed_t, 0)
        + rows_at(16, segment_ids, 0)
        + rows_at(32, router_weight.T, spare)
        + rows_at(32 + experts, gains, 0)
    ).astype(bf16)
    cosine, sine = rope_tables(seq)
    cosine = jnp.concatenate([cosine, cosine], axis=1)
    sine = jnp.concatenate([-sine, sine], axis=1)
    (
        full_output,
        upstream_all,
        packs,
        normed_row,
        qkv_cols,
        low,
        pre,
        attended,
        stats,
        attended_low,
        residual_mid,
        expert_in,
    ) = front(
        hidden_in[0],
        query_weight,
        key_weight,
        value_weight,
        output_weight,
        upstream_low,
        pack,
        cosine,
        sine,
    )
    full_output = full_output.reshape(width, width)
    packs = packs.reshape(-1, pack.shape[0], tokens)
    router = packs[:, 32 : 32 + experts, :wrows].transpose(0, 2, 1).reshape(width, -1)
    gains = packs[:, 32 + experts : 36 + experts].reshape(-1, 2, 4, tokens).sum(axis=1)
    gains = gains.transpose(1, 0, 2).reshape(4, width).astype(f32)
    gain_attn, gain_expert = gains[0], gains[3]
    own_q_gain = lax.dynamic_slice_in_dim(gains[1], blk * head_cols, head_cols)
    own_k_gain = lax.dynamic_slice_in_dim(gains[2], blk * head_cols, head_cols)
    steps = tokens // 16
    mask = packs[:, :experts].reshape(-1, experts, steps, 16)
    mask = mask.transpose(2, 0, 3, 1).reshape(steps, -1, experts)
    x = hidden_in[0].astype(f32)
    r_attn = lax.rsqrt(jnp.mean(x * x, axis=-1, keepdims=True) + epsilon)
    r_exp = lax.rsqrt(
        jnp.mean(residual_mid * residual_mid, axis=-1, keepdims=True) + epsilon
    )
    logits = dot(expert_in, router)
    top_logit = jnp.max(
        jnp.where(routed, logits, masked_score), axis=-1, keepdims=True
    )
    gates = jnp.where(routed, jnp.exp(logits - top_logit), 0.0)
    gates = gates / jnp.sum(gates, axis=-1, keepdims=True)

    outs, backs, grad_gate_local, grad_up_local, grad_down_local = moe(
        expert_in,
        upstream_all,
        mask,
        router,
        gate_weight[0],
        up_weight[0],
        down_weight[0],
    )
    outs = outs.reshape(tokens, width)
    backs = backs.reshape(tokens, width + EXTRA)
    dots = backs[:, width : width + 2 * experts]
    dots = dots + backs[:, width + 64 : width + 64 + 2 * experts]
    grad_gates = jnp.sum(dots.reshape(tokens, experts, 2), axis=2)
    layer_out = (residual_mid + outs).astype(bf16)
    upstream = upstream_low.astype(f32)
    grad_picked = gates * (
        grad_gates - jnp.sum(gates * grad_gates, axis=-1, keepdims=True)
    )
    grad_logits = jnp.where(routed, grad_picked, 0.0).astype(bf16)
    grad_expert_in = backs[:, :width] + dot_nt(grad_logits, router)
    grad_router = dot_tn(grad_logits, expert_in)
    grad_gain_expert = jnp.sum(grad_expert_in * residual_mid * r_exp, axis=0)
    grad_mid = upstream + norm_back(
        residual_mid,
        r_exp,
        gain_expert,
        grad_expert_in,
        jnp.mean(residual_mid * gain_expert * grad_expert_in, axis=-1, keepdims=True),
    )
    grad_proj = grad_mid.astype(bf16)
    grad_attended = dot_nt(grad_proj, full_output).astype(bf16)
    small = jnp.concatenate(
        [
            grad_router,
            jnp.zeros((3, width), f32),
            grad_gain_expert[None],
            jnp.zeros((20 - experts, width), f32),
        ],
        axis=0,
    )
    fields = small.shape[0]
    small = small.reshape(fields, 4, 4, 2 * wrows).transpose(1, 2, 0, 3)
    grad_normed, grad_q, grad_k, grad_v, grad_output_w, small = back(
        grad_attended,
        attended_low,
        grad_proj,
        low,
        pre,
        attended,
        stats,
        jnp.broadcast_to(stats[:, 2][None], (8, seq)),
        jnp.concatenate(
            [own_q_gain[None], own_k_gain[None], jnp.zeros((6, head_cols), f32)], axis=0
        ),
        cosine,
        sine,
        normed_row,
        qkv_cols,
        small,
    )
    input_grad = grad_mid + norm_back(
        x,
        r_attn,
        gain_attn,
        grad_normed,
        jnp.mean(x * gain_attn * grad_normed, axis=-1, keepdims=True),
    )
    small = lax.dynamic_slice_in_dim(small, (blk % 2) * wrows, wrows, axis=1)
    return (
        layer_out[None],
        input_grad[None],
        small[experts] / attention_gain.astype(f32),
        small[experts + 1],
        small[experts + 2],
        small[experts + 3],
        grad_q,
        grad_k,
        grad_v,
        grad_output_w,
        small[:experts].T,
        grad_gate_local[None],
        grad_up_local[None],
        grad_down_local[None],
    )


def any_mesh_body(
    hidden_in,
    segment_ids,
    expert_ids,
    attention_gain,
    query_gain,
    key_gain,
    expert_gain,
    query_weight,
    key_weight,
    value_weight,
    output_weight,
    router_weight,
    gate_weight,
    up_weight,
    down_weight,
    grad_out,
):
    tokens = hidden_in.shape[1]
    width = hidden_in.shape[2]
    experts = router_weight.shape[1]
    rows, blocks = lax.axis_size("row"), lax.axis_size("blk")
    devices = rows * blocks
    seq = tokens * blocks
    head_cols = width // blocks
    heads_here = HEADS // blocks
    blk = lax.axis_index("blk")
    me = lax.axis_index("row") * blocks + blk
    scale = HEAD_DIM**-0.5

    small = jnp.concatenate(
        [
            router_weight,
            attention_gain[:, None],
            query_gain[:, None],
            key_gain[:, None],
            expert_gain[:, None],
        ],
        axis=1,
    )
    small = lax.all_gather(small, BOTH, axis=0, tiled=True)
    router = small[:, :experts]
    gains = small[:, experts:].astype(f32)
    gain_attn, gain_expert = gains[:, 0], gains[:, 3]
    own_q_gain = lax.dynamic_slice_in_dim(gains[:, 1], blk * head_cols, head_cols)
    own_k_gain = lax.dynamic_slice_in_dim(gains[:, 2], blk * head_cols, head_cols)

    x = hidden_in[0].astype(f32)
    r_attn = lax.rsqrt(jnp.mean(x * x, axis=-1, keepdims=True) + epsilon)
    normed = (x * r_attn * gain_attn).astype(bf16)
    normed_row = lax.all_gather(normed, "blk", axis=0, tiled=True)
    segments = lax.all_gather(segment_ids[0], "blk", axis=0, tiled=True)

    stacked = jnp.stack([query_weight, key_weight, value_weight], axis=0)
    wrows = stacked.shape[1]
    stacked = stacked.reshape(3, wrows, blocks, head_cols).transpose(2, 1, 0, 3)
    stacked = stacked.reshape(blocks, wrows, 3 * head_cols)
    cols = lax.all_to_all(stacked, "blk", split_axis=0, concat_axis=0, tiled=True)
    cols = cols.reshape(blocks * wrows, 3 * head_cols)
    qkv_cols = lax.all_gather(cols, "row", axis=0, tiled=True)
    full_output = lax.all_gather(output_weight, BOTH, axis=0, tiled=True)

    qkv = dot(normed_row, qkv_cols)
    query_pre = qkv[:, :head_cols]
    key_pre = qkv[:, head_cols : 2 * head_cols]
    value = qkv[:, 2 * head_cols :].astype(bf16)
    squares = jnp.stack(
        [jnp.sum(query_pre * query_pre, axis=-1), jnp.sum(key_pre * key_pre, axis=-1)]
    )
    squares = lax.psum(squares, "blk") / width
    r_q = lax.rsqrt(squares[0] + epsilon)[:, None]
    r_k = lax.rsqrt(squares[1] + epsilon)[:, None]
    cosine, sine = (table[:, None] for table in rope_tables(seq))

    def heads(v):
        return v.reshape(seq, heads_here, HEAD_DIM)

    query = rope(heads(query_pre * r_q * own_q_gain), cosine, sine).astype(bf16)
    key = rope(heads(key_pre * r_k * own_k_gain), cosine, sine).astype(bf16)
    value = heads(value)
    places = jnp.arange(seq, dtype=jnp.int32)
    allowed = (places[None, :] <= places[:, None]) & (
        segments[None, :] == segments[:, None]
    )
    scores = jnp.einsum("qhd,khd->hqk", query, key, preferred_element_type=f32) * scale
    scores = jnp.where(allowed[None], scores, masked_score)
    top = jnp.max(scores, axis=-1, keepdims=True)
    weights = jnp.where(allowed[None], jnp.exp(scores - top), 0.0)
    total = jnp.sum(weights, axis=-1, keepdims=True)
    probs = weights / total
    probs_low = probs.astype(bf16)
    attended = jnp.einsum("hqk,khd->qhd", probs_low, value, preferred_element_type=f32)
    attended_low_cols = attended.astype(bf16).reshape(blocks, tokens, head_cols)
    attended_low = lax.all_to_all(
        attended_low_cols, "blk", split_axis=0, concat_axis=0, tiled=True
    )
    attended_low = attended_low.transpose(1, 0, 2).reshape(tokens, width)

    residual_mid = x + dot(attended_low, full_output)
    r_exp = lax.rsqrt(
        jnp.mean(residual_mid * residual_mid, axis=-1, keepdims=True) + epsilon
    )
    expert_in = (residual_mid * r_exp * gain_expert).astype(bf16)
    logits = dot(expert_in, router)
    routes = expert_ids[0]
    routed = jnp.any(
        routes[:, :, None] == jnp.arange(experts, dtype=jnp.int32)[None, None, :],
        axis=1,
    )
    top_logit = jnp.max(
        jnp.where(routed, logits, masked_score), axis=-1, keepdims=True
    )
    gates = jnp.where(routed, jnp.exp(logits - top_logit), 0.0)
    gates = gates / jnp.sum(gates, axis=-1, keepdims=True)

    gate_local, up_local, down_local = gate_weight[0], up_weight[0], down_weight[0]
    outs, backs, grad_gates, sums = experts_by_scan(
        expert_in, grad_out[0], gates, gate_local, up_local, down_local
    )
    grad_gate_local, grad_up_local, grad_down_local = sums
    layer_out = (residual_mid + outs).astype(bf16)
    upstream = grad_out[0].astype(f32)
    grad_picked = gates * (
        grad_gates - jnp.sum(gates * grad_gates, axis=-1, keepdims=True)
    )
    grad_logits = jnp.where(routed, grad_picked, 0.0).astype(bf16)
    grad_expert_in = backs + dot_nt(
        grad_logits, router
    )
    grad_router = dot_tn(expert_in, grad_logits)
    grad_gain_expert = jnp.sum(grad_expert_in * residual_mid * r_exp, axis=0)
    grad_mid = upstream + norm_back(
        residual_mid,
        r_exp,
        gain_expert,
        grad_expert_in,
        jnp.mean(residual_mid * gain_expert * grad_expert_in, axis=-1, keepdims=True),
    )
    grad_proj = grad_mid.astype(bf16)
    grad_output_w = dot_tn(attended_low, grad_proj).astype(bf16)
    grad_output_w = lax.psum_scatter(
        grad_output_w, BOTH, scatter_dimension=0, tiled=True
    ).astype(f32)
    grad_attended = dot_nt(grad_proj, full_output).astype(bf16)
    grad_attended = grad_attended.reshape(tokens, blocks, head_cols).transpose(1, 0, 2)
    grad_attended = lax.all_to_all(
        grad_attended, "blk", split_axis=0, concat_axis=0, tiled=True
    )
    grad_attended = grad_attended.reshape(seq, heads_here, HEAD_DIM)
    row_delta = jnp.sum(grad_attended.astype(f32) * attended, axis=-1).T
    grad_probs = jnp.einsum(
        "qhd,khd->hqk", grad_attended, value, preferred_element_type=f32
    )
    grad_scores = (probs * (grad_probs - row_delta[:, :, None])).astype(bf16)
    grad_value = jnp.einsum(
        "hqk,qhd->khd", probs_low, grad_attended, preferred_element_type=f32
    ).astype(bf16)
    grad_query = (
        jnp.einsum("hqk,khd->qhd", grad_scores, key, preferred_element_type=f32) * scale
    )
    grad_key = (
        jnp.einsum("hqk,qhd->khd", grad_scores, query, preferred_element_type=f32)
        * scale
    )
    grad_query = rope(grad_query, cosine, -sine).reshape(seq, head_cols)
    grad_key = rope(grad_key, cosine, -sine).reshape(seq, head_cols)
    means = jnp.stack(
        [
            jnp.sum(query_pre * own_q_gain * grad_query, axis=-1),
            jnp.sum(key_pre * own_k_gain * grad_key, axis=-1),
        ]
    )
    means = lax.psum(means, "blk") / width
    grad_q_gain = jnp.sum(grad_query * query_pre * r_q, axis=0)
    grad_k_gain = jnp.sum(grad_key * key_pre * r_k, axis=0)
    grad_query_pre = norm_back(query_pre, r_q, own_q_gain, grad_query, means[0][:, None])
    grad_key_pre = norm_back(key_pre, r_k, own_k_gain, grad_key, means[1][:, None])
    grad_qkv = jnp.concatenate(
        [
            grad_query_pre.astype(bf16),
            grad_key_pre.astype(bf16),
            grad_value.reshape(seq, head_cols),
        ],
        axis=1,
    )
    grad_w = dot_tn(normed_row, grad_qkv).astype(bf16)
    grad_w = lax.psum_scatter(grad_w, "row", scatter_dimension=0, tiled=True)
    grad_w = grad_w.reshape(blocks, wrows, 3 * head_cols)
    grad_w = lax.all_to_all(grad_w, "blk", split_axis=0, concat_axis=0, tiled=True)
    grad_w = grad_w.reshape(blocks, wrows, 3, head_cols).transpose(2, 1, 0, 3)
    grad_w = grad_w.reshape(3, wrows, width).astype(f32)
    grad_normed = dot_nt(grad_qkv, qkv_cols).astype(bf16)
    grad_normed = lax.psum_scatter(
        grad_normed, "blk", scatter_dimension=0, tiled=True
    ).astype(f32)
    grad_gain_attn = jnp.sum(grad_normed * x * r_attn, axis=0)
    input_grad = grad_mid + norm_back(
        x,
        r_attn,
        gain_attn,
        grad_normed,
        jnp.mean(x * gain_attn * grad_normed, axis=-1, keepdims=True),
    )

    def placed(vector):
        return lax.dynamic_update_slice_in_dim(
            jnp.zeros((width,), f32), vector, blk * head_cols, axis=0
        )

    small_grads = jnp.concatenate(
        [
            grad_router,
            grad_gain_attn[:, None],
            placed(grad_q_gain)[:, None],
            placed(grad_k_gain)[:, None],
            grad_gain_expert[:, None],
        ],
        axis=1,
    )
    small_grads = lax.psum_scatter(small_grads, BOTH, scatter_dimension=0, tiled=True)
    return (
        layer_out[None],
        input_grad[None],
        small_grads[:, experts],
        small_grads[:, experts + 1],
        small_grads[:, experts + 2],
        small_grads[:, experts + 3],
        grad_w[0],
        grad_w[1],
        grad_w[2],
        grad_output_w,
        small_grads[:, :experts],
        grad_gate_local[None],
        grad_up_local[None],
        grad_down_local[None],
    )


def solution(mesh):
    tokens3 = P("row", "blk", None)
    vector, matrix, cube = P(BOTH), P(BOTH, None), P(BOTH, None, None)
    own = (mesh.shape["row"], mesh.shape["blk"]) == (4, 8)
    return jax.shard_map(
        own_mesh_body if own else any_mesh_body,
        mesh=mesh,
        in_specs=(
            tokens3,
            P("row", "blk"),
            tokens3,
            vector,
            vector,
            vector,
            vector,
            matrix,
            matrix,
            matrix,
            matrix,
            matrix,
            cube,
            cube,
            cube,
            tokens3,
        ),
        out_specs=(
            tokens3,
            tokens3,
            vector,
            vector,
            vector,
            vector,
            matrix,
            matrix,
            matrix,
            matrix,
            matrix,
            cube,
            cube,
            cube,
        ),
        check_vma=False,
    )
```

```python
import functools
import math

import jax
import jax.numpy as jnp
from jax import lax
from jax.experimental import pallas as pl
from jax.experimental.pallas import tpu as pltpu
from jax.sharding import PartitionSpec as P

HEADS = 16
HEAD_DIM = 128
TOP_K = 8

epsilon = 1e-05
masked_score = -1e30
BOTH = ("row", "blk")
MESH = pl.DeviceIdType.MESH
bf16 = jnp.bfloat16
f32 = jnp.float32
EXTRA = 128
ZCOLS = 256


def dot(a, b):
    return jnp.dot(a, b, preferred_element_type=f32)


def dot_nt(a, b):
    return lax.dot_general(a, b, (((1,), (1,)), ((), ())), preferred_element_type=f32)


def dot_tn(a, b):
    return lax.dot_general(a, b, (((0,), (0,)), ((), ())), preferred_element_type=f32)


def place():
    row, blk = lax.axis_index("row"), lax.axis_index("blk")
    return row, blk // 2, blk % 2


def partners():
    row, z, c = place()
    blk = z * 2 + c
    return {
        "sib": (row, z * 2 + (1 - c)),
        "x": (row ^ 1, blk),
        "y": (row ^ 2, blk),
        "z1": (row, ((z + 1) % 4) * 2 + c),
        "z2": (row, ((z + 2) % 4) * 2 + c),
        "z3": (row, ((z + 3) % 4) * 2 + c),
    }


def remote(src, dst, send, recv, to):
    return pltpu.make_async_remote_copy(
        src_ref=src,
        dst_ref=dst,
        send_sem=send,
        recv_sem=recv,
        device_id=to,
        device_id_type=MESH,
    )


def greet(targets):
    barrier = pltpu.get_barrier_semaphore()
    for to in targets:
        pl.semaphore_signal(barrier, inc=1, device_id=to, device_id_type=MESH)
    pl.semaphore_wait(barrier, len(targets))


def moe_kernel(
    steps,
    x_ref,
    c_ref,
    mask_ref,
    router_ref,
    gate_ref,
    up_ref,
    down_ref,
    xall,
    out_ref,
    back_ref,
    dwg_out,
    dwu_out,
    dwd_out,
    wgu_ref,
    wd_ref,
    dwg_ref,
    dwu_ref,
    dwd_ref,
    xbuf,
    cbuf,
    hbuf,
    gbuf,
    po,
    pb,
    ro,
    rb,
    so,
    sb,
    p1ao,
    p1bo,
    p1ab,
    p1bb,
    p2o,
    p2b,
    zo,
    zb,
    gz,
    gp1,
    gp2,
    ag_send,
    ag_recv,
    rs_send,
    rs_recv,
    load_sem,
    weight_sem,
):
    row, z, c = place()
    to = partners()
    width = x_ref.shape[-1]
    half = width // 2
    hidden = wd_ref.shape[0]
    me = row * 8 + z * 2 + c
    expert = me // 2

    weights = [
        pltpu.make_async_copy(src, dst, weight_sem.at[k])
        for k, (src, dst) in enumerate(
            (
                (gate_ref, wgu_ref.at[:, pl.ds(0, hidden)]),
                (up_ref, wgu_ref.at[:, pl.ds(hidden, hidden)]),
                (down_ref, wd_ref),
            )
        )
    ]
    sums = [
        pltpu.make_async_copy(src, dst, weight_sem.at[3 + k])
        for k, (src, dst) in enumerate(
            ((dwg_ref, dwg_out), (dwu_ref, dwu_out), (dwd_ref, dwd_out))
        )
    ]
    for cp in weights:
        cp.start()
    greet(list(to.values()))

    def ag(j, k, src, dst, who):
        return remote(src, dst, ag_send.at[j, k], ag_recv.at[j, k], to[who])

    def own_copy(j):
        return pltpu.make_async_copy(
            x_ref.at[j], xall.at[j, row, z, c], load_sem.at[2 + j % 4]
        )

    def z_copies(j):
        slot = xall.at[j, row, z, c]
        return [ag(j, k, x_ref.at[j], slot, "z%d" % (k + 1)) for k in range(3)]

    def line_copies(j):
        line = xall.at[j, row, :, c]
        return [
            ag(j, 3, line, line, "x"),
            ag(j, 4, line, line, "y"),
            ag(j, 5, line, line, "sib"),
        ]

    def relay_copies(j):
        a = xall.at[j, row ^ 1, :, c, :, pl.ds(0, half)]
        b = xall.at[j, row ^ 2, :, c, :, pl.ds(half, half)]
        s1 = xall.at[j, row ^ 1, :, c]
        s2 = xall.at[j, row ^ 2, :, c]
        return [
            ag(j, 6, a, a, "y"),
            ag(j, 7, b, b, "x"),
            ag(j, 8, s1, s1, "sib"),
            ag(j, 9, s2, s2, "sib"),
        ]

    def last_copies(j):
        s3 = xall.at[j, row ^ 3, :, c]
        return [ag(j, 10, s3, s3, "sib")]

    def ag_z(j):
        own_copy(j).start()
        for cp in z_copies(j):
            cp.start()

    def ag_xy(j):
        own_copy(j).wait()
        for cp in z_copies(j):
            cp.wait_recv()
        for cp in line_copies(j):
            cp.start()

    def ag_rel(j):
        for cp in line_copies(j)[:2]:
            cp.wait_recv()
        for cp in relay_copies(j):
            cp.start()

    def ag_fin(j):
        for cp in relay_copies(j)[:2]:
            cp.wait_recv()
        for cp in last_copies(j):
            cp.start()

    def loads(j):
        return [
            pltpu.make_async_copy(xall.at[j], xbuf.at[j % 2], load_sem.at[0]),
            pltpu.make_async_copy(c_ref.at[j], cbuf.at[j % 2], load_sem.at[1]),
        ]

    def ag_done(j):
        line_copies(j)[2].wait_recv()
        for cp in relay_copies(j)[2:] + last_copies(j):
            cp.wait_recv()
        for cp in loads(j):
            cp.start()

    def ag_sent(j):
        for cp in z_copies(j) + line_copies(j) + relay_copies(j) + last_copies(j):
            cp.wait_send()

    arrays = (
        (po, ro, so, p1ao, p1bo, p2o, zo, out_ref),
        (pb, rb, sb, p1ab, p1bb, p2b, zb, back_ref),
    )
    near_z, near_cut = ZCOLS, ZCOLS // 2
    mid = near_z + p1ao.shape[-1]

    def rs(i, q, k, src, dst, who):
        s = i % 2
        return remote(src, dst, rs_send.at[q, s, k], rs_recv.at[q, s, k], to[who])

    def rs_sib_copy(q, i):
        p, r = arrays[q][:2]
        return rs(i, q, 0, p.at[:, :, 1 - c], r.at[i % 2], "sib")

    def p1_copies(q, i):
        p, r, s, p1a, p1b, p2, zz, out = arrays[q]
        part = s.at[i % 2, row ^ 3]
        rest = p.shape[-1] - mid
        return [
            rs(i, q, 1, part.at[:, :, pl.ds(near_z, mid - near_z)], p1a.at[i % 2], "y"),
            rs(i, q, 2, part.at[:, :, pl.ds(mid, rest)], p1b.at[i % 2], "x"),
        ]

    def p2_copies(q, i):
        p, r, s, p1a, p1b, p2, zz, out = arrays[q]
        cols = pl.ds(near_z, p.shape[-1] - near_z)
        return [
            rs(i, q, 3, s.at[i % 2, row ^ 1, :, :, cols], p2.at[i % 2, 0], "x"),
            rs(i, q, 4, s.at[i % 2, row ^ 2, :, :, cols], p2.at[i % 2, 1], "y"),
        ]

    def rsz_copies(q, i):
        p, r, s, p1a, p1b, p2, zz, out = arrays[q]
        cols = pl.ds(near_z, p.shape[-1] - near_z)
        return [
            rs(
                i,
                q,
                5 + k,
                s.at[i % 2, row, (z + k + 1) % 4, :, cols],
                zz.at[i % 2, k],
                "z%d" % (k + 1),
            )
            for k in range(3)
        ]

    def first_z_copies(q, i):
        s = arrays[q][2]
        return [
            rs(
                i,
                q,
                8 + k,
                s.at[i % 2, :, (z + k + 1) % 4, :, pl.ds(0, near_z)],
                gz.at[q, i % 2, k],
                "z%d" % (k + 1),
            )
            for k in range(3)
        ]

    def first_p1_copies(q, i):
        part = arrays[q][2].at[i % 2, row ^ 3, z]
        return [
            rs(i, q, 11, part.at[:, pl.ds(0, near_cut)], gp1.at[q, i % 2, 0], "y"),
            rs(i, q, 12, part.at[:, pl.ds(near_cut, near_cut)], gp1.at[q, i % 2, 1], "x"),
        ]

    def first_p2_copies(q, i):
        s = arrays[q][2]
        cols = pl.ds(0, near_z)
        return [
            rs(i, q, 13, s.at[i % 2, row ^ 1, z, :, cols], gp2.at[q, i % 2, 0], "x"),
            rs(i, q, 14, s.at[i % 2, row ^ 2, z, :, cols], gp2.at[q, i % 2, 1], "y"),
        ]

    def rs_sib(q, i):
        rs_sib_copy(q, i).start()

    def rs_p1(q, i):
        p, r, s, p1a, p1b, p2, zz, out = arrays[q]
        cp = rs_sib_copy(q, i)
        cp.wait_recv()

        @pl.loop(0, 4)
        def _(a):
            s[i % 2, a] = (
                p[a, :, c].astype(f32) + r[i % 2, a].astype(f32)
            ).astype(bf16)

        cp.wait_send()
        for cp in p1_copies(q, i) + first_z_copies(q, i):
            cp.start()

    def rs_p2(q, i):
        p, r, s, p1a, p1b, p2, zz, out = arrays[q]
        rest = p.shape[-1] - mid
        copies = p1_copies(q, i)
        copies[0].wait_recv()
        at = s.at[i % 2, row ^ 1, :, :, pl.ds(near_z, mid - near_z)]
        at[...] = added(at[...], p1a[i % 2])
        out_copies = p2_copies(q, i)
        out_copies[0].start()
        copies[1].wait_recv()
        at = s.at[i % 2, row ^ 2, :, :, pl.ds(mid, rest)]
        at[...] = added(at[...], p1b[i % 2])
        out_copies[1].start()
        for cp in first_z_copies(q, i):
            cp.wait_recv()
        at = s.at[i % 2, :, z, :, pl.ds(0, near_z)]
        at[...] = added(at[...], gz[q, i % 2, 0], gz[q, i % 2, 1], gz[q, i % 2, 2])
        for cp in first_p1_copies(q, i):
            cp.start()

    def rs_z(q, i):
        p, r, s, p1a, p1b, p2, zz, out = arrays[q]
        for cp in p2_copies(q, i):
            cp.wait_recv()
        at = s.at[i % 2, row, :, :, pl.ds(near_z, p.shape[-1] - near_z)]
        at[...] = added(at[...], p2[i % 2, 0], p2[i % 2, 1])
        for cp in rsz_copies(q, i):
            cp.start()
        for cp in first_p1_copies(q, i):
            cp.wait_recv()
        at = s.at[i % 2, row ^ 1, z, :, pl.ds(0, near_cut)]
        at[...] = added(at[...], gp1[q, i % 2, 0])
        at = s.at[i % 2, row ^ 2, z, :, pl.ds(near_cut, near_cut)]
        at[...] = added(at[...], gp1[q, i % 2, 1])
        for cp in first_p2_copies(q, i):
            cp.start()

    def rs_fin(q, i):
        p, r, s, p1a, p1b, p2, zz, out = arrays[q]
        copies = rsz_copies(q, i)
        for cp in copies:
            cp.wait_recv()
        total = s[i % 2, row, z, :, near_z:].astype(f32)
        for k in range(3):
            total = total + zz[i % 2, k].astype(f32)
        out[i, :, near_z:] = total
        first = first_p2_copies(q, i)
        for cp in first:
            cp.wait_recv()
        total = s[i % 2, row, z, :, :near_z].astype(f32)
        for k in range(2):
            total = total + gp2[q, i % 2, k].astype(f32)
        out[i, :, :near_z] = total
        for cp in copies + p2_copies(q, i) + p1_copies(q, i):
            cp.wait_send()
        for cp in first + first_p1_copies(q, i) + first_z_copies(q, i):
            cp.wait_send()

    lanes = po.shape[3]
    rows_here = 16 * lanes
    cut = 512

    def tile(i, t):
        s = i % 2
        xt = xbuf[s, 2 * t : 2 * t + 2].reshape(rows_here, width)
        mask = mask_ref[i, t * rows_here : (t + 1) * rows_here, :].astype(f32)
        logits = dot(xt, router_ref[...])[:, : mask.shape[-1]]
        logits = jnp.where(mask > 0, logits, masked_score)
        top = jnp.max(logits, axis=-1, keepdims=True)
        raised = jnp.where(mask > 0, jnp.exp(logits - top), 0.0)
        lane = lax.broadcasted_iota(jnp.int32, raised.shape, 1)
        gate = jnp.sum(
            jnp.where(lane == expert, raised, 0.0), axis=-1, keepdims=True
        ) / jnp.sum(raised, axis=-1, keepdims=True)
        both = dot(xt, wgu_ref[...])
        gp, up = both[:, :hidden], both[:, hidden:]
        sig = jax.nn.sigmoid(gp)
        silu = gp * sig
        hid = (silu * up).astype(bf16)
        hbuf[t * rows_here : (t + 1) * rows_here, :] = hid
        slope = up * sig * (1.0 + gp * (1.0 - sig))
        dots = jnp.zeros((rows_here, 1), f32)
        ghid = jnp.zeros((rows_here, hidden), f32)
        for n in range(width // cut):
            cols = slice(n * cut, (n + 1) * cut)
            wd = wd_ref[:, cols]
            part = dot(hid, wd).astype(bf16).astype(f32)
            cf = cbuf[s, 2 * t : 2 * t + 2, :, :, :, cols]
            shape = cf.shape
            cf = cf.reshape(rows_here, cut).astype(f32)
            dots = dots + jnp.sum(part * cf, axis=-1, keepdims=True)
            po[2 * t : 2 * t + 2, :, :, :, cols] = (
                (gate * part).astype(bf16).reshape(shape)
            )
            gpart = (gate * cf).astype(bf16)
            cbuf[s, 2 * t : 2 * t + 2, :, :, :, cols] = gpart.reshape(shape)
            ghid = ghid + dot_nt(gpart, wd)
        dgp = (ghid * slope).astype(bf16)
        dup = (ghid * silu).astype(bf16)
        grads = jnp.concatenate([dgp, dup], axis=1)
        gbuf[t * rows_here : (t + 1) * rows_here, :] = grads
        for n in range(width // cut):
            cols = slice(n * cut, (n + 1) * cut)
            bk = dot_nt(grads, wgu_ref[cols, :]).astype(bf16)
            pb[2 * t : 2 * t + 2, :, :, :, cols] = bk.reshape(shape)
        high = dots.astype(bf16).astype(f32)
        low = dots - high
        lane = lax.broadcasted_iota(jnp.int32, (rows_here, EXTRA), 1)
        extra = jnp.where(lane == me, high, jnp.where(lane == me + 64, low, 0.0))
        pb[2 * t : 2 * t + 2, :, :, :, width:] = extra.astype(bf16).reshape(
            shape[:-1] + (EXTRA,)
        )

    def weight_grads(i):
        s = i % 2
        every = 2 * rows_here

        @pl.loop(0, width // 256)
        def _(n):
            cols = pl.ds(pl.multiple_of(n * 256, 256), 256)
            xt = xbuf[s, :, :, :, :, cols].reshape(every, 256)
            r = dot_tn(xt, gbuf[...])
            dwg_ref[cols, :] += r[:, :hidden]
            dwu_ref[cols, :] += r[:, hidden:]

        @pl.loop(0, width // cut)
        def _(n):
            cols = pl.ds(pl.multiple_of(n * cut, cut), cut)
            gpart = cbuf[s, :, :, :, :, cols].reshape(every, cut)
            dwd_ref[:, cols] += dot_tn(hbuf[...], gpart)

    ag_z(0)
    ag_z(1)
    dwg_ref[...] = jnp.zeros_like(dwg_ref)
    dwu_ref[...] = jnp.zeros_like(dwu_ref)
    dwd_ref[...] = jnp.zeros_like(dwd_ref)
    for cp in weights:
        cp.wait()
    ag_xy(0)
    ag_z(2)
    ag_xy(1)
    ag_rel(0)
    ag_fin(0)
    ag_rel(1)
    ag_done(0)
    ag_fin(1)

    @pl.loop(0, steps + 2)
    def _(i):
        def when(low, high, *work):
            @pl.when((i >= low) & (i < high))
            def _():
                for f in work:
                    f()

        @pl.when(i + 3 < steps)
        def _():
            ag_z(i + 3)

        @pl.when(i + 2 < steps)
        def _():
            ag_xy(i + 2)

        when(1, steps + 1, lambda: rs_p2(0, i - 1))
        when(2, steps + 2, lambda: rs_z(1, i - 2))

        @pl.when(i < steps)
        def _():
            for cp in loads(i):
                cp.wait()
            tile(i, 0)

        @pl.when(i + 2 < steps)
        def _():
            ag_rel(i + 2)

        when(1, steps + 1, lambda: rs_p2(1, i - 1))
        when(2, steps + 2, lambda: rs_fin(0, i - 2))

        @pl.when(i < steps)
        def _():
            tile(i, 1)
            rs_sib(0, i)
            rs_sib(1, i)

        @pl.when(i + 2 < steps)
        def _():
            ag_fin(i + 2)

        when(0, steps, lambda: rs_p1(0, i))
        when(1, steps + 1, lambda: rs_z(0, i - 1))
        when(2, steps + 2, lambda: rs_fin(1, i - 2))
        when(0, steps, lambda: rs_p1(1, i))

        @pl.when(i < steps)
        def _():
            weight_grads(i)

        @pl.when(i == steps - 1)
        def _():
            for cp in sums:
                cp.start()

        @pl.when(i + 1 < steps)
        def _():
            ag_done(i + 1)

    @pl.loop(0, steps)
    def _(j):
        ag_sent(j)

    for cp in sums:
        cp.wait()


def moe(expert_in, upstream_all, mask, router, gate, up, down):
    tokens, width = expert_in.shape
    hidden = down.shape[0]
    steps = tokens // 16
    wide = width + EXTRA
    mid = ZCOLS + (width - ZCOLS) // 2
    any_, vm = pl.BlockSpec(memory_space=pl.ANY), pl.BlockSpec(memory_space=pltpu.VMEM)
    dma = pltpu.SemaphoreType.DMA
    router = jnp.pad(router, ((0, 0), (0, 128 - router.shape[1])))
    results = pl.pallas_call(
        functools.partial(moe_kernel, steps),
        out_shape=(
            jax.ShapeDtypeStruct((steps, 4, 4, 2, 16, width), bf16),
            jax.ShapeDtypeStruct((steps, 16, width), f32),
            jax.ShapeDtypeStruct((steps, 16, wide), f32),
            jax.ShapeDtypeStruct((width, hidden), f32),
            jax.ShapeDtypeStruct((width, hidden), f32),
            jax.ShapeDtypeStruct((hidden, width), f32),
        ),
        in_specs=[any_, any_, vm, vm, any_, any_, any_],
        out_specs=(any_, vm, vm, any_, any_, any_),
        scratch_shapes=[
            pltpu.VMEM((width, 2 * hidden), bf16),
            pltpu.VMEM((hidden, width), bf16),
            pltpu.VMEM((width, hidden), f32),
            pltpu.VMEM((width, hidden), f32),
            pltpu.VMEM((hidden, width), f32),
            pltpu.VMEM((2, 4, 4, 2, 16, width), bf16),
            pltpu.VMEM((2, 4, 4, 2, 16, width), bf16),
            pltpu.VMEM((512, hidden), bf16),
            pltpu.VMEM((512, 2 * hidden), bf16),
            pltpu.VMEM((4, 4, 2, 16, width), bf16),
            pltpu.VMEM((4, 4, 2, 16, wide), bf16),
            pltpu.VMEM((2, 4, 4, 16, width), bf16),
            pltpu.VMEM((2, 4, 4, 16, wide), bf16),
            pltpu.VMEM((2, 4, 4, 16, width), bf16),
            pltpu.VMEM((2, 4, 4, 16, wide), bf16),
            pltpu.VMEM((2, 4, 16, mid - ZCOLS), bf16),
            pltpu.VMEM((2, 4, 16, width - mid), bf16),
            pltpu.VMEM((2, 4, 16, mid - ZCOLS), bf16),
            pltpu.VMEM((2, 4, 16, wide - mid), bf16),
            pltpu.VMEM((2, 2, 4, 16, width - ZCOLS), bf16),
            pltpu.VMEM((2, 2, 4, 16, wide - ZCOLS), bf16),
            pltpu.VMEM((2, 3, 16, width - ZCOLS), bf16),
            pltpu.VMEM((2, 3, 16, wide - ZCOLS), bf16),
            pltpu.VMEM((2, 2, 3, 4, 16, ZCOLS), bf16),
            pltpu.VMEM((2, 2, 2, 16, ZCOLS // 2), bf16),
            pltpu.VMEM((2, 2, 2, 16, ZCOLS), bf16),
            dma((steps, 11)),
            dma((steps, 11)),
            dma((2, 2, 15)),
            dma((2, 2, 15)),
            dma((6,)),
            dma((6,)),
        ],
        compiler_params=pltpu.CompilerParams(
            collective_id=1, has_side_effects=True, vmem_limit_bytes=60 * 2**20
        ),
        cost_estimate=pl.CostEstimate(
            flops=78 * 10**9, bytes_accessed=10**8, transcendentals=0
        ),
    )(
        expert_in.reshape(steps, 16, width),
        upstream_all,
        mask,
        router,
        gate,
        up,
        down,
    )
    return results[1:]


class Copies:
    def __init__(self, send, recv):
        self.send, self.recv, self.count, self.made = send, recv, 0, []

    def __call__(self, src, dst, who):
        k = self.count
        self.count += 1
        return remote(src, dst, self.send.at[k], self.recv.at[k], who)


def row_mates():
    row, z, c = place()
    mates = [(row, z * 2 + (1 - c))]
    for k in (1, 3, 2):
        for flip in (0, 1):
            mates.append((row, ((z + k) % 4) * 2 + (c ^ flip)))
    return mates


def gather_stages(copy, src, slots, cut, own_sem):
    row, z, c = place()
    to = partners()
    own = slots.at[row, z, c]
    line = slots.at[row, :, c]
    width = src.shape[-1]
    if cut:
        a = slots.at[row ^ 1, :, c, :, pl.ds(0, cut)]
        b = slots.at[row ^ 2, :, c, :, pl.ds(cut, width - cut)]
    else:
        a = slots.at[row ^ 1, pl.ds(0, 2), c]
        b = slots.at[row ^ 2, pl.ds(2, 2), c]
    s1, s2, s3 = (slots.at[row ^ k, :, c] for k in (1, 2, 3))
    local = pltpu.make_async_copy(src, own, own_sem)
    along_z = [copy(src, own, to["z%d" % k]) for k in (1, 3, 2)]
    over = [copy(line, line, to[k]) for k in ("x", "y", "sib")]
    relay = [copy(a, a, to["y"]), copy(b, b, to["x"])]
    inside = [copy(s1, s1, to["sib"]), copy(s2, s2, to["sib"])]
    last = [copy(s3, s3, to["sib"])]

    def start(some):
        for cp in some:
            cp.start()

    def arrived(some):
        for cp in some:
            cp.wait_recv()

    def first():
        local.start()
        start(along_z)

    def second():
        local.wait()
        arrived(along_z)
        start(over)

    def third():
        arrived(over[:2])
        start(relay + inside)

    def fourth():
        arrived(relay)
        start(last)

    def fifth():
        arrived(over[2:] + inside + last)
        for cp in along_z + over + relay + inside + last:
            cp.wait_send()

    return first, second, third, fourth, fifth


def norm_rows(v):
    return lax.rsqrt(jnp.mean(v * v, axis=-1, keepdims=True) + epsilon)


def turned(v, cosine, sine):
    heads = []
    for h in range(v.shape[1] // HEAD_DIM):
        one = v[:, h * HEAD_DIM : (h + 1) * HEAD_DIM]
        heads.append(one * cosine + pltpu.roll(one, HEAD_DIM // 2, 1) * sine)
    return jnp.concatenate(heads, axis=1)


def row_pairs(cols):
    row = lax.broadcasted_iota(jnp.int32, (8, 2 * cols), 0)
    lane = lax.broadcasted_iota(jnp.int32, (8, 2 * cols), 1)
    return jnp.where((lane // cols) == row, 1.0, 0.0).astype(f32)


def sums_by_row(pairs, v):
    return lax.dot_general(
        pairs,
        v,
        (((1,), (1,)), ((), ())),
        precision=lax.Precision.HIGHEST,
        preferred_element_type=f32,
    )


def slot_stages(copy, src, slot, k, cut, own_sem):
    row, z, c = place()
    to = partners()
    there = (z + k) % 4
    own = slot(row, z)
    s0, s1, s2, s3 = (slot(row ^ r, there) for r in range(4))
    width = src.shape[-1]
    a = slot(row ^ 1, there).at[:, :, pl.ds(0, cut)]
    b = slot(row ^ 2, there).at[:, :, pl.ds(cut, width - cut)]
    if k:
        along_z = [copy(src, own, to["z%d" % (4 - k)])]
        over = [copy(s0, s0, to[w]) for w in ("x", "y", "sib")]
    else:
        along_z = []
        local = pltpu.make_async_copy(src, own, own_sem)
        over = [copy(src, own, to[w]) for w in ("x", "y", "sib")]
    relay = [copy(a, a, to["y"]), copy(b, b, to["x"])]
    inside = [copy(s1, s1, to["sib"]), copy(s2, s2, to["sib"])]
    last = [copy(s3, s3, to["sib"])]

    def start(some):
        for cp in some:
            cp.start()

    def arrived(some):
        for cp in some:
            cp.wait_recv()

    def first():
        if k:
            start(along_z)
        else:
            local.start()

    def second():
        arrived(along_z)
        start(over)

    def third():
        arrived(over[:2])
        start(relay + inside)

    def fourth():
        arrived(relay)
        start(last)

    def fifth():
        if not k:
            local.wait()
        arrived(over[2:] + inside + last)
        for cp in along_z + over + relay + inside + last:
            cp.wait_send()

    return first, second, third, fourth, fifth


def front_kernel(
    h_ref,
    wq_ref,
    wk_ref,
    wv_ref,
    wo_ref,
    up_ref,
    pack_ref,
    cos_ref,
    sin_ref,
    woall,
    call,
    packs,
    normed_out,
    wcols_out,
    low_out,
    pre_out,
    att_out,
    stat_ref,
    home_ref,
    mid_ref,
    expert_ref,
    hrow,
    normed_ref,
    wcols,
    low_ref,
    pre_ref,
    att_ref,
    wo_buf,
    gains_ref,
    sums_ref,
    sums_land,
    att_low,
    send,
    recv,
    local_sem,
):
    row, z, c = place()
    blk = z * 2 + c
    to = partners()
    mates = row_mates()
    greet(mates + [to["x"], to["y"]])
    copy = Copies(send, recv)
    cols_here = wcols.shape[3] // 3
    tokens, width = h_ref.shape
    seq = 8 * tokens
    wrows = wq_ref.shape[0]

    pack_stages = gather_stages(copy, pack_ref, packs, 0, local_sem.at[0])
    parts = up_ref.shape[0] // 4
    streams = []
    for k in (0, 1, 3, 2):
        streams.append(
            slot_stages(
                copy,
                wo_ref,
                lambda r, q: woall.at[r, q, c],
                k,
                width // 2,
                local_sem.at[9 + len(streams)],
            )
        )
        for j in range(parts):
            part = pl.ds(j * 4, 4)
            streams.append(
                slot_stages(
                    copy,
                    up_ref.at[part],
                    lambda r, q, part=part: call.at[part, r, q, c],
                    k,
                    width // 2,
                    local_sem.at[9 + len(streams)],
                )
            )
    for_output = streams[:: parts + 1]
    for_upstream = [one for one in streams if one not in for_output]
    saves = [
        pltpu.make_async_copy(src, dst, local_sem.at[9 + len(streams) + k])
        for k, (src, dst) in enumerate(
            (
                (wcols, wcols_out),
                (normed_ref, normed_out),
                (pre_ref, pre_out),
                (low_ref, low_out),
                (att_ref, att_out),
            )
        )
    ]
    wo_load = pltpu.make_async_copy(woall, wo_buf, local_sem.at[9 + len(streams) + 5])
    ticks = [0]

    def tick():
        t = ticks[0]
        ticks[0] += 1
        for stage, lag in ((0, 0), (1, 1), (2, 2), (3, 3)):
            if 0 <= t - lag < len(streams):
                streams[t - lag][stage]()

    own_rows = pltpu.make_async_copy(h_ref, hrow.at[blk], local_sem.at[5])
    up_to, down_to = (row, blk + 2), (row, blk - 2)
    sib = to["sib"]
    own_sib = copy(h_ref, hrow.at[blk], sib)
    ups, downs = [], []
    for t in range(3):
        src = h_ref if t == 0 else hrow.at[blk - 2 * t]
        up = copy(src, hrow.at[blk - 2 * t], up_to)
        got = hrow.at[blk - 2 - 2 * t]
        ups.append((up, copy(got, got, sib), (z < 3) & (z >= t), z >= t + 1))
        src = h_ref if t == 0 else hrow.at[blk + 2 * t]
        down = copy(src, hrow.at[blk + 2 * t], down_to)
        got = hrow.at[blk + 2 + 2 * t]
        downs.append((down, copy(got, got, sib), (z > 0) & (z + t <= 3), z + t + 1 <= 3))

    def line_start(t):
        for cp, hand, sends, gets in (ups[t], downs[t]):
            pl.when(sends)(cp.start)

    def line_arrived(t):
        for cp, hand, sends, gets in (ups[t], downs[t]):

            @pl.when(gets)
            def _():
                cp.wait_recv()
                hand.start()

    def line_done():
        own_rows.wait()
        own_sib.wait()
        for t in range(3):
            for cp, hand, sends, gets in (ups[t], downs[t]):
                pl.when(sends)(cp.wait_send)
                pl.when(gets)(hand.wait)

    def columns(b):
        return pl.ds(pl.multiple_of(b * cols_here, cols_here), cols_here)

    own_cols, col_copies = [], []
    for j, w in enumerate((wq_ref, wk_ref, wv_ref)):
        there = pl.ds(j * cols_here, cols_here)
        own_cols.append(
            pltpu.make_async_copy(
                w.at[:, columns(blk)], wcols.at[row, blk, :, there], local_sem.at[6 + j]
            )
        )
        for mate in mates:
            col_copies.append(
                copy(w.at[:, columns(mate[1])], wcols.at[row, blk, :, there], mate)
            )
    half = wcols.shape[1] // 2
    col_over = [copy(wcols.at[row], wcols.at[row], to[k]) for k in ("x", "y")]
    a = wcols.at[row ^ 1, pl.ds(0, half)]
    b = wcols.at[row ^ 2, pl.ds(half, half)]
    col_relay = [copy(a, a, to["y"]), copy(b, b, to["x"])]
    sum_copies = [
        copy(sums_ref, sums_land.at[k], mate) for k, mate in enumerate(mates)
    ]
    home_copies = [
        copy(att_low.at[mate[1]], home_ref.at[:, columns(blk)], mate) for mate in mates
    ]

    def start(some):
        for cp in some:
            cp.start()

    def arrived(some):
        for cp in some:
            cp.wait_recv()

    own_rows.start()
    start(own_cols)
    line_start(0)
    own_sib.start()
    tick()
    tick()
    pack_stages[0]()
    start(col_copies)
    tick()
    pack_stages[1]()
    tick()
    line_arrived(0)
    line_start(1)
    tick()
    pack_stages[2]()
    for cp in own_cols:
        cp.wait()
    arrived(col_copies)
    start(col_over)
    pack_stages[3]()
    line_arrived(1)
    line_start(2)
    tick()
    arrived(col_over)
    start(col_relay)
    tick()
    line_arrived(2)
    pack_stages[4]()
    arrived(col_relay)
    line_done()
    tick()
    start(saves[:1])

    pieces = []
    for r in range(4):
        for q in range(4):
            pieces.append(
                packs[r, q, 0, 48:64, :].astype(f32) + packs[r, q, 1, 48:64, :].astype(f32)
            )
    gains_ref[...] = jnp.concatenate(pieces, axis=1)[0:8]
    gain_attn = gains_ref[0:1, :]
    segments = jnp.concatenate(
        [
            packs[row, q, k, 16:32, :].astype(f32)[0:1]
            for q in range(4)
            for k in range(2)
        ],
        axis=1,
    )
    pairs = row_pairs(cols_here)
    block = 256
    blocks = seq // block

    for t in range(blocks):
        rows = slice(t * block, (t + 1) * block)
        per = block // tokens
        v = hrow[t * per : (t + 1) * per].reshape(block, width).astype(f32)
        normed = (v * norm_rows(v) * gain_attn).astype(bf16)
        normed_ref[rows, :] = normed
        pre = dot(normed, wcols[...].reshape(width, 3 * cols_here))
        pre_ref[rows, :] = pre[:, : 2 * cols_here]
        low_ref[rows, 2 * cols_here :] = pre[:, 2 * cols_here :].astype(bf16)
        both = pre[:, : 2 * cols_here]
        squares = sums_by_row(pairs, both * both)
        sums_ref[2 * t : 2 * t + 2, :] = squares[0:2]
        if t % 2:
            tick()
    start(saves[1:3])
    start(sum_copies)
    tick()
    total = sums_ref[...]
    for k, cp in enumerate(sum_copies):
        cp.wait_recv()
        total = total + sums_land[k]
    scales = lax.rsqrt(total * (1.0 / width) + epsilon)
    gain_q = gains_ref[1:2, columns(blk)]
    gain_k = gains_ref[2:3, columns(blk)]
    for t in range(blocks):
        rows = slice(t * block, (t + 1) * block)
        turned_scales = jnp.concatenate(
            [scales[2 * t : 2 * t + 2], segments[:, rows], jnp.zeros((5, block), f32)],
            axis=0,
        ).T
        stat_ref[rows, :] = jnp.concatenate(
            [turned_scales, jnp.zeros((block, 120), f32)], axis=1
        )
        cosine, sine = cos_ref[rows, :], sin_ref[rows, :]
        q = pre_ref[rows, :cols_here] * turned_scales[:, 0:1] * gain_q
        low_ref[rows, :cols_here] = turned(q, cosine, sine).astype(bf16)
        k = pre_ref[rows, cols_here : 2 * cols_here] * turned_scales[:, 1:2] * gain_k
        low_ref[rows, cols_here : 2 * cols_here] = turned(k, cosine, sine).astype(bf16)
    tick()

    for t in range(blocks):
        rows = slice(t * block, (t + 1) * block)
        keys = (t + 1) * block
        stat = stat_ref[rows, :]
        place_q = lax.broadcasted_iota(jnp.int32, (block, keys), 0) + t * block
        place_k = lax.broadcasted_iota(jnp.int32, (block, keys), 1)
        allowed = (place_k <= place_q) & (segments[:, :keys] == stat[:, 2:3])
        lane = lax.broadcasted_iota(jnp.int32, stat.shape, 1)
        for h in range(cols_here // HEAD_DIM):
            cols = slice(h * HEAD_DIM, (h + 1) * HEAD_DIM)
            q = low_ref[rows, cols]
            k = low_ref[0:keys, cols_here + h * HEAD_DIM : cols_here + (h + 1) * HEAD_DIM]
            v = low_ref[
                0:keys, 2 * cols_here + h * HEAD_DIM : 2 * cols_here + (h + 1) * HEAD_DIM
            ]
            scores = jnp.where(allowed, dot_nt(q, k) * HEAD_DIM**-0.5, masked_score)
            top = jnp.max(scores, axis=-1, keepdims=True)
            raised = jnp.where(allowed, jnp.exp(scores - top), 0.0)
            share = 1.0 / jnp.sum(raised, axis=-1, keepdims=True)
            out = dot((raised * share).astype(bf16), v)
            att_ref[rows, cols] = out
            per = block // tokens
            att_low[t * per : (t + 1) * per, :, cols] = out.astype(bf16).reshape(
                per, tokens, HEAD_DIM
            )
            stat = jnp.where(lane == 3 + h, top, jnp.where(lane == 5 + h, share, stat))
        stat_ref[rows, :] = stat
    start(saves[3:])
    home_ref[:, columns(blk)] = att_low[blk]
    start(home_copies)
    tick()
    while ticks[0] < len(streams) - parts + 3:
        tick()
    for stages in for_output:
        stages[4]()
    wo_load.start()
    arrived(home_copies)
    wo_load.wait()
    mid = hrow[blk].astype(f32)
    cut = 512
    for n in range(width // cut):
        cols = slice(n * cut, (n + 1) * cut)
        mid_ref[:, cols] = mid[:, cols] + dot(
            home_ref[...], wo_buf[:, :, :, :, :, cols].reshape(width, cut)
        )
    mid = mid_ref[...]
    expert_ref[...] = (mid * norm_rows(mid) * gains_ref[3:4, :]).astype(bf16)
    while ticks[0] < len(streams) + 3:
        tick()
    for stages in for_upstream:
        stages[4]()
    for cp in col_copies + col_over + col_relay + sum_copies + home_copies:
        cp.wait_send()
    for cp in saves:
        cp.wait()


def front(hidden, wq, wk, wv, wo, upstream, pack, cosine, sine):
    any_, vm = pl.BlockSpec(memory_space=pl.ANY), pl.BlockSpec(memory_space=pltpu.VMEM)
    tokens, width = hidden.shape
    wrows = wq.shape[0]
    seq, cols = 8 * tokens, width // 8
    dma = pltpu.SemaphoreType.DMA
    streams = 4 * (1 + tokens // 64)
    count = 11 + 9 * streams + 13 + 21 + 4 + 14
    shape = jax.ShapeDtypeStruct
    return pl.pallas_call(
        front_kernel,
        out_shape=(
            shape((4, 4, 2, wrows // 16, 16, width), bf16),
            shape((tokens // 16, 4, 4, 2, 16, width), bf16),
            shape((4, 4, 2) + pack.shape, bf16),
            shape((seq, width), bf16),
            shape((4, 8, wrows, 3 * cols), bf16),
            shape((seq, 3 * cols), bf16),
            shape((seq, 2 * cols), f32),
            shape((seq, cols), f32),
            shape((seq, 128), f32),
            shape((tokens, width), bf16),
            shape((tokens, width), f32),
            shape((tokens, width), bf16),
        ),
        in_specs=[any_] * 7 + [vm] * 2,
        out_specs=(any_, any_, vm) + (any_,) * 5 + (vm,) * 4,
        scratch_shapes=[
            pltpu.VMEM((8, tokens, width), bf16),
            pltpu.VMEM((seq, width), bf16),
            pltpu.VMEM((4, 8, wrows, 3 * cols), bf16),
            pltpu.VMEM((seq, 3 * cols), bf16),
            pltpu.VMEM((seq, 2 * cols), f32),
            pltpu.VMEM((seq, cols), f32),
            pltpu.VMEM((4, 4, 2, wrows // 16, 16, width), bf16),
            pltpu.VMEM((8, width), f32),
            pltpu.VMEM((8, seq // 4), f32),
            pltpu.VMEM((7, 8, seq // 4), f32),
            pltpu.VMEM((8, tokens, cols), bf16),
            dma((count,)),
            dma((count,)),
            dma((16 + streams,)),
        ],
        compiler_params=pltpu.CompilerParams(
            collective_id=2, has_side_effects=True, vmem_limit_bytes=56 * 2**20
        ),
        cost_estimate=pl.CostEstimate(
            flops=10**10, bytes_accessed=2 * 10**8, transcendentals=0
        ),
    )(
        hidden,
        wq,
        wk,
        wv,
        wo.reshape(-1, 16, width),
        upstream.reshape(-1, 16, width),
        pack,
        cosine,
        sine,
    )


def added(total, *extra):
    total = total.astype(f32)
    for one in extra:
        total = total + one.astype(f32)
    return total.astype(bf16)


def reduce_stages(copy, src, got, p1a, p1b, p2, land, out):
    row, z, c = place()
    to = partners()
    half = src.shape[-1] // 2

    def own(r):
        return src.at[r, :, c]

    inside = copy(src.at[:, :, 1 - c], got, to["sib"])
    far = [
        copy(own(row ^ 3).at[:, :, pl.ds(0, half)], p1a, to["y"]),
        copy(own(row ^ 3).at[:, :, pl.ds(half, half)], p1b, to["x"]),
    ]
    near = [
        copy(own(row ^ 1), p2.at[0], to["x"]),
        copy(own(row ^ 2), p2.at[1], to["y"]),
    ]
    home = [
        copy(src.at[row, (z + k) % 4, c], land.at[k - 1], to["z%d" % k])
        for k in (1, 3, 2)
    ]

    def first():
        inside.start()

    def second():
        inside.wait_recv()
        for k in (3, 1, 2, 0):
            at = own(row ^ k)
            at[...] = added(at[...], got[row ^ k])
            if k == 3:
                for cp in far:
                    cp.start()

    def third():
        far[0].wait_recv()
        at = own(row ^ 1).at[:, :, pl.ds(0, half)]
        at[...] = added(at[...], p1a[...])
        near[0].start()
        far[1].wait_recv()
        at = own(row ^ 2).at[:, :, pl.ds(half, half)]
        at[...] = added(at[...], p1b[...])
        near[1].start()

    def fourth():
        for cp in near:
            cp.wait_recv()
        at = own(row)
        at[...] = added(at[...], p2[0], p2[1])
        for cp in home:
            cp.start()

    def fifth():
        for cp in home:
            cp.wait_recv()
        total = src[row, z, c].astype(f32)
        for k in range(3):
            total = total + land[k].astype(f32)
        out[...] = total
        for cp in [inside] + far + near + home:
            cp.wait_send()

    return first, second, third, fourth, fifth


def back_kernel(
    ga_home,
    attended_ref,
    proj_ref,
    low_ref,
    pre_ref,
    att_ref,
    stat_ref,
    seg_ref,
    gain_ref,
    cos_ref,
    sin_ref,
    normed_in,
    wcols_in,
    small_ref,
    gn_out,
    q_out,
    k_out,
    v_out,
    wo_out,
    small_out,
    normed_ref,
    wcols,
    ga,
    dq_ref,
    dk_ref,
    dv_ref,
    grads_ref,
    sums_ref,
    sums_land,
    gn,
    gn_sib,
    gn_land,
    gw,
    gw_p1,
    gw_p2,
    gw_land,
    small,
    sm_sib,
    sm_p1a,
    sm_p1b,
    sm_p2,
    sm_land,
    dwo_ref,
    wo_got,
    wo_p1a,
    wo_p1b,
    wo_p2,
    wo_land,
    send,
    recv,
    local_sem,
):
    row, z, c = place()
    blk = z * 2 + c
    to = partners()
    mates = row_mates()
    greet(mates + [to["x"], to["y"]])
    copy = Copies(send, recv)
    tokens, width = ga_home.shape
    seq = 8 * tokens
    cols_here = att_ref.shape[1]
    wrows = wo_out.shape[0]
    scale = HEAD_DIM**-0.5
    block = 256
    blocks = seq // block
    per = block // tokens

    def start(some):
        for cp in some:
            cp.start()

    def arrived(some):
        for cp in some:
            cp.wait_recv()

    def columns(b):
        return pl.ds(pl.multiple_of(b * cols_here, cols_here), cols_here)

    streams = []
    for j in range(wrows // 16):
        part = pl.ds(j * 16, 16)
        streams.append(
            reduce_stages(
                copy,
                dwo_ref.at[:, :, :, part],
                wo_got.at[j],
                wo_p1a.at[j],
                wo_p1b.at[j],
                wo_p2.at[j],
                wo_land.at[j],
                wo_out.at[part],
            )
        )
    ticks = [0]

    def tick():
        t = ticks[0]
        ticks[0] += 1
        for stage in range(5):
            if 0 <= t - stage < len(streams):
                streams[t - stage][stage]()

    own_ga = pltpu.make_async_copy(
        ga_home.at[:, columns(blk)], ga.at[blk], local_sem.at[0]
    )
    ga_copies = [copy(ga_home.at[:, columns(mate[1])], ga.at[blk], mate) for mate in mates]
    sum_copies = [
        copy(sums_ref, sums_land.at[k], mate) for k, mate in enumerate(mates)
    ]
    half = gw.shape[1] // 2
    w_far = [
        copy(gw.at[row ^ 3, pl.ds(0, half)], gw_p1.at[0], to["y"]),
        copy(gw.at[row ^ 3, pl.ds(half, half)], gw_p1.at[1], to["x"]),
    ]
    w_near = [
        copy(gw.at[row ^ 1], gw_p2.at[0], to["x"]),
        copy(gw.at[row ^ 2], gw_p2.at[1], to["y"]),
    ]
    w_home = [copy(gw.at[row, mate[1]], gw_land.at[blk], mate) for mate in mates]
    d0, d1 = 3 - z, (3 * z + 2) % 5
    d2 = 3 - d1
    inner, outer = (z == 1) | (z == 2), (z == 0) | (z == 3)
    n_sib = [
        copy(gn.at[chip, 1 - c], gn_sib.at[chip], to["sib"]) for chip in (d0, d1, d2, z)
    ]
    n_relay = copy(gn.at[d0, c], gn_land.at[0], (row, (1 + z // 2) * 2 + c))
    n_inner = copy(gn.at[d0, c], gn_land.at[1], (row, (2 - z // 2) * 2 + c))
    n_home = [
        copy(gn.at[d1, c], gn_land.at[2], (row, d1 * 2 + c)),
        copy(gn.at[d2, c], gn_land.at[3], (row, d2 * 2 + c)),
    ]
    s_sib = copy(small.at[0], sm_sib, to["sib"])
    s_far = [
        copy(small.at[1, row ^ 3, 0:2], sm_p1a, to["y"]),
        copy(small.at[1, row ^ 3, 2:4], sm_p1b, to["x"]),
    ]
    s_near = [
        copy(small.at[1, row ^ 1], sm_p2.at[0], to["x"]),
        copy(small.at[1, row ^ 2], sm_p2.at[1], to["y"]),
    ]
    s_home = [
        copy(small.at[1, row, (z + k) % 4], sm_land.at[k - 1], to["z%d" % k])
        for k in (1, 3, 2)
    ]

    late = [
        pltpu.make_async_copy(src, dst, local_sem.at[1 + len(streams) + k])
        for k, (src, dst) in enumerate(
            ((normed_in, normed_ref), (wcols_in, wcols))
        )
    ]
    own_ga.start()
    start(ga_copies)
    start(late)

    @pl.loop(0, 8)
    def _(n):
        some = attended_ref[:, pl.ds(pl.multiple_of(n * block, block), block)]
        made = dot_tn(some, proj_ref[...]).astype(bf16)
        dwo_ref[n // 2, pl.ds(2 * (n % 2), 2)] = made.reshape(2, 2, wrows, width)

    tick()
    dk_ref[...] = jnp.zeros_like(dk_ref)
    dv_ref[...] = jnp.zeros_like(dv_ref)
    small[0] = small_ref[...]
    own_ga.wait()
    tick()
    arrived(ga_copies)

    segments = seg_ref[0:1, :]
    for t in range(blocks):
        rows = slice(t * block, (t + 1) * block)
        keys = (t + 1) * block
        stat = stat_ref[rows, :]
        place_q = lax.broadcasted_iota(jnp.int32, (block, keys), 0) + t * block
        place_k = lax.broadcasted_iota(jnp.int32, (block, keys), 1)
        allowed = (place_k <= place_q) & (segments[:, :keys] == stat[:, 2:3])
        for h in range(cols_here // HEAD_DIM):
            cols = slice(h * HEAD_DIM, (h + 1) * HEAD_DIM)
            q = low_ref[rows, cols]
            k = low_ref[0:keys, cols_here + h * HEAD_DIM : cols_here + (h + 1) * HEAD_DIM]
            v = low_ref[
                0:keys, 2 * cols_here + h * HEAD_DIM : 2 * cols_here + (h + 1) * HEAD_DIM
            ]
            g = ga[t * per : (t + 1) * per, :, cols].reshape(block, HEAD_DIM)
            scores = jnp.where(allowed, dot_nt(q, k) * scale, masked_score)
            raised = jnp.exp(scores - stat[:, 3 + h : 4 + h])
            probs = jnp.where(allowed, raised, 0.0) * stat[:, 5 + h : 6 + h]
            delta = jnp.sum(g.astype(f32) * att_ref[rows, cols], axis=-1, keepdims=True)
            ds = (probs * (dot_nt(g, v) - delta)).astype(bf16)
            dq_ref[rows, cols] = dot(ds, k) * scale
            dk_ref[0:keys, cols] += dot_tn(ds, q) * scale
            dv_ref[0:keys, cols] += dot_tn(probs.astype(bf16), g)
        tick()

    pairs = row_pairs(cols_here)
    gain_q, gain_k = gain_ref[0:1, :], gain_ref[1:2, :]
    for_q = jnp.zeros((1, cols_here), f32)
    for_k = jnp.zeros((1, cols_here), f32)
    for t in range(blocks):
        rows = slice(t * block, (t + 1) * block)
        cosine, sine = cos_ref[rows, :], -sin_ref[rows, :]
        q_pre, k_pre = pre_ref[rows, :cols_here], pre_ref[rows, cols_here:]
        dq = turned(dq_ref[rows, :], cosine, sine)
        dk = turned(dk_ref[rows, :], cosine, sine)
        dq_ref[rows, :] = dq
        dk_ref[rows, :] = dk
        vq, vk = dq * q_pre, dk * k_pre
        for_q = for_q + jnp.sum(vq * stat_ref[rows, 0:1], axis=0, keepdims=True)
        for_k = for_k + jnp.sum(vk * stat_ref[rows, 1:2], axis=0, keepdims=True)
        sums = sums_by_row(pairs, jnp.concatenate([vq * gain_q, vk * gain_k], axis=1))
        sums_ref[2 * t : 2 * t + 2, :] = sums[0:2]
    start(sum_copies)
    tick()
    total = sums_ref[...]
    for k, cp in enumerate(sum_copies):
        cp.wait_recv()
        total = total + sums_land[k]
    means = total * (1.0 / width)
    for t in range(blocks):
        rows = slice(t * block, (t + 1) * block)
        mean = jnp.concatenate(
            [means[2 * t : 2 * t + 2], jnp.zeros((6, block), f32)], axis=0
        ).T
        for j, (d_ref, gain) in enumerate(((dq_ref, gain_q), (dk_ref, gain_k))):
            cols = slice(j * cols_here, (j + 1) * cols_here)
            r = stat_ref[rows, j : j + 1]
            grads_ref[rows, cols] = (
                r * gain * d_ref[rows, :]
                - pre_ref[rows, cols] * (r * r * r) * mean[:, j : j + 1]
            ).astype(bf16)
        grads_ref[rows, 2 * cols_here :] = dv_ref[rows, :].astype(bf16)

    deep = 8 * wrows
    for cp in late:
        cp.wait()

    def weight_rows(k):
        there = row ^ k
        some = normed_ref[:, pl.ds(pl.multiple_of(there * deep, deep), deep)]
        gw[there] = (
            dot_tn(some, grads_ref[...]).astype(bf16).reshape(8, wrows, 3 * cols_here)
        )

    weight_rows(3)
    start(w_far)
    weights = wcols[...].reshape(width, 3 * cols_here)
    for_attn = jnp.zeros((1, width), f32)
    chips = (d0, d1, d2, z)
    for n, chip in enumerate(chips):
        tok = pl.ds(pl.multiple_of(chip * block, block), block)
        made = dot_nt(grads_ref[tok, :], weights)
        gn[chip] = made.astype(bf16).reshape(per, tokens, width)
        n_sib[n].start()
        for_attn = for_attn + jnp.sum(
            made * normed_ref[tok, :].astype(f32), axis=0, keepdims=True
        )
        if n:
            before = chips[n - 1]
            n_sib[n - 1].wait_recv()
            n_sib[n - 1].wait_send()
            gn[before, c] = added(gn[before, c], gn_sib[before])
            if n == 1:
                pl.when(outer)(n_relay.start)
                pl.when(inner)(n_inner.start)
            elif n == 2:
                n_home[0].start()
    weight_rows(1)
    weight_rows(2)

    @pl.when(inner)
    def _():
        n_relay.wait_recv()
        gn[d2, c] = added(gn[d2, c], gn_land[0])

    n_home[1].start()
    weight_rows(0)
    tick()
    for r in range(4):
        for q in range(4):
            at = (r * 4 + q) * 128
            small[0, r, q, 16:17, :] = for_attn[:, at : at + 128]
    for j in range(cols_here // 128):
        at = blk * (cols_here // 128) + j
        small[0, at // 4, at % 4, 17:18, :] = for_q[:, j * 128 : (j + 1) * 128]
        small[0, at // 4, at % 4, 18:19, :] = for_k[:, j * 128 : (j + 1) * 128]
    s_sib.start()

    arrived(w_far[:1])
    gw[row ^ 1, 0:half] = added(gw[row ^ 1, 0:half], gw_p1[0])
    w_near[0].start()
    arrived(w_far[1:])
    gw[row ^ 2, half:] = added(gw[row ^ 2, half:], gw_p1[1])
    w_near[1].start()
    s_sib.wait_recv()
    small[1] = small[0] + sm_sib[...]
    start(s_far)
    tick()
    arrived(s_far)
    small[1, row ^ 1, 0:2] = small[1, row ^ 1, 0:2] + sm_p1a[...]
    small[1, row ^ 2, 2:4] = small[1, row ^ 2, 2:4] + sm_p1b[...]
    start(s_near)
    arrived(w_near)
    for b in range(8):
        gw[row, b] = added(gw[row, b], gw_p2[0, b], gw_p2[1, b])
    start(w_home)
    arrived(s_near)
    small[1, row] = small[1, row] + sm_p2[0] + sm_p2[1]
    start(s_home)
    while ticks[0] < len(streams) + 4:
        tick()

    n_sib[3].wait_recv()
    gn_out[...] = gn[z, c].astype(f32) + gn_sib[z].astype(f32)
    arrived(n_home)
    gn_out[...] += gn_land[2].astype(f32) + gn_land[3].astype(f32)

    @pl.when(inner)
    def _():
        n_inner.wait_recv()
        n_inner.wait_send()
        gn_out[...] += gn_land[1].astype(f32)

    @pl.when(outer)
    def _():
        n_relay.wait_send()

    arrived(s_home)
    small_out[...] = small[1, row, z] + sm_land[0] + sm_land[1] + sm_land[2]
    gw_land[blk] = gw[row, blk]
    arrived(w_home)
    for b in range(8):
        for j, out in enumerate((q_out, k_out, v_out)):
            out[:, b * cols_here : (b + 1) * cols_here] = gw_land[
                b, :, j * cols_here : (j + 1) * cols_here
            ].astype(f32)
    n_sib[3].wait_send()
    for cp in ga_copies + sum_copies + w_far + w_near + w_home + n_home:
        cp.wait_send()
    for cp in [s_sib] + s_far + s_near + s_home:
        cp.wait_send()


def back(ga, att_low, proj, low, pre, att, stat, seg, gain, cosine, sine, normed, wcols, small):
    any_, vm = pl.BlockSpec(memory_space=pl.ANY), pl.BlockSpec(memory_space=pltpu.VMEM)
    tokens, width = ga.shape
    seq, cols = 8 * tokens, width // 8
    wrows = wcols.shape[2]
    fields = small.shape[2:]
    dma = pltpu.SemaphoreType.DMA
    streams = wrows // 16
    count = 8 * streams + 7 + 7 + 2 + 2 + 7 + 4 + 4 + 1 + 2 + 2 + 3
    shape, vmem = jax.ShapeDtypeStruct, pltpu.VMEM
    weight = shape((wrows, width), f32)
    return pl.pallas_call(
        back_kernel,
        out_shape=(
            shape((tokens, width), f32),
            weight,
            weight,
            weight,
            weight,
            shape(fields, f32),
        ),
        in_specs=[any_] + [vm] * 10 + [any_] * 2 + [vm],
        out_specs=(vm,) * 6,
        scratch_shapes=[
            vmem((seq, width), bf16),
            vmem((4, 8, wrows, 3 * cols), bf16),
            vmem((8, tokens, cols), bf16),
            vmem((seq, cols), f32),
            vmem((seq, cols), f32),
            vmem((seq, cols), f32),
            vmem((seq, 3 * cols), bf16),
            vmem((8, seq // 4), f32),
            vmem((7, 8, seq // 4), f32),
            vmem((4, 2, tokens, width), bf16),
            vmem((4, tokens, width), bf16),
            vmem((4, tokens, width), bf16),
            vmem((4, 8, wrows, 3 * cols), bf16),
            vmem((2, 4, wrows, 3 * cols), bf16),
            vmem((2, 8, wrows, 3 * cols), bf16),
            vmem((8, wrows, 3 * cols), bf16),
            vmem((2, 4, 4) + fields, f32),
            vmem((4, 4) + fields, f32),
            vmem((2,) + fields, f32),
            vmem((2,) + fields, f32),
            vmem((2, 4) + fields, f32),
            vmem((3,) + fields, f32),
            vmem((4, 4, 2, wrows, width), bf16),
            vmem((streams, 4, 4, 16, width), bf16),
            vmem((streams, 4, 16, width // 2), bf16),
            vmem((streams, 4, 16, width // 2), bf16),
            vmem((streams, 2, 4, 16, width), bf16),
            vmem((streams, 3, 16, width), bf16),
            dma((count,)),
            dma((count,)),
            dma((4 + streams,)),
        ],
        compiler_params=pltpu.CompilerParams(
            collective_id=7, has_side_effects=True, vmem_limit_bytes=60 * 2**20
        ),
        cost_estimate=pl.CostEstimate(
            flops=10**10, bytes_accessed=2 * 10**8, transcendentals=0
        ),
    )(
        ga,
        att_low,
        proj,
        low,
        pre,
        att,
        stat,
        seg,
        gain,
        cosine,
        sine,
        normed,
        wcols,
        small,
    )


def rope_tables(count):
    half = HEAD_DIM // 2
    frequency = jnp.exp(
        -math.log(10000.0) * 2.0 * jnp.arange(half, dtype=f32) / HEAD_DIM
    )
    angles = jnp.arange(count, dtype=f32)[:, None] * frequency[None, :]
    return jnp.cos(angles), jnp.sin(angles)


def rope(values, cosine, sine):
    half = HEAD_DIM // 2
    a, b = values[..., :half], values[..., half:]
    return jnp.concatenate([a * cosine - b * sine, b * cosine + a * sine], axis=-1)


def norm_back(v, r, g, c, mean_vgc):
    return r * g * c - v * (r * r * r) * mean_vgc


def experts_by_scan(expert_in, upstream, gates, gate_local, up_local, down_local):
    tokens, width = expert_in.shape
    experts = gates.shape[1]
    rows, blocks = lax.axis_size("row"), lax.axis_size("blk")
    devices = rows * blocks
    me = lax.axis_index("row") * blocks + lax.axis_index("blk")
    parts = devices * tokens // 2048
    step = tokens // parts
    all_gates = lax.all_gather(gates, BOTH, axis=0, tiled=False)
    own_gate = jnp.sum(
        jnp.where(
            jnp.arange(experts, dtype=jnp.int32)[None, None, :] == me // 2,
            all_gates,
            0.0,
        ),
        axis=-1,
    )

    def expert_part(sums, items):
        own_rows, own_upstream, gate_col = items
        got = lax.all_gather(own_rows, BOTH, axis=0, tiled=True)
        up_stream = lax.all_gather(own_upstream, BOTH, axis=0, tiled=True)
        gate_col = gate_col.reshape(devices * step, 1)
        gate_pre = dot(got, gate_local)
        up_pre = dot(got, up_local)
        sig = jax.nn.sigmoid(gate_pre)
        silu = gate_pre * sig
        hidden = (silu * up_pre).astype(bf16)
        part_f = dot(hidden, down_local).astype(bf16).astype(f32)
        up_f = up_stream.astype(f32)
        dots = jnp.sum(part_f * up_f, axis=-1).reshape(devices, step)
        mixed = (gate_col * part_f).astype(bf16)
        out = lax.psum_scatter(mixed, BOTH, scatter_dimension=0, tiled=True)
        grad_part = (gate_col * up_f).astype(bf16)
        grad_hidden = dot_nt(grad_part, down_local)
        grad_gate_pre = (
            grad_hidden * up_pre * sig * (1.0 + gate_pre * (1.0 - sig))
        ).astype(bf16)
        grad_up_pre = (grad_hidden * silu).astype(bf16)
        grad_rows = (
            dot_nt(grad_gate_pre, gate_local) + dot_nt(grad_up_pre, up_local)
        ).astype(bf16)
        back = lax.psum_scatter(grad_rows, BOTH, scatter_dimension=0, tiled=True)
        sums = (
            sums[0] + dot_tn(got, grad_gate_pre),
            sums[1] + dot_tn(got, grad_up_pre),
            sums[2] + dot_tn(hidden, grad_part),
        )
        return sums, (out, back, dots)

    sums = (
        jnp.zeros(gate_local.shape, f32),
        jnp.zeros(up_local.shape, f32),
        jnp.zeros(down_local.shape, f32),
    )
    items = (
        expert_in.reshape(parts, step, width),
        upstream.reshape(parts, step, width),
        own_gate.reshape(devices, parts, step).transpose(1, 0, 2),
    )
    if parts > 2:
        sums, (outs, backs, dots) = lax.scan(expert_part, sums, items)
    else:
        made = []
        for part in range(parts):
            sums, result = expert_part(sums, tuple(item[part] for item in items))
            made.append(result)
        outs, backs, dots = (jnp.stack(some) for some in zip(*made))
    dots = dots.transpose(1, 0, 2).reshape(devices, tokens)
    outs = outs.reshape(tokens, width)
    backs = backs.reshape(tokens, width)
    dots = lax.all_to_all(dots, BOTH, split_axis=0, concat_axis=0, tiled=True)
    grad_gates = jnp.sum(dots.reshape(experts, 2, tokens), axis=1).T
    return outs.astype(f32), backs.astype(f32), grad_gates, sums


def own_mesh_body(
    hidden_in,
    segment_ids,
    expert_ids,
    attention_gain,
    query_gain,
    key_gain,
    expert_gain,
    query_weight,
    key_weight,
    value_weight,
    output_weight,
    router_weight,
    gate_weight,
    up_weight,
    down_weight,
    grad_out,
):
    tokens, width = hidden_in.shape[1:]
    wrows = query_weight.shape[0]
    experts = router_weight.shape[1]
    blocks = lax.axis_size("blk")
    seq = tokens * blocks
    head_cols = width // blocks
    blk = lax.axis_index("blk")
    upstream_low = grad_out[0]

    experts_in_order = jnp.arange(experts, dtype=jnp.int32)
    routed = jnp.any(
        expert_ids[0][:, :, None] == experts_in_order[None, None, :], axis=1
    )
    routed_t = jnp.any(
        expert_ids[0].T[None, :, :] == experts_in_order[:, None, None], axis=1
    )
    gains = jnp.stack([attention_gain, query_gain, key_gain, expert_gain])
    spare = tokens - wrows
    gains = jnp.concatenate([gains, gains], axis=1)
    lane = jnp.arange(2 * wrows, dtype=jnp.int32)[None]
    gains = jnp.where(lane // wrows == blk % 2, gains, 0)

    def rows_at(first, values, lanes):
        return jnp.pad(values.astype(f32), ((first, 64 - first - values.shape[0]), (0, lanes)))

    pack = (
        rows_at(0, routed_t, 0)
        + rows_at(16, segment_ids, 0)
        + rows_at(32, router_weight.T, spare)
        + rows_at(32 + experts, gains, 0)
    ).astype(bf16)
    cosine, sine = rope_tables(seq)
    cosine = jnp.concatenate([cosine, cosine], axis=1)
    sine = jnp.concatenate([-sine, sine], axis=1)
    (
        full_output,
        upstream_all,
        packs,
        normed_row,
        qkv_cols,
        low,
        pre,
        attended,
        stats,
        attended_low,
        residual_mid,
        expert_in,
    ) = front(
        hidden_in[0],
        query_weight,
        key_weight,
        value_weight,
        output_weight,
        upstream_low,
        pack,
        cosine,
        sine,
    )
    full_output = full_output.reshape(width, width)
    packs = packs.reshape(-1, pack.shape[0], tokens)
    router = packs[:, 32 : 32 + experts, :wrows].transpose(0, 2, 1).reshape(width, -1)
    gains = packs[:, 32 + experts : 36 + experts].reshape(-1, 2, 4, tokens).sum(axis=1)
    gains = gains.transpose(1, 0, 2).reshape(4, width).astype(f32)
    gain_attn, gain_expert = gains[0], gains[3]
    own_q_gain = lax.dynamic_slice_in_dim(gains[1], blk * head_cols, head_cols)
    own_k_gain = lax.dynamic_slice_in_dim(gains[2], blk * head_cols, head_cols)
    steps = tokens // 16
    mask = packs[:, :experts].reshape(-1, experts, steps, 16)
    mask = mask.transpose(2, 0, 3, 1).reshape(steps, -1, experts)
    x = hidden_in[0].astype(f32)
    r_attn = lax.rsqrt(jnp.mean(x * x, axis=-1, keepdims=True) + epsilon)
    r_exp = lax.rsqrt(
        jnp.mean(residual_mid * residual_mid, axis=-1, keepdims=True) + epsilon
    )
    logits = dot(expert_in, router)
    top_logit = jnp.max(
        jnp.where(routed, logits, masked_score), axis=-1, keepdims=True
    )
    gates = jnp.where(routed, jnp.exp(logits - top_logit), 0.0)
    gates = gates / jnp.sum(gates, axis=-1, keepdims=True)

    outs, backs, grad_gate_local, grad_up_local, grad_down_local = moe(
        expert_in,
        upstream_all,
        mask,
        router,
        gate_weight[0],
        up_weight[0],
        down_weight[0],
    )
    outs = outs.reshape(tokens, width)
    backs = backs.reshape(tokens, width + EXTRA)
    dots = backs[:, width : width + 2 * experts]
    dots = dots + backs[:, width + 64 : width + 64 + 2 * experts]
    grad_gates = jnp.sum(dots.reshape(tokens, experts, 2), axis=2)
    layer_out = (residual_mid + outs).astype(bf16)
    upstream = upstream_low.astype(f32)
    grad_picked = gates * (
        grad_gates - jnp.sum(gates * grad_gates, axis=-1, keepdims=True)
    )
    grad_logits = jnp.where(routed, grad_picked, 0.0).astype(bf16)
    grad_expert_in = backs[:, :width] + dot_nt(grad_logits, router)
    grad_router = dot_tn(grad_logits, expert_in)
    grad_gain_expert = jnp.sum(grad_expert_in * residual_mid * r_exp, axis=0)
    grad_mid = upstream + norm_back(
        residual_mid,
        r_exp,
        gain_expert,
        grad_expert_in,
        jnp.mean(residual_mid * gain_expert * grad_expert_in, axis=-1, keepdims=True),
    )
    grad_proj = grad_mid.astype(bf16)
    grad_attended = dot_nt(grad_proj, full_output).astype(bf16)
    small = jnp.concatenate(
        [
            grad_router,
            jnp.zeros((3, width), f32),
            grad_gain_expert[None],
            jnp.zeros((20 - experts, width), f32),
        ],
        axis=0,
    )
    fields = small.shape[0]
    small = small.reshape(fields, 4, 4, 2 * wrows).transpose(1, 2, 0, 3)
    grad_normed, grad_q, grad_k, grad_v, grad_output_w, small = back(
        grad_attended,
        attended_low,
        grad_proj,
        low,
        pre,
        attended,
        stats,
        jnp.broadcast_to(stats[:, 2][None], (8, seq)),
        jnp.concatenate(
            [own_q_gain[None], own_k_gain[None], jnp.zeros((6, head_cols), f32)], axis=0
        ),
        cosine,
        sine,
        normed_row,
        qkv_cols,
        small,
    )
    input_grad = grad_mid + norm_back(
        x,
        r_attn,
        gain_attn,
        grad_normed,
        jnp.mean(x * gain_attn * grad_normed, axis=-1, keepdims=True),
    )
    small = lax.dynamic_slice_in_dim(small, (blk % 2) * wrows, wrows, axis=1)
    return (
        layer_out[None],
        input_grad[None],
        small[experts] / attention_gain.astype(f32),
        small[experts + 1],
        small[experts + 2],
        small[experts + 3],
        grad_q,
        grad_k,
        grad_v,
        grad_output_w,
        small[:experts].T,
        grad_gate_local[None],
        grad_up_local[None],
        grad_down_local[None],
    )


def any_mesh_body(
    hidden_in,
    segment_ids,
    expert_ids,
    attention_gain,
    query_gain,
    key_gain,
    expert_gain,
    query_weight,
    key_weight,
    value_weight,
    output_weight,
    router_weight,
    gate_weight,
    up_weight,
    down_weight,
    grad_out,
):
    tokens = hidden_in.shape[1]
    width = hidden_in.shape[2]
    experts = router_weight.shape[1]
    rows, blocks = lax.axis_size("row"), lax.axis_size("blk")
    devices = rows * blocks
    seq = tokens * blocks
    head_cols = width // blocks
    heads_here = HEADS // blocks
    blk = lax.axis_index("blk")
    me = lax.axis_index("row") * blocks + blk
    scale = HEAD_DIM**-0.5

    small = jnp.concatenate(
        [
            router_weight,
            attention_gain[:, None],
            query_gain[:, None],
            key_gain[:, None],
            expert_gain[:, None],
        ],
        axis=1,
    )
    small = lax.all_gather(small, BOTH, axis=0, tiled=True)
    router = small[:, :experts]
    gains = small[:, experts:].astype(f32)
    gain_attn, gain_expert = gains[:, 0], gains[:, 3]
    own_q_gain = lax.dynamic_slice_in_dim(gains[:, 1], blk * head_cols, head_cols)
    own_k_gain = lax.dynamic_slice_in_dim(gains[:, 2], blk * head_cols, head_cols)

    x = hidden_in[0].astype(f32)
    r_attn = lax.rsqrt(jnp.mean(x * x, axis=-1, keepdims=True) + epsilon)
    normed = (x * r_attn * gain_attn).astype(bf16)
    normed_row = lax.all_gather(normed, "blk", axis=0, tiled=True)
    segments = lax.all_gather(segment_ids[0], "blk", axis=0, tiled=True)

    stacked = jnp.stack([query_weight, key_weight, value_weight], axis=0)
    wrows = stacked.shape[1]
    stacked = stacked.reshape(3, wrows, blocks, head_cols).transpose(2, 1, 0, 3)
    stacked = stacked.reshape(blocks, wrows, 3 * head_cols)
    cols = lax.all_to_all(stacked, "blk", split_axis=0, concat_axis=0, tiled=True)
    cols = cols.reshape(blocks * wrows, 3 * head_cols)
    qkv_cols = lax.all_gather(cols, "row", axis=0, tiled=True)
    full_output = lax.all_gather(output_weight, BOTH, axis=0, tiled=True)

    qkv = dot(normed_row, qkv_cols)
    query_pre = qkv[:, :head_cols]
    key_pre = qkv[:, head_cols : 2 * head_cols]
    value = qkv[:, 2 * head_cols :].astype(bf16)
    squares = jnp.stack(
        [jnp.sum(query_pre * query_pre, axis=-1), jnp.sum(key_pre * key_pre, axis=-1)]
    )
    squares = lax.psum(squares, "blk") / width
    r_q = lax.rsqrt(squares[0] + epsilon)[:, None]
    r_k = lax.rsqrt(squares[1] + epsilon)[:, None]
    cosine, sine = (table[:, None] for table in rope_tables(seq))

    def heads(v):
        return v.reshape(seq, heads_here, HEAD_DIM)

    query = rope(heads(query_pre * r_q * own_q_gain), cosine, sine).astype(bf16)
    key = rope(heads(key_pre * r_k * own_k_gain), cosine, sine).astype(bf16)
    value = heads(value)
    places = jnp.arange(seq, dtype=jnp.int32)
    allowed = (places[None, :] <= places[:, None]) & (
        segments[None, :] == segments[:, None]
    )
    scores = jnp.einsum("qhd,khd->hqk", query, key, preferred_element_type=f32) * scale
    scores = jnp.where(allowed[None], scores, masked_score)
    top = jnp.max(scores, axis=-1, keepdims=True)
    weights = jnp.where(allowed[None], jnp.exp(scores - top), 0.0)
    total = jnp.sum(weights, axis=-1, keepdims=True)
    probs = weights / total
    probs_low = probs.astype(bf16)
    attended = jnp.einsum("hqk,khd->qhd", probs_low, value, preferred_element_type=f32)
    attended_low_cols = attended.astype(bf16).reshape(blocks, tokens, head_cols)
    attended_low = lax.all_to_all(
        attended_low_cols, "blk", split_axis=0, concat_axis=0, tiled=True
    )
    attended_low = attended_low.transpose(1, 0, 2).reshape(tokens, width)

    residual_mid = x + dot(attended_low, full_output)
    r_exp = lax.rsqrt(
        jnp.mean(residual_mid * residual_mid, axis=-1, keepdims=True) + epsilon
    )
    expert_in = (residual_mid * r_exp * gain_expert).astype(bf16)
    logits = dot(expert_in, router)
    routes = expert_ids[0]
    routed = jnp.any(
        routes[:, :, None] == jnp.arange(experts, dtype=jnp.int32)[None, None, :],
        axis=1,
    )
    top_logit = jnp.max(
        jnp.where(routed, logits, masked_score), axis=-1, keepdims=True
    )
    gates = jnp.where(routed, jnp.exp(logits - top_logit), 0.0)
    gates = gates / jnp.sum(gates, axis=-1, keepdims=True)

    gate_local, up_local, down_local = gate_weight[0], up_weight[0], down_weight[0]
    outs, backs, grad_gates, sums = experts_by_scan(
        expert_in, grad_out[0], gates, gate_local, up_local, down_local
    )
    grad_gate_local, grad_up_local, grad_down_local = sums
    layer_out = (residual_mid + outs).astype(bf16)
    upstream = grad_out[0].astype(f32)
    grad_picked = gates * (
        grad_gates - jnp.sum(gates * grad_gates, axis=-1, keepdims=True)
    )
    grad_logits = jnp.where(routed, grad_picked, 0.0).astype(bf16)
    grad_expert_in = backs + dot_nt(
        grad_logits, router
    )
    grad_router = dot_tn(expert_in, grad_logits)
    grad_gain_expert = jnp.sum(grad_expert_in * residual_mid * r_exp, axis=0)
    grad_mid = upstream + norm_back(
        residual_mid,
        r_exp,
        gain_expert,
        grad_expert_in,
        jnp.mean(residual_mid * gain_expert * grad_expert_in, axis=-1, keepdims=True),
    )
    grad_proj = grad_mid.astype(bf16)
    grad_output_w = dot_tn(attended_low, grad_proj).astype(bf16)
    grad_output_w = lax.psum_scatter(
        grad_output_w, BOTH, scatter_dimension=0, tiled=True
    ).astype(f32)
    grad_attended = dot_nt(grad_proj, full_output).astype(bf16)
    grad_attended = grad_attended.reshape(tokens, blocks, head_cols).transpose(1, 0, 2)
    grad_attended = lax.all_to_all(
        grad_attended, "blk", split_axis=0, concat_axis=0, tiled=True
    )
    grad_attended = grad_attended.reshape(seq, heads_here, HEAD_DIM)
    row_delta = jnp.sum(grad_attended.astype(f32) * attended, axis=-1).T
    grad_probs = jnp.einsum(
        "qhd,khd->hqk", grad_attended, value, preferred_element_type=f32
    )
    grad_scores = (probs * (grad_probs - row_delta[:, :, None])).astype(bf16)
    grad_value = jnp.einsum(
        "hqk,qhd->khd", probs_low, grad_attended, preferred_element_type=f32
    ).astype(bf16)
    grad_query = (
        jnp.einsum("hqk,khd->qhd", grad_scores, key, preferred_element_type=f32) * scale
    )
    grad_key = (
        jnp.einsum("hqk,qhd->khd", grad_scores, query, preferred_element_type=f32)
        * scale
    )
    grad_query = rope(grad_query, cosine, -sine).reshape(seq, head_cols)
    grad_key = rope(grad_key, cosine, -sine).reshape(seq, head_cols)
    means = jnp.stack(
        [
            jnp.sum(query_pre * own_q_gain * grad_query, axis=-1),
            jnp.sum(key_pre * own_k_gain * grad_key, axis=-1),
        ]
    )
    means = lax.psum(means, "blk") / width
    grad_q_gain = jnp.sum(grad_query * query_pre * r_q, axis=0)
    grad_k_gain = jnp.sum(grad_key * key_pre * r_k, axis=0)
    grad_query_pre = norm_back(query_pre, r_q, own_q_gain, grad_query, means[0][:, None])
    grad_key_pre = norm_back(key_pre, r_k, own_k_gain, grad_key, means[1][:, None])
    grad_qkv = jnp.concatenate(
        [
            grad_query_pre.astype(bf16),
            grad_key_pre.astype(bf16),
            grad_value.reshape(seq, head_cols),
        ],
        axis=1,
    )
    grad_w = dot_tn(normed_row, grad_qkv).astype(bf16)
    grad_w = lax.psum_scatter(grad_w, "row", scatter_dimension=0, tiled=True)
    grad_w = grad_w.reshape(blocks, wrows, 3 * head_cols)
    grad_w = lax.all_to_all(grad_w, "blk", split_axis=0, concat_axis=0, tiled=True)
    grad_w = grad_w.reshape(blocks, wrows, 3, head_cols).transpose(2, 1, 0, 3)
    grad_w = grad_w.reshape(3, wrows, width).astype(f32)
    grad_normed = dot_nt(grad_qkv, qkv_cols).astype(bf16)
    grad_normed = lax.psum_scatter(
        grad_normed, "blk", scatter_dimension=0, tiled=True
    ).astype(f32)
    grad_gain_attn = jnp.sum(grad_normed * x * r_attn, axis=0)
    input_grad = grad_mid + norm_back(
        x,
        r_attn,
        gain_attn,
        grad_normed,
        jnp.mean(x * gain_attn * grad_normed, axis=-1, keepdims=True),
    )

    def placed(vector):
        return lax.dynamic_update_slice_in_dim(
            jnp.zeros((width,), f32), vector, blk * head_cols, axis=0
        )

    small_grads = jnp.concatenate(
        [
            grad_router,
            grad_gain_attn[:, None],
            placed(grad_q_gain)[:, None],
            placed(grad_k_gain)[:, None],
            grad_gain_expert[:, None],
        ],
        axis=1,
    )
    small_grads = lax.psum_scatter(small_grads, BOTH, scatter_dimension=0, tiled=True)
    return (
        layer_out[None],
        input_grad[None],
        small_grads[:, experts],
        small_grads[:, experts + 1],
        small_grads[:, experts + 2],
        small_grads[:, experts + 3],
        grad_w[0],
        grad_w[1],
        grad_w[2],
        grad_output_w,
        small_grads[:, :experts],
        grad_gate_local[None],
        grad_up_local[None],
        grad_down_local[None],
    )


def solution(mesh):
    tokens3 = P("row", "blk", None)
    vector, matrix, cube = P(BOTH), P(BOTH, None), P(BOTH, None, None)
    own = (mesh.shape["row"], mesh.shape["blk"]) == (4, 8)
    return jax.shard_map(
        own_mesh_body if own else any_mesh_body,
        mesh=mesh,
        in_specs=(
            tokens3,
            P("row", "blk"),
            tokens3,
            vector,
            vector,
            vector,
            vector,
            matrix,
            matrix,
            matrix,
            matrix,
            matrix,
            cube,
            cube,
            cube,
            tokens3,
        ),
        out_specs=(
            tokens3,
            tokens3,
            vector,
            vector,
            vector,
            vector,
            matrix,
            matrix,
            matrix,
            matrix,
            matrix,
            cube,
            cube,
            cube,
        ),
        check_vma=False,
    )
```
